32 devices in a mesh: dp: 16 (over z, y, x), mp: 2 (over core).
Axes of the slice: x: 2, y: 2, z: 4, core: 2. Of those that a mesh axis runs over, the one named last changes fastest.
Arguments:
- history: bfloat16 [8, 16384, 768], P(None, ('dp', 'mp')), may hold values from -6 to 6
- depth_weights: float32 [8], replicated, may hold values from -0.6 to 0.6
- gain_attn: float32 [768], replicated, may hold values from 0.25 to 1.75
- gain_mlp: float32 [768], replicated, may hold values from 0.25 to 1.75
- qkv_weight: bfloat16 [3, 768, 768], P(None, None, 'mp'), may hold values from -0.21875 to 0.21875
- out_weight: bfloat16 [768, 768], P('mp'), may hold values from -0.875 to 0.875
- up_weight: bfloat16 [768, 3072], P(None, 'mp'), may hold values from -0.21875 to 0.21875
- down_weight: bfloat16 [3072, 768], P('mp'), may hold values from -0.109375 to 0.109375
- cotangent: bfloat16 [16384, 768], P(('dp', 'mp')), may hold values from -6 to 6
Outputs:
- block_out: bfloat16 [16384, 768], P(('dp', 'mp'))
- grad_history: bfloat16 [8, 16384, 768], P(None, ('dp', 'mp'))
- grad_depth: float32 [8], replicated
- grad_gain_attn: float32 [768], replicated
- grad_gain_mlp: float32 [768], replicated
- grad_qkv: float32 [3, 768, 768], P(None, None, 'mp')
- grad_out_proj: float32 [768, 768], P('mp')
- grad_up: float32 [768, 3072], P(None, 'mp')
- grad_down: float32 [3072, 768], P('mp')
The draws below stay inside these ranges and needn't reach their ends.
All inputs are finite; a program needn't handle non-finite values.
Results may differ from the reference program's by a relative error of at most 0.018.
Values may be sent and summed in bfloat16 or wider, within the bound.
No kernel may reach another device: no remote copies, remote signals or barrier semaphores. Data moves between devices by JAX's collectives and lax.ppermute only.
A program may use at most 192 MiB of HBM per device.

```python
import jax
import jax.numpy as jnp
from jax import lax

D = 768
HEADS = 12
HEAD_DIM = 64
FF = 3072
HIST = 8
SEQ_LEN = 1024
TOKENS = 16384


def block_scale(key, shape, pieces, smallest, top_value):
    gain = 1.0
    for axis_at, shards_of in pieces:
        steps = jax.random.uniform(jax.random.fold_in(jax.random.fold_in(key, 6), axis_at), (shards_of,), jnp.float32, smallest / len(pieces), top_value / len(pieces))
        gain = gain * jnp.repeat(jnp.exp(steps), shape[axis_at] // shards_of).reshape((-1,) + (1,) * (len(shape) - 1 - axis_at))
    return gain


def centred(stream_key, extent, scale, most, cuts=(), held_as=jnp.bfloat16):
    array = scale * jax.random.normal(stream_key, extent, jnp.float32)
    if cuts:
        array = array * block_scale(stream_key, extent, cuts, -0.22, 0.18)
    return jnp.clip(array, -most, most).astype(held_as)


def setup_inputs(seed: int = 0) -> dict:
    key_of = jax.random.split(jax.random.key(seed), 10)
    history = centred(key_of[0], (HIST, TOKENS, D), 1.0, 6.0, ((1, 32),))
    depth_weights = jnp.clip(jax.random.uniform(key_of[1], (HIST,), jnp.float32, -0.6, 0.6), -0.6, 0.6)
    gain_attn = jnp.clip(1.0 + 0.15 * jax.random.normal(key_of[2], (D,), jnp.float32), 0.25, 1.75)
    gain_mlp = jnp.clip(1.0 + 0.15 * jax.random.normal(key_of[3], (D,), jnp.float32), 0.25, 1.75)
    qkv_weight = centred(key_of[4], (3, D, D), D ** -0.5, 0.21875, ((2, 2),))
    out_weight = centred(key_of[5], (D, D), (D // 16) ** -0.5, 0.875, ((0, 2),))
    up_weight = centred(key_of[6], (D, FF), D ** -0.5, 0.21875, ((1, 2),))
    down_weight = centred(key_of[7], (FF, D), FF ** -0.5, 0.109375, ((0, 2),))
    cotangent = centred(key_of[8], (TOKENS, D), 1.0, 6.0, ((0, 32),))
    return {"history": history, "depth_weights": depth_weights, "gain_attn": gain_attn, "gain_mlp": gain_mlp, "qkv_weight": qkv_weight, "out_weight": out_weight, "up_weight": up_weight, "down_weight": down_weight, "cotangent": cotangent}


EPSILON = 1e-05
PRECISION = lax.Precision.HIGHEST
SQRT_HALF = 0.7071067811865476

@jax.custom_vjp
def low(v):
    return lax.optimization_barrier(v.astype(jnp.bfloat16)).astype(jnp.float32)

@jax.custom_vjp
def low_back(v):
    return v

def low_keep(v):
    return (low(v), None)

def low_pass(kept, grad):
    return (grad,)

def back_keep(v):
    return (v, None)

def back_low(kept, grad):
    return (low(grad),)
low.defvjp(low_keep, low_pass)
low_back.defvjp(back_keep, back_low)

def layer_norm(inputs, gain_row):
    row_mean = lax.optimization_barrier(jnp.mean(inputs, axis=-1, keepdims=True))
    centered = inputs - row_mean
    variance = lax.optimization_barrier(jnp.mean(centered * centered, axis=-1, keepdims=True))
    return centered * lax.rsqrt(variance + EPSILON) * gain_row

def gelu_value(inputs):
    return 0.5 * inputs * (1.0 + lax.erf(inputs * SQRT_HALF))

def attend(packed):
    queries, key_rows, value_rows = packed
    length = queries.shape[0]
    scores = low_back(jnp.einsum('qhe,khe->hqk', queries, key_rows, precision=PRECISION) * HEAD_DIM ** (-0.5))
    row_ids = lax.broadcasted_iota(jnp.int32, (length, length), 0)
    col_ids = lax.broadcasted_iota(jnp.int32, (length, length), 1)
    scores = jnp.where((col_ids <= row_ids)[None], scores, -jnp.inf)
    row_max = lax.optimization_barrier(jnp.max(scores, axis=-1, keepdims=True))
    exponent = jnp.exp(scores - row_max)
    attn_probs = low(exponent / lax.optimization_barrier(jnp.sum(exponent, axis=-1, keepdims=True)))
    return jnp.einsum('hqk,khe->qhe', attn_probs, value_rows, precision=PRECISION)

def forward(history, depth_weights, gain_attn, gain_mlp, qkv_weight, out_weight, up_weight, down_weight):
    mixed_rows = jnp.einsum('j,jtd->td', depth_weights, history, precision=PRECISION)
    first = low(layer_norm(mixed_rows, gain_attn))
    qkv_rows = low_back(low(jnp.einsum('td,cde->cte', first, qkv_weight, precision=PRECISION)))
    seq_count = qkv_rows.shape[1] // SEQ_LEN
    shaped = qkv_rows.reshape(3, seq_count, SEQ_LEN, HEADS, HEAD_DIM)
    attended = lax.map(jax.checkpoint(attend), (shaped[0], shaped[1], shaped[2]))
    attended = low_back(low(attended.reshape(seq_count * SEQ_LEN, D)))
    branch = low_back(jnp.dot(attended, out_weight, precision=PRECISION))
    middle = mixed_rows + branch
    second = low(layer_norm(middle, gain_mlp))
    pre_act = low_back(jnp.dot(second, up_weight, precision=PRECISION))
    hidden = low(gelu_value(pre_act))
    result = low_back(jnp.dot(hidden, down_weight, precision=PRECISION))
    return middle + result

def reference(history, depth_weights, gain_attn, gain_mlp, qkv_weight, out_weight, up_weight, down_weight, cotangent):
    float_args = (history.astype(jnp.float32), depth_weights, gain_attn, gain_mlp, qkv_weight.astype(jnp.float32), out_weight.astype(jnp.float32), up_weight.astype(jnp.float32), down_weight.astype(jnp.float32))
    output, pullback = jax.vjp(forward, *float_args)
    grads_all = pullback(cotangent.astype(jnp.float32))
    return (output.astype(jnp.bfloat16), grads_all[0].astype(jnp.bfloat16), grads_all[1], grads_all[2], grads_all[3], grads_all[4], grads_all[5], grads_all[6], grads_all[7])
```

```python
import jax
import jax.numpy as jnp
from jax import lax
from jax.sharding import PartitionSpec as P

HEAD_DIM = 64
SEQ_LEN = 1024


EPSILON = 1e-05
SQRT_HALF = 0.7071067811865476
INV_ROOT_TWO_PI = 0.3989422804014327


def layer_norm(inputs, gain_row):
    row_mean = jnp.mean(inputs, axis=-1, keepdims=True)
    centered = inputs - row_mean
    variance = jnp.mean(centered * centered, axis=-1, keepdims=True)
    inv_scale = lax.rsqrt(variance + EPSILON)
    normed = centered * inv_scale
    return (normed * gain_row, normed, inv_scale)


def norm_back(grad_rows, gain_row, normed, inv_scale):
    scaled = grad_rows * gain_row
    first_mean = jnp.mean(scaled, axis=-1, keepdims=True)
    second_mean = jnp.mean(scaled * normed, axis=-1, keepdims=True)
    return (
        inv_scale * (scaled - first_mean - normed * second_mean),
        jnp.sum(grad_rows * normed, axis=0),
    )


def gelu_value(inputs):
    return 0.5 * inputs * (1.0 + lax.erf(inputs * SQRT_HALF))


def gelu_slope(inputs):
    normal_cdf = 0.5 * (1.0 + lax.erf(inputs * SQRT_HALF))
    return normal_cdf + inputs * jnp.exp(-0.5 * inputs * inputs) * INV_ROOT_TWO_PI


def masked_scores(queries, key_rows):
    length = queries.shape[0]
    scores = jnp.einsum(
        "qhe,khe->hqk", queries, key_rows, preferred_element_type=jnp.float32
    ) * HEAD_DIM ** (-0.5)
    row_ids = lax.broadcasted_iota(jnp.int32, (length, length), 0)
    col_ids = lax.broadcasted_iota(jnp.int32, (length, length), 1)
    return jnp.where((col_ids <= row_ids)[None], scores, -jnp.inf)


def attend_block(packed):
    queries, key_rows, value_rows = packed
    scores = masked_scores(queries, key_rows)
    row_max = jnp.max(scores, axis=-1, keepdims=True)
    exponent = jnp.exp(scores - row_max)
    row_total = jnp.sum(exponent, axis=-1, keepdims=True)
    attn_probs = (exponent / row_total).astype(jnp.bfloat16)
    attended = jnp.einsum(
        "hqk,khe->qhe", attn_probs, value_rows, preferred_element_type=jnp.float32
    )
    return (attended.astype(jnp.bfloat16), row_max + jnp.log(row_total))


def attend_back(packed):
    queries, key_rows, value_rows, grad_att, log_total = packed
    scale_factor = HEAD_DIM ** (-0.5)
    attn_probs = jnp.exp(masked_scores(queries, key_rows) - log_total)
    grad_values = jnp.einsum(
        "hqk,qhe->khe",
        attn_probs.astype(jnp.bfloat16),
        grad_att,
        preferred_element_type=jnp.float32,
    )
    grad_probs = jnp.einsum(
        "qhe,khe->hqk", grad_att, value_rows, preferred_element_type=jnp.float32
    )
    row_dot = jnp.sum(grad_probs * attn_probs, axis=-1, keepdims=True)
    grad_scores = (attn_probs * (grad_probs - row_dot)).astype(jnp.bfloat16)
    grad_queries = (
        jnp.einsum("hqk,khe->qhe", grad_scores, key_rows, preferred_element_type=jnp.float32)
        * scale_factor
    )
    grad_keys = (
        jnp.einsum("hqk,qhe->khe", grad_scores, queries, preferred_element_type=jnp.float32)
        * scale_factor
    )
    return (
        grad_queries.astype(jnp.bfloat16),
        grad_keys.astype(jnp.bfloat16),
        grad_values.astype(jnp.bfloat16),
    )


def mp_swap(rows):
    return lax.ppermute(rows, "mp", [(0, 1), (1, 0)])


def mp_gather(rows):
    other = mp_swap(rows)
    at_zero = lax.axis_index("mp") == 0
    return jnp.concatenate(
        [jnp.where(at_zero, rows, other), jnp.where(at_zero, other, rows)], axis=0
    )


def mp_scatter_sum(rows):
    half = rows.shape[0] // 2
    at = lax.axis_index("mp")
    mine = lax.dynamic_slice_in_dim(rows, at * half, half, 0)
    sent = lax.dynamic_slice_in_dim(rows, (1 - at) * half, half, 0).astype(jnp.bfloat16)
    return mine + mp_swap(sent).astype(jnp.float32)


def shards(
    history,
    depth_weights,
    gain_attn,
    gain_mlp,
    qkv_weight,
    out_weight,
    up_weight,
    down_weight,
    cotangent,
):
    mixed_rows = depth_weights[0] * history[0].astype(jnp.float32)
    for layer_index in range(1, history.shape[0]):
        mixed_rows = mixed_rows + depth_weights[layer_index] * history[layer_index].astype(
            jnp.float32
        )
    first_out, first_normed, first_inv = layer_norm(mixed_rows, gain_attn)
    first_rows = mp_gather(first_out.astype(jnp.bfloat16))
    all_rows = first_rows.shape[0]
    local_width = qkv_weight.shape[2]
    head_local = local_width // HEAD_DIM
    seq_count = all_rows // SEQ_LEN
    qkv_rows = jnp.einsum(
        "td,cde->cte", first_rows, qkv_weight, preferred_element_type=jnp.float32
    ).astype(jnp.bfloat16)
    shaped = qkv_rows.reshape(3, seq_count, SEQ_LEN, head_local, HEAD_DIM)
    attended, log_total = lax.map(attend_block, (shaped[0], shaped[1], shaped[2]))
    attended = attended.reshape(all_rows, local_width)

    def out_term():
        return jnp.dot(attended, out_weight, preferred_element_type=jnp.float32)

    branch = mp_scatter_sum(out_term())
    middle = mixed_rows + branch
    second_out, second_normed, second_inv = layer_norm(middle, gain_mlp)
    second_rows = mp_gather(second_out.astype(jnp.bfloat16))
    pre_act = jnp.dot(second_rows, up_weight, preferred_element_type=jnp.float32)
    hidden = gelu_value(pre_act).astype(jnp.bfloat16)
    hidden_part = hidden
    block_out = (
        middle
        + mp_scatter_sum(jnp.dot(hidden_part, down_weight, preferred_element_type=jnp.float32))
    ).astype(jnp.bfloat16)
    contract_rows = (((0,), (0,)), ((), ()))
    contract_cols = (((1,), (1,)), ((), ()))
    block_rows = mp_gather(cotangent)
    hidden_part = hidden
    grad_down_w = lax.dot_general(
        hidden_part, block_rows, contract_rows, preferred_element_type=jnp.float32
    )
    hidden_rows = lax.dot_general(
        block_rows, down_weight, contract_cols, preferred_element_type=jnp.float32
    )
    grad_hidden = hidden_rows
    grad_down, grad_hidden = (grad_down_w, grad_hidden)
    grad_pre = (grad_hidden * gelu_slope(pre_act)).astype(jnp.bfloat16)
    grad_up = lax.dot_general(
        second_rows, grad_pre, contract_rows, preferred_element_type=jnp.float32
    )
    grad_second = mp_scatter_sum(
        lax.dot_general(grad_pre, up_weight, contract_cols, preferred_element_type=jnp.float32)
    )
    middle_part, grad_gain_mlp = norm_back(grad_second, gain_mlp, second_normed, second_inv)
    grad_middle = cotangent.astype(jnp.float32) + middle_part
    block_rows = mp_gather(grad_middle.astype(jnp.bfloat16))
    grad_out_w = lax.dot_general(
        attended, block_rows, contract_rows, preferred_element_type=jnp.float32
    )
    att_rows = lax.dot_general(
        block_rows, out_weight, contract_cols, preferred_element_type=jnp.float32
    )
    grad_att = att_rows
    grad_out_proj, grad_att = (grad_out_w, grad_att)
    grad_att = grad_att.astype(jnp.bfloat16).reshape(seq_count, SEQ_LEN, head_local, HEAD_DIM)
    attn_grads = lax.map(attend_back, (shaped[0], shaped[1], shaped[2], grad_att, log_total))
    grad_rows_qkv = jnp.stack(attn_grads).reshape(3, all_rows, local_width)
    grad_qkv = jnp.einsum(
        "td,cte->cde", first_rows, grad_rows_qkv, preferred_element_type=jnp.float32
    )
    grad_first = mp_scatter_sum(
        jnp.einsum("cte,cde->td", grad_rows_qkv, qkv_weight, preferred_element_type=jnp.float32)
    )
    mixed_part, grad_gain_attn = norm_back(grad_first, gain_attn, first_normed, first_inv)
    grad_mixed = grad_middle + mixed_part
    grad_history = (depth_weights[:, None, None] * grad_mixed[None]).astype(jnp.bfloat16)
    depth_terms = [
        jnp.sum(history[layer_index].astype(jnp.float32) * grad_mixed)
        for layer_index in range(history.shape[0])
    ]
    grad_depth = jnp.stack(depth_terms)
    grad_gain_attn, grad_gain_mlp, grad_depth = lax.psum(
        (grad_gain_attn, grad_gain_mlp, grad_depth), ("dp", "mp")
    )

    def dp_sum(grad):
        return lax.psum(grad.astype(jnp.bfloat16), "dp").astype(jnp.float32)

    grad_down = dp_sum(grad_down)
    grad_up = dp_sum(grad_up)
    grad_out_proj = dp_sum(grad_out_proj)
    grad_qkv = dp_sum(grad_qkv)
    return (
        block_out,
        grad_history,
        grad_depth,
        grad_gain_attn,
        grad_gain_mlp,
        grad_qkv,
        grad_out_proj,
        grad_up,
        grad_down,
    )


def solution(mesh):
    in_specs = (
        P(None, ("dp", "mp"), None),
        P(),
        P(),
        P(),
        P(None, None, "mp"),
        P("mp", None),
        P(None, "mp"),
        P("mp", None),
        P(("dp", "mp"), None),
    )
    out_specs = (
        P(("dp", "mp"), None),
        P(None, ("dp", "mp"), None),
        P(),
        P(),
        P(),
        P(None, None, "mp"),
        P("mp", None),
        P(None, "mp"),
        P("mp", None),
    )
    return jax.shard_map(shards, mesh=mesh, in_specs=in_specs, out_specs=out_specs, check_vma=False)
```

```python
import functools

import jax
import jax.numpy as jnp
from jax import lax
from jax.experimental import pallas as pl
from jax.experimental.pallas import tpu as pltpu
from jax.sharding import PartitionSpec as P

HEAD_DIM = 64
EPSILON = 1e-05
SQRT_HALF = 0.7071067811865476
INV_ROOT_TWO_PI = 0.3989422804014327
LOG2E = 1.4426950408889634
NEG = -1e30
TILE = 256
ROW_BLOCK = 128
VMEM_BYTES = 48 * 2**20

PLAIN = (((1,), (0,)), ((), ()))
CONTRACT_COLS = (((1,), (1,)), ((), ()))
CONTRACT_ROWS = (((0,), (0,)), ((), ()))


def dot(lhs, rhs, dims=PLAIN):
    return lax.dot_general(lhs, rhs, dims, preferred_element_type=jnp.float32)


def cost(flops, moved, exps=0):
    return pl.CostEstimate(flops=flops, bytes_accessed=moved, transcendentals=exps)


def params():
    return pltpu.CompilerParams(vmem_limit_bytes=VMEM_BYTES)


def normalize(inputs):
    row_mean = jnp.mean(inputs, axis=-1, keepdims=True)
    centered = inputs - row_mean
    variance = jnp.mean(centered * centered, axis=-1, keepdims=True)
    inv_scale = lax.rsqrt(variance + EPSILON)
    return centered * inv_scale, inv_scale


def norm_back(grad_rows, gain_row, normed, inv_scale):
    scaled = grad_rows * gain_row
    first_mean = jnp.mean(scaled, axis=-1, keepdims=True)
    second_mean = jnp.mean(scaled * normed, axis=-1, keepdims=True)
    return inv_scale * (scaled - first_mean - normed * second_mean)


def gelu_value(inputs):
    return 0.5 * inputs * (1.0 + lax.erf(inputs * SQRT_HALF))


def gelu_slope(inputs):
    normal_cdf = 0.5 * (1.0 + lax.erf(inputs * SQRT_HALF))
    return normal_cdf + inputs * jnp.exp(-0.5 * inputs * inputs) * INV_ROOT_TWO_PI


def mix_kernel(weights_ref, history_ref, gain_ref, mixed_ref, first_ref):
    mixed = weights_ref[0] * history_ref[0].astype(jnp.float32)
    for layer in range(1, history_ref.shape[0]):
        mixed = mixed + weights_ref[layer] * history_ref[layer].astype(jnp.float32)
    mixed_ref[...] = mixed
    normed, _ = normalize(mixed)
    first_ref[...] = (normed * gain_ref[...]).astype(jnp.bfloat16)


def mix(weights, history, gain):
    layers, rows, width = history.shape
    return pl.pallas_call(
        mix_kernel,
        grid=(rows // ROW_BLOCK,),
        in_specs=[
            pl.BlockSpec(memory_space=pltpu.SMEM),
            pl.BlockSpec((layers, ROW_BLOCK, width), lambda i: (0, i, 0)),
            pl.BlockSpec((1, width), lambda i: (0, 0)),
        ],
        out_specs=[
            pl.BlockSpec((ROW_BLOCK, width), lambda i: (i, 0)),
            pl.BlockSpec((ROW_BLOCK, width), lambda i: (i, 0)),
        ],
        out_shape=[
            jax.ShapeDtypeStruct((rows, width), jnp.float32),
            jax.ShapeDtypeStruct((rows, width), jnp.bfloat16),
        ],
        compiler_params=params(),
        cost_estimate=cost(30 * rows * width, 22 * rows * width),
        name="mix",
    )(weights, history, gain[None])


def unmix_kernel(
    weights_ref, history_ref, gain_ref, mixed_ref, middle_ref, own_ref, other_ref,
    grads_ref, gain_grad_ref, depth_ref,
):
    grad_first = own_ref[...] + other_ref[...].astype(jnp.float32)
    normed, inv_scale = normalize(mixed_ref[...])
    grad_mixed = middle_ref[...] + norm_back(grad_first, gain_ref[...], normed, inv_scale)
    gain_term = jnp.sum(grad_first * normed, axis=0, keepdims=True)
    step = pl.program_id(0)

    @pl.when(step == 0)
    def _():
        gain_grad_ref[...] = jnp.zeros_like(gain_grad_ref)
        depth_ref[...] = jnp.zeros_like(depth_ref)

    gain_grad_ref[...] += gain_term
    for layer in range(history_ref.shape[0]):
        grads_ref[layer] = (weights_ref[layer] * grad_mixed).astype(jnp.bfloat16)
        product = history_ref[layer].astype(jnp.float32) * grad_mixed
        depth_ref[layer : layer + 1] += jnp.sum(product, axis=0, keepdims=True)


def unmix(weights, history, gain, mixed, grad_middle, own, other):
    layers, rows, width = history.shape
    row_spec = pl.BlockSpec((ROW_BLOCK, width), lambda i: (i, 0))
    layer_spec = pl.BlockSpec((layers, ROW_BLOCK, width), lambda i: (0, i, 0))
    return pl.pallas_call(
        unmix_kernel,
        grid=(rows // ROW_BLOCK,),
        in_specs=[
            pl.BlockSpec(memory_space=pltpu.SMEM),
            layer_spec,
            pl.BlockSpec((1, width), lambda i: (0, 0)),
            row_spec,
            row_spec,
            row_spec,
            row_spec,
        ],
        out_specs=[
            layer_spec,
            pl.BlockSpec((1, width), lambda i: (0, 0)),
            pl.BlockSpec((layers, width), lambda i: (0, 0)),
        ],
        out_shape=[
            jax.ShapeDtypeStruct(history.shape, jnp.bfloat16),
            jax.ShapeDtypeStruct((1, width), jnp.float32),
            jax.ShapeDtypeStruct((layers, width), jnp.float32),
        ],
        compiler_params=params(),
        cost_estimate=cost(60 * rows * width, 46 * rows * width),
        name="unmix",
    )(weights, history, gain[None], mixed, grad_middle, own, other)


def head_mask(head):
    lanes = lax.broadcasted_iota(jnp.int32, (1, 2 * HEAD_DIM), 1)
    return (lanes // HEAD_DIM) == head


def future_mask():
    keys = lax.broadcasted_iota(jnp.int32, (TILE, TILE), 0)
    asks = lax.broadcasted_iota(jnp.int32, (TILE, TILE), 1)
    return keys > asks


def attend_kernel(at_ref, qkv_ref, out_ref, lse_ref):
    rows = out_ref.shape[1]
    tiles = rows // TILE
    first = at_ref[0]
    scale = HEAD_DIM ** (-0.5) * LOG2E
    places = (first, 1 - first)
    later = future_mask()
    half_keys = [qkv_ref[1, places[half]] for half in range(2)]
    half_values = [qkv_ref[2, places[half]].T for half in range(2)]
    for half in range(2):
        for tile in range(tiles):
            at_rows = pl.ds(tile * TILE, TILE)
            queries = qkv_ref[0, places[half], at_rows, :]
            outs = []
            for head in range(2):
                asked = jnp.where(head_mask(head), queries, jnp.zeros_like(queries))
                spans = []
                if half == 1:
                    spans.append((0, 0, rows))
                if tile > 0:
                    spans.append((half, 0, tile * TILE))
                spans.append((half, tile * TILE, TILE))
                scores = [
                    dot(half_keys[where][start : start + size], asked, CONTRACT_COLS)
                    for where, start, size in spans
                ]
                scores[-1] = jnp.where(later, NEG, scores[-1])
                top = functools.reduce(
                    jnp.maximum, [jnp.max(part, axis=0, keepdims=True) for part in scores]
                )
                top = top * scale
                total = 0.0
                summed = 0.0
                for part, (where, start, size) in zip(scores, spans):
                    weight = jnp.exp2(part * scale - top)
                    total = total + jnp.sum(weight, axis=0, keepdims=True)
                    summed = summed + dot(
                        half_values[where][head * HEAD_DIM : (head + 1) * HEAD_DIM, start : start + size],
                        weight.astype(jnp.bfloat16),
                    )
                outs.append(summed / total)
                lse_ref[0, head, half, :, at_rows] = top + jnp.log2(total)
            joined = jnp.concatenate(outs, axis=0).T
            out_ref[places[half], at_rows, :] = joined.astype(jnp.bfloat16)


def attend(at, qkv):
    rows = qkv.shape[2]
    width = qkv.shape[3]
    pairs = width // (2 * HEAD_DIM)
    return pl.pallas_call(
        attend_kernel,
        grid_spec=pltpu.PrefetchScalarGridSpec(
            num_scalar_prefetch=1,
            grid=(pairs,),
            in_specs=[pl.BlockSpec((3, 2, rows, 2 * HEAD_DIM), lambda i, at: (0, 0, 0, i))],
            out_specs=[
                pl.BlockSpec((2, rows, 2 * HEAD_DIM), lambda i, at: (0, 0, i)),
                pl.BlockSpec((1, 2, 2, 1, rows), lambda i, at: (i, 0, 0, 0, 0)),
            ],
        ),
        out_shape=[
            jax.ShapeDtypeStruct((2, rows, width), jnp.bfloat16),
            jax.ShapeDtypeStruct((pairs, 2, 2, 1, rows), jnp.float32),
        ],
        compiler_params=params(),
        cost_estimate=cost(24 * rows * rows * width, 10 * rows * width, 8 * rows * rows),
        name="attend",
    )(at, qkv)


def attend_back_kernel(at_ref, qkv_ref, grad_ref, att_ref, lse_ref, out_ref):
    rows = grad_ref.shape[1]
    tiles = rows // TILE
    first = at_ref[0]
    plain = HEAD_DIM ** (-0.5)
    scale = plain * LOG2E
    places = (first, 1 - first)
    later = future_mask()
    bf16 = jnp.bfloat16
    grads = [grad_ref[places[half]] for half in range(2)]
    queries = [qkv_ref[0, places[half]] for half in range(2)]
    keys = [qkv_ref[1, places[half]] for half in range(2)]
    values = [qkv_ref[2, places[half]] for half in range(2)]
    keys_t = [part.T for part in keys]
    deltas = []
    for half in range(2):
        product = grads[half].astype(jnp.float32) * att_ref[places[half]].astype(jnp.float32)
        product = product.T
        deltas.append([
            jnp.sum(product[head * HEAD_DIM : (head + 1) * HEAD_DIM], axis=0, keepdims=True)
            for head in range(2)
        ])
    masked = [head_mask(head) for head in range(2)]

    def only(head, part):
        return jnp.where(masked[head], part, jnp.zeros_like(part))

    chunks = [(half, tile) for half in range(2) for tile in range(tiles)]
    key_grads = [[None, None] for _ in chunks]
    value_grads = [[None, None] for _ in chunks]
    for ask, (ask_half, ask_tile) in enumerate(chunks):
        ask_rows = slice(ask_tile * TILE, (ask_tile + 1) * TILE)
        query_grads = []
        for head in range(2):
            asked = only(head, queries[ask_half][ask_rows])
            grad = only(head, grads[ask_half][ask_rows])
            lse = lse_ref[0, head, ask_half, :, ask_rows]
            delta = deltas[ask_half][head][:, ask_rows]
            query_grad = None
            for key in range(ask + 1):
                key_half, key_tile = chunks[key]
                key_rows = slice(key_tile * TILE, (key_tile + 1) * TILE)
                scores = dot(keys[key_half][key_rows], asked, CONTRACT_COLS)
                probs = jnp.exp2(scores * scale - lse)
                if key == ask:
                    probs = jnp.where(later, 0.0, probs)
                grad_probs = dot(values[key_half][key_rows], grad, CONTRACT_COLS)
                grad_scores = (probs * (grad_probs - delta)).astype(bf16)
                value_term = dot(probs.astype(bf16), grad)
                key_term = dot(grad_scores, asked)
                query_term = dot(
                    keys_t[key_half][head * HEAD_DIM : (head + 1) * HEAD_DIM, key_rows], grad_scores
                )
                query_grad = query_term if query_grad is None else query_grad + query_term
                for sums, term in ((key_grads, key_term), (value_grads, value_term)):
                    old = sums[key][0]
                    sums[key][0] = term if old is None else old + term
            query_grads.append(query_grad)
        joined = (jnp.concatenate(query_grads, axis=0) * plain).T
        out_ref[0, places[ask_half], pl.ds(ask_tile * TILE, TILE), :] = joined.astype(bf16)
    for key, (half, tile) in enumerate(chunks):
        at_rows = pl.ds(tile * TILE, TILE)
        out_ref[1, places[half], at_rows, :] = (key_grads[key][0] * plain).astype(bf16)
        out_ref[2, places[half], at_rows, :] = value_grads[key][0].astype(bf16)


def attend_back(at, pair, qkv, grad, attended, lse):
    rows = qkv.shape[2]
    width = qkv.shape[3]
    return pl.pallas_call(
        attend_back_kernel,
        grid_spec=pltpu.PrefetchScalarGridSpec(
            num_scalar_prefetch=1,
            grid=(1,),
            in_specs=[
                pl.BlockSpec((3, 2, rows, 2 * HEAD_DIM), lambda i, at: (0, 0, 0, pair)),
                pl.BlockSpec((2, rows, 2 * HEAD_DIM), lambda i, at: (0, 0, pair)),
                pl.BlockSpec((2, rows, 2 * HEAD_DIM), lambda i, at: (0, 0, pair)),
                pl.BlockSpec((1, 2, 2, 1, rows), lambda i, at: (pair, 0, 0, 0, 0)),
            ],
            out_specs=pl.BlockSpec((3, 2, rows, 2 * HEAD_DIM), lambda i, at: (0, 0, 0, 0)),
        ),
        out_shape=jax.ShapeDtypeStruct((3, 2, rows, 2 * HEAD_DIM), jnp.bfloat16),
        compiler_params=params(),
        cost_estimate=cost(20 * rows * rows * 2 * HEAD_DIM, 10 * rows * width, 3 * rows * rows),
        name="attend_back",
    )(at, qkv, grad, attended, lse)


def mp_swap(rows):
    return lax.ppermute(rows, "mp", [(0, 1), (1, 0)])


def both(own):
    return jnp.concatenate([own, mp_swap(own)], axis=0)


def bit_swap(rows, bit):
    size = lax.axis_size("dp")
    return lax.ppermute(rows, "dp", [(i, i ^ (1 << bit)) for i in range(size)])


def bit_orders():
    count = lax.axis_size("dp").bit_length() - 1
    low, high = list(range(min(count, 3))), list(range(min(count, 3), count))
    return [low[turn:] + low[:turn] + high for turn in range(3)]


def my_bit(bit):
    return (lax.axis_index("dp") >> bit) & 1


def half_sent(part, bit):
    half = part.shape[0] // 2
    return lax.dynamic_slice_in_dim(part, (1 - my_bit(bit)) * half, half, 0)


def half_added(part, came, bit):
    half = part.shape[0] // 2
    kept = lax.dynamic_slice_in_dim(part, my_bit(bit) * half, half, 0)
    return (kept.astype(jnp.float32) + came.astype(jnp.float32)).astype(part.dtype)


def halves_joined(part, came, bit):
    at_zero = my_bit(bit) == 0
    return jnp.concatenate(
        [jnp.where(at_zero, part, came), jnp.where(at_zero, came, part)], axis=0
    )


def phase(sends, work, *operands):
    arrays = [array for array, _ in sends]
    arrays, operands = lax.optimization_barrier((arrays, operands))
    came = [bit_swap(array, bit) for array, (_, bit) in zip(arrays, sends)]
    return lax.optimization_barrier((came, work(*operands)))


def sum_sends(parts, step):
    return [(half_sent(part, order[step]), order[step]) for part, order in zip(parts, bit_orders())]


def sum_takes(parts, came, step):
    return [
        half_added(part, other, order[step])
        for part, other, order in zip(parts, came, bit_orders())
    ]


def join_sends(parts, step):
    return [(part, order[-1 - step]) for part, order in zip(parts, bit_orders())]


def join_takes(parts, came, step):
    return [
        halves_joined(part, other, order[-1 - step])
        for part, other, order in zip(parts, came, bit_orders())
    ]


def blocked(grad):
    return grad.reshape(lax.axis_size("dp"), -1, grad.shape[-1])


def bands(grad, count):
    return jnp.split(grad, count, axis=-1)


def flat(blocks, start, size):
    return blocks[:, start : start + size].reshape(-1, blocks.shape[-1])


def shards(
    history,
    depth_weights,
    gain_attn,
    gain_mlp,
    qkv_weight,
    out_weight,
    up_weight,
    down_weight,
    cotangent,
):
    bf16, f32 = jnp.bfloat16, jnp.float32
    rows, width = cotangent.shape
    local_width = qkv_weight.shape[2]
    pairs = local_width // (2 * HEAD_DIM)
    steps = lax.axis_size("dp").bit_length() - 1
    at = lax.axis_index("mp").astype(jnp.int32)[None]

    cot_rows = both(cotangent)
    mixed, first = mix(depth_weights, history, gain_attn)
    first_rows = both(first)
    qkv = jnp.einsum("td,cde->cte", first_rows, qkv_weight, preferred_element_type=f32).astype(bf16)
    qkv = qkv.reshape(3, 2, rows, local_width)
    attended, log_total = attend(at, qkv)
    out_other = mp_swap(dot(attended[1], out_weight).astype(bf16))
    middle = mixed + dot(attended[0], out_weight) + out_other.astype(f32)
    second_normed, second_inv = normalize(middle)
    second = (second_normed * gain_mlp).astype(bf16)
    second_rows = both(second)
    pre_act = dot(second_rows, up_weight)
    hidden = gelu_value(pre_act).astype(bf16)
    grad_hidden = dot(cot_rows, down_weight, CONTRACT_COLS)
    grad_pre = (grad_hidden * gelu_slope(pre_act)).astype(bf16)
    grad_down = dot(hidden, cot_rows, CONTRACT_ROWS).astype(bf16)
    grad_up = dot(second_rows, grad_pre, CONTRACT_ROWS).astype(bf16)
    down_bands, up_bands = bands(grad_down, 3), bands(grad_up, 6)
    mlp = [
        jnp.concatenate(
            [blocked(down_bands[i]), blocked(up_bands[2 * i]), blocked(up_bands[2 * i + 1])], axis=1
        )
        for i in range(3)
    ]

    def back_to_attention(grad_pre):
        second_other = mp_swap(dot(grad_pre[rows:], up_weight, CONTRACT_COLS).astype(bf16))
        grad_second = dot(grad_pre[:rows], up_weight, CONTRACT_COLS) + second_other.astype(f32)
        gain_term = jnp.sum(grad_second * second_normed, axis=0)
        grad_middle = cotangent.astype(f32) + norm_back(
            grad_second, gain_mlp, second_normed, second_inv
        )
        middle_rows = both(grad_middle.astype(bf16))
        grad_att = dot(middle_rows, out_weight, CONTRACT_COLS).astype(bf16)
        return gain_term, grad_middle, middle_rows, grad_att.reshape(2, rows, local_width)

    sends = sum_sends(mlp, 0)
    came, (grad_gain_mlp, grad_middle, middle_rows, grad_att) = phase(
        sends, back_to_attention, grad_pre
    )
    mlp = sum_takes(mlp, came, 0)

    def back_pairs(count):
        def work(grad_att, done):
            for pair in range(len(done), min(pairs, len(done) + count)):
                done = done + [attend_back(at, pair, qkv, grad_att, attended, log_total)]
            return grad_att, done

        return work

    done = []
    for step in range(1, steps):
        count = -(-pairs // max(1, steps - 1))
        came, (grad_att, done) = phase(sum_sends(mlp, step), back_pairs(count), grad_att, done)
        mlp = sum_takes(mlp, came, step)
    _, done = back_pairs(pairs)(grad_att, done)
    grad_rows = jnp.concatenate(done, axis=-1)
    grad_qkv = jnp.einsum(
        "td,cte->cde",
        first_rows,
        grad_rows.reshape(3, 2 * rows, local_width),
        preferred_element_type=f32,
    ).astype(bf16)
    grad_out = dot(
        attended.reshape(2 * rows, local_width), middle_rows, CONTRACT_ROWS
    ).astype(bf16)
    third = local_width // 3
    att = []
    for i in range(3):
        left, right = bands(grad_out[i * third : (i + 1) * third], 2)
        att.append(jnp.concatenate([blocked(grad_qkv[i]), blocked(left), blocked(right)], axis=1))

    def back_to_start(grad_rows):
        terms = [
            sum(dot(grad_rows[c, half], qkv_weight[c], CONTRACT_COLS) for c in range(3))
            for half in (1, 0)
        ]
        first_other = mp_swap(terms[0].astype(bf16))
        return terms[1], first_other

    def finish_history(own, other):
        return unmix(depth_weights, history, gain_attn, mixed, grad_middle, own, other)

    def finish_block(hidden):
        hidden_other = mp_swap(dot(hidden[rows:], down_weight).astype(bf16))
        return (middle + dot(hidden[:rows], down_weight) + hidden_other.astype(f32)).astype(bf16)

    def nothing():
        return ()

    small = None
    for step in range(steps):
        sends = join_sends(mlp, step) + sum_sends(att, step)
        if step == 0:
            came, firsts = phase(sends, back_to_start, grad_rows)
        elif step == 1:
            came, (grad_history, grad_gain_attn, depth_terms) = phase(sends, finish_history, *firsts)
            small = jnp.concatenate([grad_gain_attn[0], grad_gain_mlp, jnp.sum(depth_terms, axis=1)])
        elif step == 2:
            came, (block_out, small_other) = phase(
                sends, lambda hidden, small: (finish_block(hidden), mp_swap(small)), hidden, small
            )
            small = small + small_other
        else:
            came, _ = phase(sends, nothing)
        mlp = join_takes(mlp, came[:3], step)
        att = sum_takes(att, came[3:], step)

    for step in range(steps):
        came, _ = phase(join_sends(att, step) + [(small, step)], nothing)
        att = join_takes(att, came[:3], step)
        small = small + came[3]

    grad_gain_attn, grad_gain_mlp, grad_depth = jnp.split(small, [width, 2 * width])
    size = lax.axis_size("dp")
    tall, short = down_weight.shape[0] // size, width // size
    grad_down = jnp.concatenate([flat(part, 0, tall) for part in mlp], axis=1).astype(f32)
    grad_up = jnp.concatenate(
        [flat(part, tall + i * short, short) for part in mlp for i in range(2)], axis=1
    ).astype(f32)
    grad_qkv = jnp.stack([flat(part, 0, short) for part in att]).astype(f32)
    thin = third // size
    grad_out = jnp.concatenate(
        [
            jnp.concatenate([flat(part, short + i * thin, thin) for i in range(2)], axis=1)
            for part in att
        ],
        axis=0,
    ).astype(f32)
    return (
        block_out,
        grad_history,
        grad_depth,
        grad_gain_attn,
        grad_gain_mlp,
        grad_qkv,
        grad_out,
        grad_up,
        grad_down,
    )


def solution(mesh):
    in_specs = (
        P(None, ("dp", "mp"), None),
        P(),
        P(),
        P(),
        P(None, None, "mp"),
        P("mp", None),
        P(None, "mp"),
        P("mp", None),
        P(("dp", "mp"), None),
    )
    out_specs = (
        P(("dp", "mp"), None),
        P(None, ("dp", "mp"), None),
        P(),
        P(),
        P(),
        P(None, None, "mp"),
        P("mp", None),
        P(None, "mp"),
        P("mp", None),
    )
    return jax.shard_map(shards, mesh=mesh, in_specs=in_specs, out_specs=out_specs, check_vma=False)
```

```python
import functools

import jax
import jax.numpy as jnp
from jax import lax
from jax.experimental import pallas as pl
from jax.experimental.pallas import tpu as pltpu
from jax.sharding import PartitionSpec as P

HEAD_DIM = 64
EPSILON = 1e-05
SQRT_HALF = 0.7071067811865476
INV_ROOT_TWO_PI = 0.3989422804014327
LOG2E = 1.4426950408889634
NEG = -1e30
TILE = 256
ROW_BLOCK = 128
VMEM_BYTES = 32 * 2**20
SPLITS = 4
PAIR = 2 * HEAD_DIM
CHUNK = 512

PLAIN = (((1,), (0,)), ((), ()))
CONTRACT_COLS = (((1,), (1,)), ((), ()))
CONTRACT_ROWS = (((0,), (0,)), ((), ()))


def dot(lhs, rhs, dims=PLAIN):
    return lax.dot_general(lhs, rhs, dims, preferred_element_type=jnp.float32)


def cost(flops, moved, exps=0):
    return pl.CostEstimate(flops=flops, bytes_accessed=moved, transcendentals=exps)


def params():
    return pltpu.CompilerParams(vmem_limit_bytes=VMEM_BYTES)


def normalize(inputs):
    row_mean = jnp.mean(inputs, axis=-1, keepdims=True)
    centered = inputs - row_mean
    variance = jnp.mean(centered * centered, axis=-1, keepdims=True)
    inv_scale = lax.rsqrt(variance + EPSILON)
    return centered * inv_scale, inv_scale


def norm_back(grad_rows, gain_row, normed, inv_scale):
    scaled = grad_rows * gain_row
    first_mean = jnp.mean(scaled, axis=-1, keepdims=True)
    second_mean = jnp.mean(scaled * normed, axis=-1, keepdims=True)
    return inv_scale * (scaled - first_mean - normed * second_mean)


def gelu_value(inputs):
    return 0.5 * inputs * (1.0 + lax.erf(inputs * SQRT_HALF))


def gelu_slope(inputs):
    normal_cdf = 0.5 * (1.0 + lax.erf(inputs * SQRT_HALF))
    return normal_cdf + inputs * jnp.exp(-0.5 * inputs * inputs) * INV_ROOT_TWO_PI


def mix_kernel(weights_ref, history_ref, gain_ref, mixed_ref, first_ref):
    mixed = weights_ref[0] * history_ref[0].astype(jnp.float32)
    for layer in range(1, history_ref.shape[0]):
        mixed = mixed + weights_ref[layer] * history_ref[layer].astype(jnp.float32)
    mixed_ref[...] = mixed
    normed, _ = normalize(mixed)
    first_ref[...] = (normed * gain_ref[...]).astype(jnp.bfloat16)


def mix(weights, history, gain):
    layers, rows, width = history.shape
    return pl.pallas_call(
        mix_kernel,
        grid=(rows // ROW_BLOCK,),
        in_specs=[
            pl.BlockSpec(memory_space=pltpu.SMEM),
            pl.BlockSpec((layers, ROW_BLOCK, width), lambda i: (0, i, 0)),
            pl.BlockSpec((1, width), lambda i: (0, 0)),
        ],
        out_specs=[
            pl.BlockSpec((ROW_BLOCK, width), lambda i: (i, 0)),
            pl.BlockSpec((ROW_BLOCK, width), lambda i: (i, 0)),
        ],
        out_shape=[
            jax.ShapeDtypeStruct((rows, width), jnp.float32),
            jax.ShapeDtypeStruct((rows, width), jnp.bfloat16),
        ],
        compiler_params=params(),
        cost_estimate=cost(30 * rows * width, 22 * rows * width),
        name="mix",
    )(weights, history, gain[None])


def unmix_kernel(
    weights_ref, history_ref, gain_ref, mixed_ref, middle_ref, own_ref, other_ref, *refs
):
    grads_ref, gain_grad_ref, depth_ref = refs[-3:]
    grad_first = own_ref[...] + other_ref[...].astype(jnp.float32)
    normed, inv_scale = normalize(mixed_ref[...])
    grad_mixed = middle_ref[...] + norm_back(grad_first, gain_ref[...], normed, inv_scale)
    gain_term = jnp.sum(grad_first * normed, axis=0, keepdims=True)
    step = pl.program_id(0)

    @pl.when(step == 0)
    def _():
        gain_grad_ref[...] = jnp.zeros_like(gain_grad_ref)
        depth_ref[...] = jnp.zeros_like(depth_ref)

    gain_grad_ref[...] += gain_term
    for layer in range(history_ref.shape[0]):
        grads_ref[layer] = (weights_ref[layer] * grad_mixed).astype(jnp.bfloat16)
        product = history_ref[layer].astype(jnp.float32) * grad_mixed
        depth_ref[layer : layer + 1] += jnp.sum(product, axis=0, keepdims=True)


def unmix(weights, history, gain, mixed, grad_middle, own, other, after=()):
    layers, rows, width = history.shape
    row_spec = pl.BlockSpec((ROW_BLOCK, width), lambda i: (i, 0))
    layer_spec = pl.BlockSpec((layers, ROW_BLOCK, width), lambda i: (0, i, 0))
    return pl.pallas_call(
        unmix_kernel,
        grid=(rows // ROW_BLOCK,),
        in_specs=[
            pl.BlockSpec(memory_space=pltpu.SMEM),
            layer_spec,
            pl.BlockSpec((1, width), lambda i: (0, 0)),
            row_spec,
            row_spec,
            row_spec,
            row_spec,
        ]
        + [pl.BlockSpec(memory_space=pl.ANY)] * len(after),
        out_specs=[
            layer_spec,
            pl.BlockSpec((1, width), lambda i: (0, 0)),
            pl.BlockSpec((layers, width), lambda i: (0, 0)),
        ],
        out_shape=[
            jax.ShapeDtypeStruct(history.shape, jnp.bfloat16),
            jax.ShapeDtypeStruct((1, width), jnp.float32),
            jax.ShapeDtypeStruct((layers, width), jnp.float32),
        ],
        compiler_params=params(),
        cost_estimate=cost(1000, 1000),
        name="unmix",
    )(weights, history, gain[None], mixed, grad_middle, own, other, *after)


def head_mask(head):
    lanes = lax.broadcasted_iota(jnp.int32, (1, PAIR), 1)
    return (lanes // HEAD_DIM) == head


def future_mask():
    keys = lax.broadcasted_iota(jnp.int32, (TILE, TILE), 0)
    asks = lax.broadcasted_iota(jnp.int32, (TILE, TILE), 1)
    return keys > asks


def local_call(kernel, name, at, arrays, outs, after=(), scratch=()):
    in_vmem = pl.BlockSpec(memory_space=pltpu.VMEM)
    return pl.pallas_call(
        kernel,
        in_specs=[pl.BlockSpec(memory_space=pltpu.SMEM)]
        + [in_vmem] * len(arrays)
        + [pl.BlockSpec(memory_space=pl.ANY)] * len(after),
        out_specs=[in_vmem] * len(outs),
        out_shape=[jax.ShapeDtypeStruct(shape, dtype) for shape, dtype in outs],
        scratch_shapes=list(scratch),
        compiler_params=params(),
        cost_estimate=cost(1000, 1000),
        name=name,
    )(at, *arrays, *after)


def attend_kernel(
    at_ref, own_ref, other_ref, weight_ref, out_weight_ref,
    qkv_ref, att_ref, lse_ref, out_own_ref, out_other_ref,
):
    rows = own_ref.shape[0]
    tiles = rows // TILE
    first = at_ref[0]
    scale = HEAD_DIM ** (-0.5) * LOG2E
    places = (first, 1 - first)
    later = future_mask()

    def one_pair(pair, carry):
        lanes = pl.ds(pl.multiple_of(pair * PAIR, PAIR), PAIR)
        weight = jnp.concatenate([weight_ref[c, :, lanes] for c in range(3)], axis=1)
        for side, ref in enumerate((own_ref, other_ref)):
            made = dot(ref[...], weight).astype(jnp.bfloat16)
            for c in range(3):
                qkv_ref[c, side, :, lanes] = made[:, c * PAIR : (c + 1) * PAIR]
        half_keys = [qkv_ref[1, places[half], :, lanes] for half in range(2)]
        half_values = [qkv_ref[2, places[half], :, lanes].T for half in range(2)]
        for half in range(2):
            for tile in range(tiles):
                at_rows = pl.ds(tile * TILE, TILE)
                queries = qkv_ref[0, places[half], at_rows, lanes]
                outs = []
                for head in range(2):
                    asked = jnp.where(head_mask(head), queries, jnp.zeros_like(queries))
                    spans = []
                    if half == 1:
                        spans.append((0, 0, rows))
                    if tile > 0:
                        spans.append((half, 0, tile * TILE))
                    spans.append((half, tile * TILE, TILE))
                    scores = [
                        dot(half_keys[where][start : start + size], asked, CONTRACT_COLS)
                        for where, start, size in spans
                    ]
                    scores[-1] = jnp.where(later, NEG, scores[-1])
                    top = functools.reduce(
                        jnp.maximum, [jnp.max(part, axis=0, keepdims=True) for part in scores]
                    )
                    top = top * scale
                    total = 0.0
                    summed = 0.0
                    mine = slice(head * HEAD_DIM, (head + 1) * HEAD_DIM)
                    for part, (where, start, size) in zip(scores, spans):
                        weights = jnp.exp2(part * scale - top)
                        total = total + jnp.sum(weights, axis=0, keepdims=True)
                        summed = summed + dot(
                            half_values[where][mine, start : start + size],
                            weights.astype(jnp.bfloat16),
                        )
                    outs.append(summed / total)
                    lse_ref[pair, head, half, :, at_rows] = top + jnp.log2(total)
                joined = jnp.concatenate(outs, axis=0).T
                att_ref[places[half], at_rows, lanes] = joined.astype(jnp.bfloat16)
        return carry

    lax.fori_loop(0, att_ref.shape[2] // PAIR, one_pair, 0)
    out_other_ref[...] = dot(att_ref[1], out_weight_ref[...]).astype(jnp.bfloat16)
    out_own_ref[...] = dot(att_ref[0], out_weight_ref[...])


def attend(at, own, other, weight, out_weight):
    rows, width = own.shape
    local = weight.shape[2]
    return local_call(
        attend_kernel,
        "attend",
        at,
        [own, other, weight, out_weight],
        [
            ((3, 2, rows, local), jnp.bfloat16),
            ((2, rows, local), jnp.bfloat16),
            ((local // PAIR, 2, 2, 1, rows), jnp.float32),
            ((rows, width), jnp.float32),
            ((rows, width), jnp.bfloat16),
        ],
    )


def renorm_kernel(at_ref, mixed_ref, own_ref, other_ref, gain_ref, middle_ref, second_ref):
    middle = mixed_ref[...] + own_ref[...] + other_ref[...].astype(jnp.float32)
    middle_ref[...] = middle
    second_ref[...] = (normalize(middle)[0] * gain_ref[...]).astype(jnp.bfloat16)


def renorm(at, mixed, own, other, gain):
    return local_call(
        renorm_kernel,
        "renorm",
        at,
        [mixed, own, other, gain[None]],
        [(mixed.shape, jnp.float32), (mixed.shape, jnp.bfloat16)],
    )


def split_halves(bit, rows, top, bottom, keep_ref, send_ref):
    shape = (keep_ref.shape[0], -1, keep_ref.shape[2])
    top = top.astype(jnp.bfloat16).reshape(shape)
    bottom = bottom.astype(jnp.bfloat16).reshape(shape)
    keep_ref[:, rows, :] = jnp.where(bit == 0, top, bottom)
    send_ref[:, rows, :] = jnp.where(bit == 0, bottom, top)


def mlp_kernel(
    slots, at_ref, second_own_ref, second_other_ref, cot_own_ref, cot_other_ref, up_ref, down_ref,
    keep_a_ref, send_a_ref, keep_b_ref, send_b_ref, hidden_ref, grad_pre_ref,
):
    bf16 = jnp.bfloat16
    chunks = hidden_ref.shape[2] // CHUNK
    sides = ((second_own_ref, cot_own_ref), (second_other_ref, cot_other_ref))
    early = keep_a_ref.shape[1] * keep_a_ref.shape[0] // CHUNK
    unit = CHUNK // keep_a_ref.shape[0]

    def make(chunk):
        lanes = pl.ds(chunk * CHUNK, CHUNK)
        for side, (second_ref, cot_ref) in enumerate(sides):
            pre = dot(second_ref[...], up_ref[:, lanes])
            cdf = 0.5 * (1.0 + lax.erf(pre * SQRT_HALF))
            hidden_ref[side, :, lanes] = (pre * cdf).astype(bf16)
            slope = cdf + pre * jnp.exp(-0.5 * pre * pre) * INV_ROOT_TWO_PI
            grad_hidden = dot(cot_ref[...], down_ref[lanes, :], CONTRACT_COLS)
            grad_pre_ref[side, :, lanes] = (grad_hidden * slope).astype(bf16)

    def give(chunk):
        lanes = pl.ds(chunk * CHUNK, CHUNK)
        grad_up, grad_down = 0.0, 0.0
        for side, (second_ref, cot_ref) in enumerate(sides):
            grad_up = grad_up + dot(grad_pre_ref[side, :, lanes], second_ref[...], CONTRACT_ROWS)
            grad_down = grad_down + dot(hidden_ref[side, :, lanes], cot_ref[...], CONTRACT_ROWS)
        late = chunk >= early
        refs = (keep_b_ref, send_b_ref) if late else (keep_a_ref, send_a_ref)
        rows = pl.ds((chunk - early if late else chunk) * unit, unit)
        split_halves(at_ref[slots[late]], rows, grad_up, grad_down, *refs)

    make(0)
    for chunk in range(1, chunks):
        make(chunk)
        give(chunk - 1)
    give(chunks - 1)


def mlp(at, slots, second_own, second_other, cot_own, cot_other, up, down, after=()):
    rows, width = second_own.shape
    hidden = down.shape[0]
    blocks = 2 ** (SPLITS - 1)
    chunks = hidden // CHUNK
    early = 2 * chunks // 3
    unit = CHUNK // blocks
    pieces = [((blocks, count * unit, width), jnp.bfloat16) for count in (early, chunks - early)]
    return local_call(
        functools.partial(mlp_kernel, slots),
        "mlp",
        at,
        [second_own, second_other, cot_own, cot_other, up, down],
        [pieces[0], pieces[0], pieces[1], pieces[1]] + [((2, rows, hidden), jnp.bfloat16)] * 2,
        after,
    )


def rows_kernel(transposed, at_ref, rows_ref, weight_ref, *refs):
    own_ref, other_ref = refs[-2:]
    dims = CONTRACT_COLS if transposed else PLAIN
    other_ref[...] = dot(rows_ref[1], weight_ref[...], dims).astype(jnp.bfloat16)
    own_ref[...] = dot(rows_ref[0], weight_ref[...], dims)


def rows_times(at, name, rows, weight, transposed, after=()):
    shape = (rows.shape[1], weight.shape[0 if transposed else 1])
    return local_call(
        functools.partial(rows_kernel, transposed), name, at, [rows, weight],
        [(shape, jnp.float32), (shape, jnp.bfloat16)], after,
    )


def norm_back_kernel(at_ref, own_ref, other_ref, middle_ref, cot_ref, gain_ref, *refs):
    grad_ref, narrow_ref, gain_grad_ref = refs[-3:]
    grad_second = own_ref[...] + other_ref[...].astype(jnp.float32)
    normed, inv_scale = normalize(middle_ref[...])
    grad = cot_ref[...].astype(jnp.float32) + norm_back(
        grad_second, gain_ref[...], normed, inv_scale
    )
    grad_ref[...] = grad
    narrow_ref[...] = grad.astype(jnp.bfloat16)
    gain_grad_ref[...] = jnp.sum(grad_second * normed, axis=0, keepdims=True)


def norm_back_rows(at, own, other, middle, cotangent, gain, after=()):
    shape = own.shape
    return local_call(
        norm_back_kernel,
        "norm_back_rows",
        at,
        [own, other, middle, cotangent, gain[None]],
        [(shape, jnp.float32), (shape, jnp.bfloat16), ((1, shape[1]), jnp.float32)],
        after,
    )


def attend_back_kernel(
    slot, start, at_ref, qkv_ref, att_ref, lse_ref, grad_own_ref, grad_other_ref, out_weight_ref,
    first_own_ref, first_other_ref, *refs,
):
    keep_ref, send_ref, grad_rows_ref = refs[-3:]
    rows = grad_own_ref.shape[0]
    tiles = rows // TILE
    first = at_ref[0]
    plain = HEAD_DIM ** (-0.5)
    scale = plain * LOG2E
    places = (first, 1 - first)
    later = future_mask()
    bf16 = jnp.bfloat16
    sides = (grad_own_ref, grad_other_ref)
    firsts = (first_own_ref, first_other_ref)
    masked = [head_mask(head) for head in range(2)]
    unit = 4 * PAIR // (2 * keep_ref.shape[0])
    count = keep_ref.shape[1] // unit
    is_own = [places[half] == 0 for half in range(2)]
    chunks = [(half, tile) for half in range(2) for tile in range(tiles)]

    def only(head, part):
        return jnp.where(masked[head], part, jnp.zeros_like(part))

    def plus(old, term):
        return term if old is None else old + term

    for step in range(count):
        pair = start + step
        lanes = pl.ds(pair * PAIR, PAIR)
        outer = [
            dot(ref[...], out_weight_ref[lanes, :], CONTRACT_COLS).astype(bf16) for ref in sides
        ]
        grads = [jnp.where(is_own[half], outer[0], outer[1]) for half in range(2)]
        queries, keys, values = [
            [qkv_ref[c, places[half], :, lanes] for half in range(2)] for c in range(3)
        ]
        keys_t = [part.T for part in keys]
        deltas = []
        for half in range(2):
            attended = att_ref[places[half], :, lanes].astype(jnp.float32)
            product = (grads[half].astype(jnp.float32) * attended).T
            deltas.append([
                jnp.sum(product[head * HEAD_DIM : (head + 1) * HEAD_DIM], axis=0, keepdims=True)
                for head in range(2)
            ])
        key_grads = [None for _ in chunks]
        value_grads = [None for _ in chunks]
        query_grads = []
        for ask, (ask_half, ask_tile) in enumerate(chunks):
            ask_rows = slice(ask_tile * TILE, (ask_tile + 1) * TILE)
            sums_here = []
            for head in range(2):
                asked = only(head, queries[ask_half][ask_rows])
                grad = only(head, grads[ask_half][ask_rows])
                lse = lse_ref[pair, head, ask_half, :, ask_rows]
                delta = deltas[ask_half][head][:, ask_rows]
                query_grad = None
                for key in range(ask + 1):
                    key_half, key_tile = chunks[key]
                    key_rows = slice(key_tile * TILE, (key_tile + 1) * TILE)
                    scores = dot(keys[key_half][key_rows], asked, CONTRACT_COLS)
                    probs = jnp.exp2(scores * scale - lse)
                    if key == ask:
                        probs = jnp.where(later, 0.0, probs)
                    grad_probs = dot(values[key_half][key_rows], grad, CONTRACT_COLS)
                    grad_scores = (probs * (grad_probs - delta)).astype(bf16)
                    value_grads[key] = plus(value_grads[key], dot(probs.astype(bf16), grad))
                    key_grads[key] = plus(key_grads[key], dot(grad_scores, asked))
                    mine = slice(head * HEAD_DIM, (head + 1) * HEAD_DIM)
                    query_grad = plus(
                        query_grad, dot(keys_t[key_half][mine, key_rows], grad_scores)
                    )
                sums_here.append(query_grad)
            query_grads.append((jnp.concatenate(sums_here, axis=0) * plain).astype(bf16))
        turned = []
        for half in range(2):
            at_half = [i for i, (where, _) in enumerate(chunks) if where == half]
            query_t = jnp.concatenate([query_grads[i] for i in at_half], axis=1)
            key = jnp.concatenate([(key_grads[i] * plain).astype(bf16) for i in at_half], axis=0)
            value = jnp.concatenate([value_grads[i].astype(bf16) for i in at_half], axis=0)
            turned.append([query_t, key.T, value.T, att_ref[places[half], :, lanes].T])
            for c, part in enumerate((query_t.T, key, value)):
                grad_rows_ref[c, places[half], :, step * PAIR : (step + 1) * PAIR] = part
        top, bottom = 0.0, 0.0
        for side in range(2):
            mine = [jnp.where(is_own[side], a, b) for a, b in zip(turned[0], turned[1])]
            rows_here = firsts[side][...]
            top = top + dot(jnp.concatenate(mine[:2], axis=0), rows_here)
            bottom = bottom + jnp.concatenate(
                [dot(mine[2], rows_here), dot(mine[3], sides[side][...])], axis=0
            )
        split_halves(
            at_ref[slot], pl.ds(step * unit, unit), top, bottom, keep_ref, send_ref
        )


def attend_back(at, slot, start, count, qkv, att, lse, grad_own, grad_other, out_weight,
                first_own, first_other, after=()):
    rows, width = grad_own.shape
    blocks = 2 ** (SPLITS - 1)
    unit = 4 * PAIR // (2 * blocks)
    pieces = ((blocks, count * unit, width), jnp.bfloat16)
    return local_call(
        functools.partial(attend_back_kernel, slot, start),
        "attend_back",
        at,
        [qkv, att, lse, grad_own, grad_other, out_weight, first_own, first_other],
        [pieces, pieces, ((3, 2, rows, count * PAIR), jnp.bfloat16)],
        after,
    )


def first_back_kernel(at_ref, weight_ref, *refs):
    own_ref, other_ref = refs[-2:]
    groups = []
    start = 0
    for ref in refs[:-2]:
        if len(ref.shape) != 4:
            break
        groups.append((ref, start))
        start += ref.shape[3]
    for side, out_ref in ((1, other_ref), (0, own_ref)):
        total = 0.0
        for ref, begin in groups:
            for c in range(3):
                lanes = slice(begin, begin + ref.shape[3])
                total = total + dot(ref[c, side], weight_ref[c, :, lanes], CONTRACT_COLS)
        out_ref[...] = total.astype(out_ref.dtype)


def first_back(at, weight, groups, after=()):
    shape = (groups[0].shape[2], weight.shape[1])
    return local_call(
        first_back_kernel, "first_back", at, [weight, *groups],
        [(shape, jnp.float32), (shape, jnp.bfloat16)], after,
    )


def fold_kernel(slot, at_ref, kept_ref, came_ref, *refs):
    keep_ref, send_ref = refs[-2:]
    half = keep_ref.shape[0]
    bit = at_ref[slot]
    for target, start in ((send_ref, (1 - bit) * half), (keep_ref, bit * half)):
        for index in range(half):
            total = kept_ref[start + index].astype(jnp.float32) + came_ref[
                start + index
            ].astype(jnp.float32)
            target[index] = total.astype(jnp.bfloat16)


def add_kernel(at_ref, kept_ref, came_ref, *refs):
    total = kept_ref[...].astype(jnp.float32) + came_ref[...].astype(jnp.float32)
    refs[-1][...] = total.astype(jnp.bfloat16)


def join_kernel(slot, at_ref, mine_ref, came_ref, *refs):
    both_ref = refs[-1]
    half = mine_ref.shape[0]
    bit = at_ref[slot]
    for source, start in ((mine_ref, bit * half), (came_ref, (1 - bit) * half)):
        for index in range(half):
            both_ref[start + index] = source[index]


def fold(at, slot, kept, came, after=()):
    blocks, rows, width = kept.shape
    if blocks == 1:
        outs = [(kept.shape, jnp.bfloat16)]
        return local_call(add_kernel, "add", at, [kept, came], outs, after)[0]
    outs = [((blocks // 2, rows, width), jnp.bfloat16)] * 2
    return local_call(
        functools.partial(fold_kernel, slot), "fold", at, [kept, came], outs, after
    )


def join(at, slot, mine, came, after=()):
    blocks, rows, width = mine.shape
    outs = [((2 * blocks, rows, width), jnp.bfloat16)]
    return local_call(
        functools.partial(join_kernel, slot), "join", at, [mine, came], outs, after
    )[0]


def in_order(bit, mine, came):
    rows = mine.shape[0] * mine.shape[1]
    mine = mine.reshape(rows, -1).astype(jnp.float32)
    came = came.reshape(rows, -1).astype(jnp.float32)
    return jnp.where(bit == 0, mine, came), jnp.where(bit == 0, came, mine)


def finish_mlp_kernel(slot, at_ref, mine_ref, came_ref, *refs):
    up_ref, down_ref = refs[-2:]
    top, bottom = in_order(at_ref[slot], mine_ref[...], came_ref[...])
    up_ref[...] = top.T
    down_ref[...] = bottom


def finish_mlp(at, slot, start, mine, came, width, hidden, old=None, after=()):
    blocks, rows, _ = mine.shape
    unit = CHUNK // blocks
    part = pl.BlockSpec((blocks, unit, width), lambda i, at: (0, i, 0))
    return pl.pallas_call(
        functools.partial(finish_mlp_kernel, slot),
        grid_spec=pltpu.PrefetchScalarGridSpec(
            num_scalar_prefetch=1,
            grid=(rows // unit,),
            in_specs=[part, part]
            + [pl.BlockSpec(memory_space=pl.ANY)] * (len(old or []) + len(after)),
            out_specs=[
                pl.BlockSpec((width, CHUNK), lambda i, at: (0, start + i)),
                pl.BlockSpec((CHUNK, width), lambda i, at: (start + i, 0)),
            ],
        ),
        out_shape=[
            jax.ShapeDtypeStruct((width, hidden), jnp.float32),
            jax.ShapeDtypeStruct((hidden, width), jnp.float32),
        ],
        input_output_aliases={3: 0, 4: 1} if old else {},
        compiler_params=params(),
        cost_estimate=cost(1000, 1000),
        name="finish_mlp",
    )(at, mine, came, *(old or []), *after)


def finish_attend_kernel(slot, at_ref, mine_ref, came_ref, *refs):
    qkv_ref, out_ref = refs[-2:]
    top, bottom = in_order(at_ref[slot], mine_ref[...], came_ref[...])
    qkv_ref[0] = top[:PAIR].T
    qkv_ref[1] = top[PAIR:].T
    qkv_ref[2] = bottom[:PAIR].T
    out_ref[...] = bottom[PAIR:]


def finish_attend(at, slot, start, mine, came, width, local, old=None, after=()):
    blocks, rows, _ = mine.shape
    unit = 2 * PAIR // blocks
    part = pl.BlockSpec((blocks, unit, width), lambda i, at: (0, i, 0))
    return pl.pallas_call(
        functools.partial(finish_attend_kernel, slot),
        grid_spec=pltpu.PrefetchScalarGridSpec(
            num_scalar_prefetch=1,
            grid=(rows // unit,),
            in_specs=[part, part]
            + [pl.BlockSpec(memory_space=pl.ANY)] * (len(old or []) + len(after)),
            out_specs=[
                pl.BlockSpec((3, width, PAIR), lambda i, at: (0, 0, start + i)),
                pl.BlockSpec((PAIR, width), lambda i, at: (start + i, 0)),
            ],
        ),
        out_shape=[
            jax.ShapeDtypeStruct((3, width, local), jnp.float32),
            jax.ShapeDtypeStruct((local, width), jnp.float32),
        ],
        input_output_aliases={3: 0, 4: 1} if old else {},
        compiler_params=params(),
        cost_estimate=cost(1000, 1000),
        name="finish_attend",
    )(at, mine, came, *(old or []), *after)


def mp_swap(rows):
    return lax.ppermute(rows, "mp", [(0, 1), (1, 0)])


def dp_bits():
    return lax.axis_size("dp").bit_length() - 1


def orders(kind):
    if kind == 0:
        return (0, 1, 2, 3), (1, 0, 2, 3)
    return (2, 0, 1, 3), (2, 1, 0, 3)


def bit_swap(rows, bits):
    size, cores = lax.axis_size("dp"), lax.axis_size("mp")
    pairs = [
        (i * cores + core, (i ^ (1 << bits[core])) * cores + core)
        for i in range(size)
        for core in range(cores)
    ]
    return lax.ppermute(rows, ("dp", "mp"), pairs)


def step_bits(kind, step):
    return [order[step] for order in orders(kind)]


def slot_of(kind, step):
    return 1 + kind * SPLITS + step


def where_am_i():
    core, index = lax.axis_index("mp"), lax.axis_index("dp")
    values = [core]
    for kind in range(2):
        for step in range(SPLITS):
            bits = step_bits(kind, step)
            values.append((index >> jnp.where(core == 0, bits[0], bits[1])) & 1)
    return jnp.stack(values).astype(jnp.int32)


class Stream:
    def __init__(self, at, kind, kept, sent):
        self.at, self.kind, self.kept, self.step = at, kind, kept, 0
        self.came = bit_swap(sent, step_bits(kind, 0))

    def advance(self, after=()):
        step, kind = self.step, self.kind
        self.step += 1
        if step < SPLITS - 1:
            self.kept, sent = fold(
                self.at, slot_of(kind, step + 1), self.kept, self.came, after
            )
            self.came = bit_swap(sent, step_bits(kind, step + 1))
            return self.kept
        if step == SPLITS - 1:
            self.kept = fold(self.at, 0, self.kept, self.came, after)
            for bit in range(SPLITS, dp_bits()):
                other = bit_swap(self.kept, [bit, bit])
                self.kept = fold(self.at, 0, self.kept, other)
        else:
            bit_step = 2 * SPLITS - 1 - step
            self.kept = join(self.at, slot_of(kind, bit_step), self.kept, self.came, after)
        self.came = bit_swap(self.kept, step_bits(kind, 2 * SPLITS - 2 - step))
        return self.kept


def shards(
    history,
    depth_weights,
    gain_attn,
    gain_mlp,
    qkv_weight,
    out_weight,
    up_weight,
    down_weight,
    cotangent,
):
    width = cotangent.shape[1]
    local = out_weight.shape[0]
    hidden = down_weight.shape[0]
    pairs = local // PAIR
    chunks = hidden // CHUNK
    at = where_am_i()

    cot_other = mp_swap(cotangent)
    mixed, first = mix(depth_weights, history, gain_attn)
    first_other = mp_swap(first)
    qkv, att, lse, out_own, out_other = attend(at, first, first_other, qkv_weight, out_weight)
    middle, second = renorm(at, mixed, out_own, mp_swap(out_other), gain_mlp)
    second_other = mp_swap(second)
    early = 2 * chunks // 3
    kept_a, sent_a, kept_b, sent_b, hidden_rows, grad_pre = mlp(
        at, (slot_of(0, 0), slot_of(1, 0)), second, second_other, cotangent, cot_other,
        up_weight, down_weight,
    )
    mlp_a = Stream(at, 0, kept_a, sent_a)
    mlp_b = Stream(at, 1, kept_b, sent_b)
    grad_own, grad_other = rows_times(at, "second_back", grad_pre, up_weight, True)
    block_own, block_other = rows_times(
        at, "block", hidden_rows, down_weight, False, after=[grad_own]
    )
    grad_middle, narrow, gain_grad_mlp = norm_back_rows(
        at, grad_own, mp_swap(grad_other), middle, cotangent, gain_mlp, after=[block_own]
    )
    narrow_other = mp_swap(narrow)
    early_pairs = 2 * pairs // 3
    back_args = (qkv, att, lse, narrow, narrow_other, out_weight, first, first_other)
    kept, sent, early_rows = attend_back(at, slot_of(0, 0), 0, early_pairs, *back_args)
    att_a = Stream(at, 0, kept, sent)
    last = early_rows
    for stream in (mlp_a, mlp_b):
        last = stream.advance([last])
    kept, sent, late_rows = attend_back(
        at, slot_of(1, 0), early_pairs, pairs - early_pairs, *back_args, after=[last]
    )
    att_b = Stream(at, 1, kept, sent)
    first_own_grad, first_other_grad = first_back(at, qkv_weight, [early_rows, late_rows])
    first_came = mp_swap(first_other_grad)
    last = first_own_grad
    for stream in (mlp_b, mlp_a, att_a, att_b):
        last = stream.advance([last])
    grad_history, gain_grad_attn, depth_terms = unmix(
        depth_weights, history, gain_attn, mixed, grad_middle, first_own_grad, first_came,
        after=[last],
    )
    last = depth_terms
    block_out = (
        middle + block_own + mp_swap(block_other).astype(jnp.float32)
    ).astype(jnp.bfloat16)
    small = jnp.concatenate(
        [gain_grad_attn[0], gain_grad_mlp[0], jnp.sum(depth_terms, axis=1)]
    )
    small = small + mp_swap(small)
    for bit in range(dp_bits()):
        small = small + bit_swap(small, [bit, bit])
    gain_grad_attn, gain_grad_mlp, grad_depth = jnp.split(small, [width, 2 * width])

    streams = [mlp_b, mlp_a, att_b, att_a]
    while any(stream.step < 2 * SPLITS - 1 for stream in streams):
        for stream in streams:
            if stream.step < 2 * SPLITS - 1:
                last = stream.advance([last])
    grads = finish_mlp(
        at, slot_of(1, 0), early, mlp_b.kept, mlp_b.came, width, hidden, after=[last]
    )
    grad_up, grad_down = finish_mlp(
        at, slot_of(0, 0), 0, mlp_a.kept, mlp_a.came, width, hidden, grads
    )
    grads = finish_attend(
        at, slot_of(1, 0), early_pairs, att_b.kept, att_b.came, width, local, after=[grad_up]
    )
    grad_qkv, grad_out = finish_attend(
        at, slot_of(0, 0), 0, att_a.kept, att_a.came, width, local, grads
    )
    return (
        block_out,
        grad_history,
        grad_depth,
        gain_grad_attn,
        gain_grad_mlp,
        grad_qkv,
        grad_out,
        grad_up,
        grad_down,
    )


def solution(mesh):
    in_specs = (
        P(None, ("dp", "mp"), None),
        P(),
        P(),
        P(),
        P(None, None, "mp"),
        P("mp", None),
        P(None, "mp"),
        P("mp", None),
        P(("dp", "mp"), None),
    )
    out_specs = (
        P(("dp", "mp"), None),
        P(None, ("dp", "mp"), None),
        P(),
        P(),
        P(),
        P(None, None, "mp"),
        P("mp", None),
        P(None, "mp"),
        P("mp", None),
    )
    return jax.shard_map(shards, mesh=mesh, in_specs=in_specs, out_specs=out_specs, check_vma=False)
```

```python
import functools

import jax
import jax.numpy as jnp
from jax import lax
from jax.experimental import pallas as pl
from jax.experimental.pallas import tpu as pltpu
from jax.sharding import PartitionSpec as P

HEAD_DIM = 64
EPSILON = 1e-05
SQRT_HALF = 0.7071067811865476
INV_ROOT_TWO_PI = 0.3989422804014327
LOG2E = 1.4426950408889634
NEG = -1e30
TILE = 256
ROW_BLOCK = 64
VMEM_BYTES = 32 * 2**20
SPLITS = 4
PAIR = 2 * HEAD_DIM
CHUNK = 512
ORDER = (
    "nb", "ab0", "ab1", "Mb", "ab2", "fb", "Ma", "Aa", "Mb", "um", "Ab", "Mb", "Ma", "Ab",
    "Aa", "Ma", "Mb", "sm", "Ab", "Aa", "blk", "sm", "Ab", "Ma", "Aa", "sm", "Mb", "Ab", "Ab",
    "Ma", "sm", "Aa", "Ma", "Ab", "Aa", "Mb", "Ma", "sm", "bo", "Mb", "fAb", "Aa", "fMa",
    "fAa", "fMb",
)
KINDS = (
    ((0, 1, 2, 3), (2, 0, 1, 3)),
    ((1, 0, 2, 3), (2, 1, 0, 3)),
    ((0, 1, 2, 3), (1, 0, 2, 3)),
    ((2, 0, 1, 3), (2, 1, 0, 3)),
)
KIND = {"Ma": 0, "Mb": 1, "Aa": 2, "Ab": 3}
EARLY = 3

PLAIN = (((1,), (0,)), ((), ()))
CONTRACT_COLS = (((1,), (1,)), ((), ()))
CONTRACT_ROWS = (((0,), (0,)), ((), ()))


def dot(lhs, rhs, dims=PLAIN):
    return lax.dot_general(lhs, rhs, dims, preferred_element_type=jnp.float32)


def cost(flops, moved, exps=0):
    return pl.CostEstimate(flops=flops, bytes_accessed=moved, transcendentals=exps)


def params():
    return pltpu.CompilerParams(vmem_limit_bytes=VMEM_BYTES)


def normalize(inputs):
    row_mean = jnp.mean(inputs, axis=-1, keepdims=True)
    centered = inputs - row_mean
    variance = jnp.mean(centered * centered, axis=-1, keepdims=True)
    inv_scale = lax.rsqrt(variance + EPSILON)
    return centered * inv_scale, inv_scale


def norm_back(grad_rows, gain_row, normed, inv_scale):
    scaled = grad_rows * gain_row
    first_mean = jnp.mean(scaled, axis=-1, keepdims=True)
    second_mean = jnp.mean(scaled * normed, axis=-1, keepdims=True)
    return inv_scale * (scaled - first_mean - normed * second_mean)


def gelu_value(inputs):
    return 0.5 * inputs * (1.0 + lax.erf(inputs * SQRT_HALF))


def gelu_slope(inputs):
    normal_cdf = 0.5 * (1.0 + lax.erf(inputs * SQRT_HALF))
    return normal_cdf + inputs * jnp.exp(-0.5 * inputs * inputs) * INV_ROOT_TWO_PI


def layer_copies(history_ref, held_ref, sems, out=False):
    copies = []
    for index in range(held_ref.shape[0]):
        rows = pl.ds(index * ROW_BLOCK, ROW_BLOCK)
        ends = (history_ref.at[:, rows, :], held_ref.at[index])
        copies.append(
            pltpu.make_async_copy(ends[out], ends[not out], sems.at[index])
        )
    return copies


def mix_kernel(weights_ref, gain_ref, history_ref, mixed_ref, first_ref, held_ref, sems):
    copies = layer_copies(history_ref, held_ref, sems)
    for copy in copies:
        copy.start()
    for index, copy in enumerate(copies):
        rows = pl.ds(index * ROW_BLOCK, ROW_BLOCK)
        copy.wait()
        mixed = weights_ref[0] * held_ref[index, 0].astype(jnp.float32)
        for layer in range(1, held_ref.shape[1]):
            mixed = mixed + weights_ref[layer] * held_ref[index, layer].astype(jnp.float32)
        mixed_ref[rows, :] = mixed
        normed, _ = normalize(mixed)
        first_ref[rows, :] = (normed * gain_ref[...]).astype(jnp.bfloat16)


def mix(weights, history, gain):
    layers, rows, width = history.shape
    in_vmem = pl.BlockSpec(memory_space=pltpu.VMEM)
    blocks = rows // ROW_BLOCK
    return pl.pallas_call(
        mix_kernel,
        in_specs=[
            pl.BlockSpec(memory_space=pltpu.SMEM),
            in_vmem,
            pl.BlockSpec(memory_space=pltpu.HBM),
        ],
        out_specs=[in_vmem, in_vmem],
        out_shape=[
            jax.ShapeDtypeStruct((rows, width), jnp.float32),
            jax.ShapeDtypeStruct((rows, width), jnp.bfloat16),
        ],
        scratch_shapes=[
            pltpu.VMEM((blocks, layers, ROW_BLOCK, width), jnp.bfloat16),
            pltpu.SemaphoreType.DMA((blocks,)),
        ],
        compiler_params=params(),
        cost_estimate=cost(1000, 1000),
        name="mix",
    )(weights, gain[None], history)


def unmix_kernel(
    weights_ref, gain_ref, mixed_ref, middle_ref, own_ref, other_ref, gain_mlp_ref, history_ref,
    *refs,
):
    grads_ref, small_ref, held_ref, given_ref, in_sems, out_sems = refs[-6:]
    copies = layer_copies(history_ref, held_ref, in_sems)
    gives = layer_copies(grads_ref, given_ref, out_sems, True)
    for copy in copies:
        copy.start()
    layers = held_ref.shape[1]
    small_ref[...] = jnp.zeros_like(small_ref)
    small_ref[1:2] = gain_mlp_ref[...]
    for index, (copy, give) in enumerate(zip(copies, gives)):
        rows = pl.ds(index * ROW_BLOCK, ROW_BLOCK)
        grad_first = own_ref[rows, :] + other_ref[rows, :].astype(jnp.float32)
        normed, inv_scale = normalize(mixed_ref[rows, :])
        grad_mixed = middle_ref[rows, :] + norm_back(
            grad_first, gain_ref[...], normed, inv_scale
        )
        small_ref[0:1] += jnp.sum(grad_first * normed, axis=0, keepdims=True)
        copy.wait()
        for layer in range(layers):
            given_ref[index, layer] = (weights_ref[layer] * grad_mixed).astype(jnp.bfloat16)
            product = held_ref[index, layer].astype(jnp.float32) * grad_mixed
            small_ref[8 + layer : 9 + layer] += jnp.sum(product, axis=0, keepdims=True)
        give.start()
    for give in gives:
        give.wait()


def unmix(weights, history, gain, mixed, grad_middle, own, other, gain_grad_mlp, after=()):
    layers, rows, width = history.shape
    in_vmem = pl.BlockSpec(memory_space=pltpu.VMEM)
    in_hbm = pl.BlockSpec(memory_space=pltpu.HBM)
    blocks = rows // ROW_BLOCK
    held = pltpu.VMEM((blocks, layers, ROW_BLOCK, width), jnp.bfloat16)
    return pl.pallas_call(
        unmix_kernel,
        in_specs=[pl.BlockSpec(memory_space=pltpu.SMEM)]
        + [in_vmem] * 6
        + [in_hbm]
        + [pl.BlockSpec(memory_space=pl.ANY)] * len(after),
        out_specs=[in_hbm, in_vmem],
        out_shape=[
            jax.ShapeDtypeStruct(history.shape, jnp.bfloat16),
            jax.ShapeDtypeStruct((8 + layers, width), jnp.float32),
        ],
        scratch_shapes=[
            held,
            held,
            pltpu.SemaphoreType.DMA((blocks,)),
            pltpu.SemaphoreType.DMA((blocks,)),
        ],
        compiler_params=params(),
        cost_estimate=cost(1000, 1000),
        name="unmix",
    )(weights, gain[None], mixed, grad_middle, own, other, gain_grad_mlp, history, *after)


def head_mask(head):
    lanes = lax.broadcasted_iota(jnp.int32, (1, PAIR), 1)
    return (lanes // HEAD_DIM) == head


def future_mask():
    keys = lax.broadcasted_iota(jnp.int32, (TILE, TILE), 0)
    asks = lax.broadcasted_iota(jnp.int32, (TILE, TILE), 1)
    return keys > asks


def local_call(kernel, name, at, arrays, outs, after=(), scratch=(), aliases=None):
    in_vmem = pl.BlockSpec(memory_space=pltpu.VMEM)
    return pl.pallas_call(
        kernel,
        in_specs=[pl.BlockSpec(memory_space=pltpu.SMEM)]
        + [in_vmem] * len(arrays)
        + [pl.BlockSpec(memory_space=pl.ANY)] * len(after),
        out_specs=[in_vmem] * len(outs),
        out_shape=[jax.ShapeDtypeStruct(shape, dtype) for shape, dtype in outs],
        scratch_shapes=list(scratch),
        input_output_aliases=aliases or {},
        compiler_params=params(),
        cost_estimate=cost(1000, 1000),
        name=name,
    )(at, *arrays, *after)


def attend_kernel(
    at_ref, own_ref, other_ref, weight_ref, out_weight_ref,
    qkv_ref, att_ref, lse_ref, out_own_ref, out_other_ref,
):
    rows = own_ref.shape[0]
    tiles = rows // TILE
    first = at_ref[0]
    scale = HEAD_DIM ** (-0.5) * LOG2E
    places = (first, 1 - first)
    later = future_mask()

    def one_pair(pair, carry):
        lanes = pl.ds(pl.multiple_of(pair * PAIR, PAIR), PAIR)
        weight = jnp.concatenate([weight_ref[c, :, lanes] for c in range(3)], axis=1)
        for side, ref in enumerate((own_ref, other_ref)):
            made = dot(ref[...], weight).astype(jnp.bfloat16)
            for c in range(3):
                qkv_ref[c, side, :, lanes] = made[:, c * PAIR : (c + 1) * PAIR]
        half_keys = [qkv_ref[1, places[half], :, lanes] for half in range(2)]
        half_values = [qkv_ref[2, places[half], :, lanes].T for half in range(2)]
        for half in range(2):
            for tile in range(tiles):
                at_rows = pl.ds(tile * TILE, TILE)
                queries = qkv_ref[0, places[half], at_rows, lanes]
                outs = []
                for head in range(2):
                    asked = jnp.where(head_mask(head), queries, jnp.zeros_like(queries))
                    spans = []
                    if half == 1:
                        spans.append((0, 0, rows))
                    if tile > 0:
                        spans.append((half, 0, tile * TILE))
                    spans.append((half, tile * TILE, TILE))
                    scores = [
                        dot(half_keys[where][start : start + size], asked, CONTRACT_COLS)
                        for where, start, size in spans
                    ]
                    scores[-1] = jnp.where(later, NEG, scores[-1])
                    top = functools.reduce(
                        jnp.maximum, [jnp.max(part, axis=0, keepdims=True) for part in scores]
                    )
                    top = top * scale
                    total = 0.0
                    summed = 0.0
                    mine = slice(head * HEAD_DIM, (head + 1) * HEAD_DIM)
                    for part, (where, start, size) in zip(scores, spans):
                        weights = jnp.exp2(part * scale - top)
                        total = total + jnp.sum(weights, axis=0, keepdims=True)
                        summed = summed + dot(
                            half_values[where][mine, start : start + size],
                            weights.astype(jnp.bfloat16),
                        )
                    outs.append(summed / total)
                    lse_ref[pair, head, half, :, at_rows] = top + jnp.log2(total)
                joined = jnp.concatenate(outs, axis=0).T
                att_ref[places[half], at_rows, lanes] = joined.astype(jnp.bfloat16)
        return carry

    lax.fori_loop(0, att_ref.shape[2] // PAIR, one_pair, 0)
    out_other_ref[...] = dot(att_ref[1], out_weight_ref[...]).astype(jnp.bfloat16)
    out_own_ref[...] = dot(att_ref[0], out_weight_ref[...])


def attend(at, own, other, weight, out_weight):
    rows, width = own.shape
    local = weight.shape[2]
    return local_call(
        attend_kernel,
        "attend",
        at,
        [own, other, weight, out_weight],
        [
            ((3, 2, rows, local), jnp.bfloat16),
            ((2, rows, local), jnp.bfloat16),
            ((local // PAIR, 2, 2, 1, rows), jnp.float32),
            ((rows, width), jnp.float32),
            ((rows, width), jnp.bfloat16),
        ],
    )


def renorm_kernel(at_ref, mixed_ref, own_ref, other_ref, gain_ref, middle_ref, second_ref):
    middle = mixed_ref[...] + own_ref[...] + other_ref[...].astype(jnp.float32)
    middle_ref[...] = middle
    second_ref[...] = (normalize(middle)[0] * gain_ref[...]).astype(jnp.bfloat16)


def renorm(at, mixed, own, other, gain):
    return local_call(
        renorm_kernel,
        "renorm",
        at,
        [mixed, own, other, gain[None]],
        [(mixed.shape, jnp.float32), (mixed.shape, jnp.bfloat16)],
    )


def split_halves(bit, rows, top, bottom, keep_ref, send_ref):
    shape = (keep_ref.shape[0], -1, keep_ref.shape[2])
    top = top.astype(jnp.bfloat16).reshape(shape)
    bottom = bottom.astype(jnp.bfloat16).reshape(shape)
    keep_ref[:, rows, :] = jnp.where(bit == 0, top, bottom)
    send_ref[:, rows, :] = jnp.where(bit == 0, bottom, top)


def mlp_kernel(
    slots, at_ref, second_own_ref, second_other_ref, cot_own_ref, cot_other_ref, up_ref, down_ref,
    *refs,
):
    (
        keep_a_ref, send_a_ref, keep_b_ref, send_b_ref, hidden_ref, own_ref, other_ref, grad_pre_ref
    ) = refs[-8:]
    bf16 = jnp.bfloat16
    chunks = hidden_ref.shape[2] // CHUNK
    sides = ((second_own_ref, cot_own_ref), (second_other_ref, cot_other_ref))
    unit = TILE // keep_a_ref.shape[0]
    early = keep_a_ref.shape[1] // unit

    def make(chunk):
        lanes = pl.ds(chunk * CHUNK, CHUNK)
        for side, (second_ref, cot_ref) in enumerate(sides):
            pre = dot(second_ref[...], up_ref[:, lanes])
            cdf = 0.5 * (1.0 + lax.erf(pre * SQRT_HALF))
            hidden_ref[side, :, lanes] = (pre * cdf).astype(bf16)
            slope = cdf + pre * jnp.exp(-0.5 * pre * pre) * INV_ROOT_TWO_PI
            grad_hidden = dot(cot_ref[...], down_ref[lanes, :], CONTRACT_COLS)
            grad_pre_ref[side, :, lanes] = (grad_hidden * slope).astype(bf16)

    def give(chunk):
        lanes = pl.ds(chunk * CHUNK, CHUNK)
        grad_up, grad_down = 0.0, 0.0
        for side, (second_ref, cot_ref) in enumerate(sides):
            grad_up = grad_up + dot(grad_pre_ref[side, :, lanes], second_ref[...], CONTRACT_ROWS)
            grad_down = grad_down + dot(hidden_ref[side, :, lanes], cot_ref[...], CONTRACT_ROWS)
        for part in range(CHUNK // TILE):
            tile = chunk * (CHUNK // TILE) + part
            late = tile >= early
            refs = (keep_b_ref, send_b_ref) if late else (keep_a_ref, send_a_ref)
            place = pl.ds((tile - early if late else tile) * unit, unit)
            rows = slice(part * TILE, (part + 1) * TILE)
            split_halves(at_ref[slots[late]], place, grad_up[rows], grad_down[rows], *refs)

    make(0)
    for chunk in range(1, chunks):
        make(chunk)
        give(chunk - 1)
    give(chunks - 1)
    other_ref[...] = dot(grad_pre_ref[1], up_ref[...], CONTRACT_COLS).astype(bf16)
    own_ref[...] = dot(grad_pre_ref[0], up_ref[...], CONTRACT_COLS)


def mlp(at, slots, second_own, second_other, cot_own, cot_other, up, down, after=()):
    rows, width = second_own.shape
    hidden = down.shape[0]
    blocks = 2 ** (SPLITS - 1)
    tiles = hidden // TILE
    unit = TILE // blocks
    pieces = [
        ((blocks, count * unit, width), jnp.bfloat16) for count in (EARLY, tiles - EARLY)
    ]
    return local_call(
        functools.partial(mlp_kernel, slots),
        "mlp",
        at,
        [second_own, second_other, cot_own, cot_other, up, down],
        [pieces[0], pieces[0], pieces[1], pieces[1]]
        + [
            ((2, rows, hidden), jnp.bfloat16),
            ((rows, width), jnp.float32),
            ((rows, width), jnp.bfloat16),
        ],
        after,
        [pltpu.VMEM((2, rows, hidden), jnp.bfloat16)],
    )


def rows_kernel(at_ref, rows_ref, weight_ref, *refs):
    own_ref, other_ref = refs[-2:]
    other_ref[...] = dot(rows_ref[1], weight_ref[...]).astype(jnp.bfloat16)
    own_ref[...] = dot(rows_ref[0], weight_ref[...])


def rows_times(at, rows, weight, after=()):
    shape = (rows.shape[1], weight.shape[1])
    return local_call(
        rows_kernel, "block", at, [rows, weight], [(shape, jnp.float32), (shape, jnp.bfloat16)],
        after,
    )


def block_kernel(at_ref, middle_ref, own_ref, other_ref, *refs):
    total = middle_ref[...] + own_ref[...] + other_ref[...].astype(jnp.float32)
    refs[-1][...] = total.astype(jnp.bfloat16)


def block_sum(at, middle, own, other, after=()):
    outs = [(middle.shape, jnp.bfloat16)]
    return local_call(block_kernel, "block_sum", at, [middle, own, other], outs, after)[0]


def small_kernel(at_ref, mine_ref, came_ref, *refs):
    refs[-1][...] = mine_ref[...] + came_ref[...]


def small_sum(at, mine, came, after=()):
    outs = [(mine.shape, jnp.float32)]
    return local_call(small_kernel, "small", at, [mine, came], outs, after)[0]


def norm_back_kernel(at_ref, own_ref, other_ref, middle_ref, cot_ref, gain_ref, *refs):
    grad_ref, narrow_ref, gain_grad_ref = refs[-3:]
    grad_second = own_ref[...] + other_ref[...].astype(jnp.float32)
    normed, inv_scale = normalize(middle_ref[...])
    grad = cot_ref[...].astype(jnp.float32) + norm_back(
        grad_second, gain_ref[...], normed, inv_scale
    )
    grad_ref[...] = grad
    narrow_ref[...] = grad.astype(jnp.bfloat16)
    gain_grad_ref[...] = jnp.sum(grad_second * normed, axis=0, keepdims=True)


def norm_back_rows(at, own, other, middle, cotangent, gain, after=()):
    shape = own.shape
    return local_call(
        norm_back_kernel,
        "norm_back_rows",
        at,
        [own, other, middle, cotangent, gain[None]],
        [(shape, jnp.float32), (shape, jnp.bfloat16), ((1, shape[1]), jnp.float32)],
        after,
    )


def attend_back_kernel(
    slot, pair, place, at_ref, qkv_ref, att_ref, lse_ref, grad_own_ref, grad_other_ref, out_weight_ref,
    first_own_ref, first_other_ref, *refs,
):
    keep_ref, send_ref, grad_rows_ref = refs[-3:]
    rows = grad_own_ref.shape[0]
    tiles = rows // TILE
    first = at_ref[0]
    plain = HEAD_DIM ** (-0.5)
    scale = plain * LOG2E
    places = (first, 1 - first)
    later = future_mask()
    bf16 = jnp.bfloat16
    sides = (grad_own_ref, grad_other_ref)
    firsts = (first_own_ref, first_other_ref)
    masked = [head_mask(head) for head in range(2)]
    unit = 4 * PAIR // (2 * keep_ref.shape[0])
    is_own = [places[half] == 0 for half in range(2)]
    chunks = [(half, tile) for half in range(2) for tile in range(tiles)]

    def only(head, part):
        return jnp.where(masked[head], part, jnp.zeros_like(part))

    def plus(old, term):
        return term if old is None else old + term

    lanes = pl.ds(pair * PAIR, PAIR)
    outer = [
        dot(ref[...], out_weight_ref[lanes, :], CONTRACT_COLS).astype(bf16) for ref in sides
    ]
    grads = [jnp.where(is_own[half], outer[0], outer[1]) for half in range(2)]
    queries, keys, values = [
        [qkv_ref[c, places[half], :, lanes] for half in range(2)] for c in range(3)
    ]
    keys_t = [part.T for part in keys]
    deltas = []
    for half in range(2):
        attended = att_ref[places[half], :, lanes].astype(jnp.float32)
        product = (grads[half].astype(jnp.float32) * attended).T
        deltas.append([
            jnp.sum(product[head * HEAD_DIM : (head + 1) * HEAD_DIM], axis=0, keepdims=True)
            for head in range(2)
        ])
    key_grads = [None for _ in chunks]
    value_grads = [None for _ in chunks]
    query_grads = []
    for ask, (ask_half, ask_tile) in enumerate(chunks):
        ask_rows = slice(ask_tile * TILE, (ask_tile + 1) * TILE)
        sums_here = []
        for head in range(2):
            asked = only(head, queries[ask_half][ask_rows])
            grad = only(head, grads[ask_half][ask_rows])
            lse = lse_ref[pair, head, ask_half, :, ask_rows]
            delta = deltas[ask_half][head][:, ask_rows]
            query_grad = None
            for key in range(ask + 1):
                key_half, key_tile = chunks[key]
                key_rows = slice(key_tile * TILE, (key_tile + 1) * TILE)
                scores = dot(keys[key_half][key_rows], asked, CONTRACT_COLS)
                probs = jnp.exp2(scores * scale - lse)
                if key == ask:
                    probs = jnp.where(later, 0.0, probs)
                grad_probs = dot(values[key_half][key_rows], grad, CONTRACT_COLS)
                grad_scores = (probs * (grad_probs - delta)).astype(bf16)
                value_grads[key] = plus(value_grads[key], dot(probs.astype(bf16), grad))
                key_grads[key] = plus(key_grads[key], dot(grad_scores, asked))
                mine = slice(head * HEAD_DIM, (head + 1) * HEAD_DIM)
                query_grad = plus(
                    query_grad, dot(keys_t[key_half][mine, key_rows], grad_scores)
                )
            sums_here.append(query_grad)
        query_grads.append((jnp.concatenate(sums_here, axis=0) * plain).astype(bf16))
    turned = []
    for half in range(2):
        at_half = [i for i, (where, _) in enumerate(chunks) if where == half]
        query_t = jnp.concatenate([query_grads[i] for i in at_half], axis=1)
        key = jnp.concatenate([(key_grads[i] * plain).astype(bf16) for i in at_half], axis=0)
        value = jnp.concatenate([value_grads[i].astype(bf16) for i in at_half], axis=0)
        turned.append([query_t, key.T, value.T, att_ref[places[half], :, lanes].T])
        for c, part in enumerate((query_t.T, key, value)):
            grad_rows_ref[c, places[half]] = part
    top, bottom = 0.0, 0.0
    for side in range(2):
        mine = [jnp.where(is_own[side], a, b) for a, b in zip(turned[0], turned[1])]
        rows_here = firsts[side][...]
        top = top + dot(jnp.concatenate(mine[:2], axis=0), rows_here)
        bottom = bottom + jnp.concatenate(
            [dot(mine[2], rows_here), dot(mine[3], sides[side][...])], axis=0
        )
    split_halves(
        at_ref[slot], pl.ds(place * unit, unit), top, bottom, keep_ref, send_ref
    )


def attend_back(at, slot, pair, place, count, qkv, att, lse, grad_own, grad_other, out_weight,
                first_own, first_other, old=(), after=()):
    rows, width = grad_own.shape
    blocks = 2 ** (SPLITS - 1)
    unit = 4 * PAIR // (2 * blocks)
    pieces = ((blocks, count * unit, width), jnp.bfloat16)
    arrays = [qkv, att, lse, grad_own, grad_other, out_weight, first_own, first_other, *old]
    return local_call(
        functools.partial(attend_back_kernel, slot, pair, place),
        "attend_back",
        at,
        arrays,
        [pieces, pieces, ((3, 2, rows, PAIR), jnp.bfloat16)],
        after,
        aliases={len(arrays) - 1: 0, len(arrays): 1} if old else {},
    )


def first_back_kernel(count, at_ref, weight_ref, *refs):
    own_ref, other_ref = refs[-2:]
    groups = []
    start = 0
    for ref in refs[:count]:
        groups.append((ref, start))
        start += ref.shape[3]
    for side, out_ref in ((1, other_ref), (0, own_ref)):
        total = 0.0
        for ref, begin in groups:
            for c in range(3):
                lanes = slice(begin, begin + ref.shape[3])
                total = total + dot(ref[c, side], weight_ref[c, :, lanes], CONTRACT_COLS)
        out_ref[...] = total.astype(out_ref.dtype)


def first_back(at, weight, groups, after=()):
    shape = (groups[0].shape[2], weight.shape[1])
    return local_call(
        functools.partial(first_back_kernel, len(groups)), "first_back", at, [weight, *groups],
        [(shape, jnp.float32), (shape, jnp.bfloat16)], after,
    )


def fold_kernel(slot, at_ref, kept_ref, came_ref, *refs):
    keep_ref, send_ref = refs[-2:]
    half = keep_ref.shape[0]
    bit = at_ref[slot]
    for target, start in ((send_ref, (1 - bit) * half), (keep_ref, bit * half)):
        for index in range(half):
            total = kept_ref[start + index].astype(jnp.float32) + came_ref[
                start + index
            ].astype(jnp.float32)
            target[index] = total.astype(jnp.bfloat16)


def add_kernel(at_ref, kept_ref, came_ref, *refs):
    total = kept_ref[...].astype(jnp.float32) + came_ref[...].astype(jnp.float32)
    refs[-1][...] = total.astype(jnp.bfloat16)


def join_kernel(slot, at_ref, mine_ref, came_ref, *refs):
    both_ref = refs[-1]
    half = mine_ref.shape[0]
    bit = at_ref[slot]
    for source, start in ((mine_ref, bit * half), (came_ref, (1 - bit) * half)):
        for index in range(half):
            both_ref[start + index] = source[index]


def fold(at, slot, kept, came, after=()):
    blocks, rows, width = kept.shape
    if blocks == 1:
        outs = [(kept.shape, jnp.bfloat16)]
        return local_call(add_kernel, "add", at, [kept, came], outs, after)[0]
    outs = [((blocks // 2, rows, width), jnp.bfloat16)] * 2
    return local_call(
        functools.partial(fold_kernel, slot), "fold", at, [kept, came], outs, after
    )


def join(at, slot, mine, came, after=()):
    blocks, rows, width = mine.shape
    outs = [((2 * blocks, rows, width), jnp.bfloat16)]
    return local_call(
        functools.partial(join_kernel, slot), "join", at, [mine, came], outs, after
    )[0]


def in_order(bit, mine, came):
    rows = mine.shape[0] * mine.shape[1]
    mine = mine.reshape(rows, -1).astype(jnp.float32)
    came = came.reshape(rows, -1).astype(jnp.float32)
    return jnp.where(bit == 0, mine, came), jnp.where(bit == 0, came, mine)


def finish_mlp_kernel(slot, at_ref, mine_ref, came_ref, *refs):
    up_ref, down_ref, token_ref = refs[-3:]
    token_ref[...] = jnp.zeros_like(token_ref)
    top, bottom = in_order(at_ref[slot], mine_ref[...], came_ref[...])
    up_ref[...] = top.T
    down_ref[...] = bottom


def finish_mlp(at, slot, start, mine, came, width, hidden, old=None, after=()):
    blocks, rows, _ = mine.shape
    unit = TILE // blocks
    part = pl.BlockSpec((blocks, unit, TILE), lambda i, j, at: (0, i, j))
    return pl.pallas_call(
        functools.partial(finish_mlp_kernel, slot),
        grid_spec=pltpu.PrefetchScalarGridSpec(
            num_scalar_prefetch=1,
            grid=(rows // unit, width // TILE),
            in_specs=[part, part]
            + [pl.BlockSpec(memory_space=pl.ANY)] * (len(old or []) + len(after)),
            out_specs=[
                pl.BlockSpec((TILE, TILE), lambda i, j, at: (j, start + i)),
                pl.BlockSpec((TILE, TILE), lambda i, j, at: (start + i, j)),
                pl.BlockSpec((8, 128), lambda i, j, at: (0, 0)),
            ],
        ),
        out_shape=[
            jax.ShapeDtypeStruct((width, hidden), jnp.float32),
            jax.ShapeDtypeStruct((hidden, width), jnp.float32),
            jax.ShapeDtypeStruct((8, 128), jnp.float32),
        ],
        input_output_aliases={3: 0, 4: 1} if old else {},
        compiler_params=params(),
        cost_estimate=cost(1000, 1000),
        name="finish_mlp",
    )(at, mine, came, *(old or []), *after)


def finish_attend_kernel(slot, at_ref, mine_ref, came_ref, *refs):
    qkv_ref, out_ref, token_ref = refs[-3:]
    token_ref[...] = jnp.zeros_like(token_ref)
    top, bottom = in_order(at_ref[slot], mine_ref[...], came_ref[...])
    qkv_ref[0] = top[:PAIR].T
    qkv_ref[1] = top[PAIR:].T
    qkv_ref[2] = bottom[:PAIR].T
    out_ref[...] = bottom[PAIR:]


def finish_attend(at, slot, start, mine, came, width, local, old=None, after=()):
    blocks, rows, _ = mine.shape
    unit = 2 * PAIR // blocks
    part = pl.BlockSpec((blocks, unit, TILE), lambda i, j, at: (0, i, j))
    return pl.pallas_call(
        functools.partial(finish_attend_kernel, slot),
        grid_spec=pltpu.PrefetchScalarGridSpec(
            num_scalar_prefetch=1,
            grid=(rows // unit, width // TILE),
            in_specs=[part, part]
            + [pl.BlockSpec(memory_space=pl.ANY)] * (len(old or []) + len(after)),
            out_specs=[
                pl.BlockSpec((3, TILE, PAIR), lambda i, j, at: (0, j, start + i)),
                pl.BlockSpec((PAIR, TILE), lambda i, j, at: (start + i, j)),
                pl.BlockSpec((8, 128), lambda i, j, at: (0, 0)),
            ],
        ),
        out_shape=[
            jax.ShapeDtypeStruct((3, width, local), jnp.float32),
            jax.ShapeDtypeStruct((local, width), jnp.float32),
            jax.ShapeDtypeStruct((8, 128), jnp.float32),
        ],
        input_output_aliases={3: 0, 4: 1} if old else {},
        compiler_params=params(),
        cost_estimate=cost(1000, 1000),
        name="finish_attend",
    )(at, mine, came, *(old or []), *after)


def mp_swap(rows):
    return lax.ppermute(rows, "mp", [(0, 1), (1, 0)])


def dp_bits():
    return lax.axis_size("dp").bit_length() - 1


def bit_swap(rows, bits):
    size, cores = lax.axis_size("dp"), lax.axis_size("mp")
    pairs = [
        (i * cores + core, (i ^ (1 << bits[core])) * cores + core)
        for i in range(size)
        for core in range(cores)
    ]
    return lax.ppermute(rows, ("dp", "mp"), pairs)


def step_bits(kind, step):
    return [order[step] for order in KINDS[kind]]


def slot_of(kind, step):
    return 1 + kind * SPLITS + step


def where_am_i():
    core, index = lax.axis_index("mp"), lax.axis_index("dp")
    values = [core]
    for kind in range(len(KINDS)):
        for step in range(SPLITS):
            bits = step_bits(kind, step)
            values.append((index >> jnp.where(core == 0, bits[0], bits[1])) & 1)
    return jnp.stack(values).astype(jnp.int32)


class Stream:
    def __init__(self, at, kind, kept, sent):
        self.at, self.kind, self.kept, self.step = at, kind, kept, 0
        self.came = bit_swap(sent, step_bits(kind, 0))

    def advance(self, after=()):
        step, kind = self.step, self.kind
        self.step += 1
        if step < SPLITS - 1:
            self.kept, sent = fold(
                self.at, slot_of(kind, step + 1), self.kept, self.came, after
            )
            self.came = bit_swap(sent, step_bits(kind, step + 1))
            return self.kept
        if step == SPLITS - 1:
            self.kept = fold(self.at, 0, self.kept, self.came, after)
            for bit in range(SPLITS, dp_bits()):
                other = bit_swap(self.kept, [bit, bit])
                self.kept = fold(self.at, 0, self.kept, other)
        else:
            bit_step = 2 * SPLITS - 1 - step
            self.kept = join(self.at, slot_of(kind, bit_step), self.kept, self.came, after)
        self.came = bit_swap(self.kept, step_bits(kind, 2 * SPLITS - 2 - step))
        return self.kept


def shards(
    history,
    depth_weights,
    gain_attn,
    gain_mlp,
    qkv_weight,
    out_weight,
    up_weight,
    down_weight,
    cotangent,
):
    width = cotangent.shape[1]
    local = out_weight.shape[0]
    hidden = down_weight.shape[0]
    pairs = local // PAIR
    at = where_am_i()

    cot_other = mp_swap(cotangent)
    mixed, first = mix(depth_weights, history, gain_attn)
    first_other = mp_swap(first)
    qkv, att, lse, out_own, out_other = attend(at, first, first_other, qkv_weight, out_weight)
    middle, second = renorm(at, mixed, out_own, mp_swap(out_other), gain_mlp)
    second_other = mp_swap(second)
    kept_a, sent_a, kept_b, sent_b, hidden_rows, grad_own, grad_other = mlp(
        at, (slot_of(KIND["Ma"], 0), slot_of(KIND["Mb"], 0)), second, second_other, cotangent, cot_other,
        up_weight, down_weight,
    )
    streams = {
        "Ma": Stream(at, KIND["Ma"], kept_a, sent_a),
        "Mb": Stream(at, KIND["Mb"], kept_b, sent_b),
    }
    grad_came = mp_swap(grad_other)
    made = {}

    def back_norm(after):
        made["middle"], made["narrow"], made["gain"] = norm_back_rows(
            at, grad_own, grad_came, middle, cotangent, gain_mlp, after
        )
        made["narrow_came"] = mp_swap(made["narrow"])
        return made["gain"]

    def back_pair(pair, after):
        late = pair == pairs - 1
        name, place = ("Ab", 0) if late else ("Aa", pair)
        old = () if late or pair == 0 else made["stack"]
        kept, sent, made[pair] = attend_back(
            at, slot_of(KIND[name], 0), pair, place, 1 if late else pairs - 1, qkv, att, lse,
            made["narrow"], made["narrow_came"], out_weight, first, first_other, old, after,
        )
        made["stack"] = (kept, sent)
        if pair >= pairs - 2:
            streams[name] = Stream(at, KIND[name], kept, sent)
        return made[pair]

    def back_first(after):
        groups = [made[pair] for pair in range(pairs)]
        made["own"], other = first_back(at, qkv_weight, groups, after)
        made["came"] = mp_swap(other)
        return made["own"]

    def back_start(after):
        made["history"], made["small"] = unmix(
            depth_weights, history, gain_attn, mixed, made["middle"], made["own"], made["came"],
            made["gain"], after,
        )
        made["small_came"] = mp_swap(made["small"])
        return made["small"]

    def small_step(bit, after):
        made["small"] = small_sum(at, made["small"], made["small_came"], after)
        if bit < dp_bits():
            made["small_came"] = bit_swap(made["small"], [bit, bit])
        return made["small"]

    def block_rows(after):
        made["block"], other = rows_times(at, hidden_rows, down_weight, after)
        made["block_came"] = mp_swap(other)
        return made["block"]

    def block_end(after):
        made["out"] = block_sum(at, middle, made["block"], made["block_came"], after)
        return made["out"]

    def end_mlp(name, start, after):
        stream = streams[name]
        *made["mlp"], token = finish_mlp(
            at, slot_of(KIND[name], 0), start, stream.kept, stream.came, width, hidden,
            made.get("mlp"), after,
        )
        return token

    def end_attend(name, start, after):
        stream = streams[name]
        *made["attend"], token = finish_attend(
            at, slot_of(KIND[name], 0), start, stream.kept, stream.came, width, local,
            made.get("attend"), after,
        )
        return token

    units = {
        "nb": back_norm,
        "fb": back_first,
        "um": back_start,
        "blk": block_rows,
        "bo": block_end,
        "fMa": functools.partial(end_mlp, "Ma", 0),
        "fMb": functools.partial(end_mlp, "Mb", EARLY),
        "fAa": functools.partial(end_attend, "Aa", 0),
        "fAb": functools.partial(end_attend, "Ab", pairs - 1),
    }
    for pair in range(pairs):
        units["ab" + str(pair)] = functools.partial(back_pair, pair)
    bits = 0
    last = hidden_rows
    for name in ORDER:
        if name in streams:
            last = streams[name].advance([last])
        elif name == "sm":
            last = small_step(bits, [last])
            bits += 1
        else:
            last = units[name]([last])
    for bit in range(bits, dp_bits() + 1):
        last = small_step(bit, [last])
    small = made["small"]
    grad_depth = jnp.sum(small[8:], axis=1)
    block_out, grad_history = made["out"], made["history"]
    gain_grad_attn, gain_grad_mlp = small[0], small[1]
    (grad_up, grad_down), (grad_qkv, grad_out) = made["mlp"], made["attend"]
    return (
        block_out,
        grad_history,
        grad_depth,
        gain_grad_attn,
        gain_grad_mlp,
        grad_qkv,
        grad_out,
        grad_up,
        grad_down,
    )


def solution(mesh):
    in_specs = (
        P(None, ("dp", "mp"), None),
        P(),
        P(),
        P(),
        P(None, None, "mp"),
        P("mp", None),
        P(None, "mp"),
        P("mp", None),
        P(("dp", "mp"), None),
    )
    out_specs = (
        P(("dp", "mp"), None),
        P(None, ("dp", "mp"), None),
        P(),
        P(),
        P(),
        P(None, None, "mp"),
        P("mp", None),
        P(None, "mp"),
        P("mp", None),
    )
    return jax.shard_map(shards, mesh=mesh, in_specs=in_specs, out_specs=out_specs, check_vma=False)
```

```python
import functools

import jax
import jax.numpy as jnp
from jax import lax
from jax.experimental import pallas as pl
from jax.experimental.pallas import tpu as pltpu
from jax.sharding import PartitionSpec as P

HEAD_DIM = 64
EPSILON = 1e-05
SQRT_HALF = 0.7071067811865476
INV_ROOT_TWO_PI = 0.3989422804014327
LOG2E = 1.4426950408889634
NEG = -1e30
TILE = 256
ROW_BLOCK = 64
MIX_BLOCK = 128
SMALL_ROWS = 32
SPLITS = 3
PAIR = 2 * HEAD_DIM
CHUNK = 512
ORDER = (
    "nb", "ab0", "ab1", "Mb", "ab2", "fb", "Ma", "Aa", "blk", "Mb", "Ma", "Mb", "Ma", "Aa",
    "Ab", "um", "Mb", "Aa", "Ab", "Ab", "Ma", "Aa", "Mb", "Ma", "Aa", "Ab", "Ab", "Mb", "Ab",
    "Aa", "Ma", "fMb", "fAb", "fAa", "fMa",
)
KINDS = (
    ((2, 0, 1), (1, 2, 0)),
    ((2, 0, 1), (0, 1, 2)),
    ((0, 1, 2), (1, 2, 0)),
    ((0, 1, 2), (2, 0, 1)),
)
KIND = {"Ma": 0, "Mb": 1, "Aa": 2, "Ab": 3}
EARLY = 3

PLAIN = (((1,), (0,)), ((), ()))
CONTRACT_COLS = (((1,), (1,)), ((), ()))
CONTRACT_ROWS = (((0,), (0,)), ((), ()))


def dot(lhs, rhs, dims=PLAIN):
    return lax.dot_general(lhs, rhs, dims, preferred_element_type=jnp.float32)


def cost(flops, moved, exps=0):
    return pl.CostEstimate(flops=flops, bytes_accessed=moved, transcendentals=exps)


def params(mebibytes=8):
    return pltpu.CompilerParams(vmem_limit_bytes=mebibytes * 2**20)


def normalize(inputs):
    row_mean = jnp.mean(inputs, axis=-1, keepdims=True)
    centered = inputs - row_mean
    variance = jnp.mean(centered * centered, axis=-1, keepdims=True)
    inv_scale = lax.rsqrt(variance + EPSILON)
    return centered * inv_scale, inv_scale


def norm_back(grad_rows, gain_row, normed, inv_scale):
    scaled = grad_rows * gain_row
    first_mean = jnp.mean(scaled, axis=-1, keepdims=True)
    second_mean = jnp.mean(scaled * normed, axis=-1, keepdims=True)
    return inv_scale * (scaled - first_mean - normed * second_mean)


def gelu_value(inputs):
    return 0.5 * inputs * (1.0 + lax.erf(inputs * SQRT_HALF))


def gelu_slope(inputs):
    normal_cdf = 0.5 * (1.0 + lax.erf(inputs * SQRT_HALF))
    return normal_cdf + inputs * jnp.exp(-0.5 * inputs * inputs) * INV_ROOT_TWO_PI


def layer_copies(history_ref, held_ref, sems, out=False):
    copies = []
    for index in range(held_ref.shape[0]):
        rows = pl.ds(index * ROW_BLOCK, ROW_BLOCK)
        ends = (history_ref.at[:, rows, :], held_ref.at[index])
        copies.append(
            pltpu.make_async_copy(ends[out], ends[not out], sems.at[index])
        )
    return copies


def mix_kernel(weights_ref, gain_ref, history_ref, mixed_ref, first_ref):
    mixed = weights_ref[0] * history_ref[0].astype(jnp.float32)
    for layer in range(1, history_ref.shape[0]):
        mixed = mixed + weights_ref[layer] * history_ref[layer].astype(jnp.float32)
    mixed_ref[...] = mixed
    normed, _ = normalize(mixed)
    first_ref[...] = (normed * gain_ref[...]).astype(jnp.bfloat16)


def mix(weights, history, gain):
    layers, rows, width = history.shape
    row_spec = pl.BlockSpec((MIX_BLOCK, width), lambda i: (i, 0))
    return pl.pallas_call(
        mix_kernel,
        grid=(rows // MIX_BLOCK,),
        in_specs=[
            pl.BlockSpec(memory_space=pltpu.SMEM),
            pl.BlockSpec((1, width), lambda i: (0, 0)),
            pl.BlockSpec((layers, MIX_BLOCK, width), lambda i: (0, i, 0)),
        ],
        out_specs=[row_spec, row_spec],
        out_shape=[
            jax.ShapeDtypeStruct((rows, width), jnp.float32),
            jax.ShapeDtypeStruct((rows, width), jnp.bfloat16),
        ],
        compiler_params=params(57),
        cost_estimate=cost(1000, 1000),
        name="mix",
    )(weights, gain[None], history)


def unmix_kernel(
    weights_ref, gain_ref, mixed_ref, middle_ref, own_ref, other_ref, gain_mlp_ref,
    rows_ref, block_own_ref, block_other_ref, history_ref, *refs,
):
    (
        grads_ref, out_ref, small_ref, held_ref, given_ref, made_ref, in_sems, out_sems, made_sem
    ) = refs[-9:]
    copies = layer_copies(history_ref, held_ref, in_sems)
    gives = layer_copies(grads_ref, given_ref, out_sems, True)
    for copy in copies:
        copy.start()
    block = rows_ref[...] + block_own_ref[...] + block_other_ref[...].astype(jnp.float32)
    made_ref[...] = block.astype(jnp.bfloat16)
    make = pltpu.make_async_copy(made_ref, out_ref, made_sem)
    make.start()
    layers = held_ref.shape[1]
    small_ref[...] = jnp.zeros_like(small_ref)
    small_ref[1:2] = gain_mlp_ref[...]
    for index, (copy, give) in enumerate(zip(copies, gives)):
        rows = pl.ds(index * ROW_BLOCK, ROW_BLOCK)
        grad_first = own_ref[rows, :] + other_ref[rows, :].astype(jnp.float32)
        normed, inv_scale = normalize(mixed_ref[rows, :])
        grad_mixed = middle_ref[rows, :] + norm_back(
            grad_first, gain_ref[...], normed, inv_scale
        )
        small_ref[0:1] += jnp.sum(grad_first * normed, axis=0, keepdims=True)
        copy.wait()
        for layer in range(layers):
            given_ref[index, layer] = (weights_ref[layer] * grad_mixed).astype(jnp.bfloat16)
            product = held_ref[index, layer].astype(jnp.float32) * grad_mixed
            small_ref[8 + layer : 9 + layer] += jnp.sum(product, axis=0, keepdims=True)
        give.start()
    make.wait()
    for give in gives:
        give.wait()


def unmix(weights, history, gain, mixed, grad_middle, own, other, gain_grad_mlp, block, after=()):
    layers, rows, width = history.shape
    in_vmem = pl.BlockSpec(memory_space=pltpu.VMEM)
    in_hbm = pl.BlockSpec(memory_space=pltpu.HBM)
    blocks = rows // ROW_BLOCK
    held = pltpu.VMEM((blocks, layers, ROW_BLOCK, width), jnp.bfloat16)
    return pl.pallas_call(
        unmix_kernel,
        in_specs=[pl.BlockSpec(memory_space=pltpu.SMEM)]
        + [in_vmem] * 9
        + [in_hbm]
        + [pl.BlockSpec(memory_space=pl.ANY)] * len(after),
        out_specs=[in_hbm, in_hbm, in_vmem],
        out_shape=[
            jax.ShapeDtypeStruct(history.shape, jnp.bfloat16),
            jax.ShapeDtypeStruct((rows, width), jnp.bfloat16),
            jax.ShapeDtypeStruct((SMALL_ROWS, width), jnp.float32),
        ],
        scratch_shapes=[
            held,
            held,
            pltpu.VMEM((rows, width), jnp.bfloat16),
            pltpu.SemaphoreType.DMA((blocks,)),
            pltpu.SemaphoreType.DMA((blocks,)),
            pltpu.SemaphoreType.DMA,
        ],
        compiler_params=params(15),
        cost_estimate=cost(1000, 1000),
        name="unmix",
    )(weights, gain[None], mixed, grad_middle, own, other, gain_grad_mlp, *block, history, *after)


def head_mask(head):
    lanes = lax.broadcasted_iota(jnp.int32, (1, PAIR), 1)
    return (lanes // HEAD_DIM) == head


def future_mask():
    keys = lax.broadcasted_iota(jnp.int32, (TILE, TILE), 0)
    asks = lax.broadcasted_iota(jnp.int32, (TILE, TILE), 1)
    return keys > asks


def stacked_heads(rows):
    zero = jnp.zeros_like(rows)
    return jnp.concatenate([jnp.where(head_mask(head), rows, zero) for head in range(2)], axis=0)


def own_heads(columns):
    half = columns.shape[1] // 2
    return jnp.concatenate([columns[:HEAD_DIM, :half], columns[HEAD_DIM:, half:]], axis=0)


def local_call(kernel, name, at, arrays, outs, after=(), scratch=(), aliases=None,
               mebibytes=8):
    in_vmem = pl.BlockSpec(memory_space=pltpu.VMEM)
    return pl.pallas_call(
        kernel,
        in_specs=[pl.BlockSpec(memory_space=pltpu.SMEM)]
        + [in_vmem] * len(arrays)
        + [pl.BlockSpec(memory_space=pl.ANY)] * len(after),
        out_specs=[in_vmem] * len(outs),
        out_shape=[jax.ShapeDtypeStruct(shape, dtype) for shape, dtype in outs],
        scratch_shapes=list(scratch),
        input_output_aliases=aliases or {},
        compiler_params=params(mebibytes),
        cost_estimate=cost(1000, 1000),
        name=name,
    )(at, *arrays, *after)


def attend_kernel(
    at_ref, own_ref, other_ref, weight_ref, out_weight_ref,
    qkv_ref, att_ref, lse_ref, out_own_ref, out_other_ref,
):
    rows = own_ref.shape[0]
    tiles = rows // TILE
    first = at_ref[0]
    scale = HEAD_DIM ** (-0.5) * LOG2E
    places = (first, 1 - first)
    later = jnp.concatenate([future_mask()] * 2, axis=1)

    def one_pair(pair, carry):
        lanes = pl.ds(pl.multiple_of(pair * PAIR, PAIR), PAIR)
        weight = jnp.concatenate([weight_ref[c, :, lanes] for c in range(3)], axis=1)
        for side, ref in enumerate((own_ref, other_ref)):
            made = dot(ref[...], weight).astype(jnp.bfloat16)
            for c in range(3):
                qkv_ref[c, side, :, lanes] = made[:, c * PAIR : (c + 1) * PAIR]
        half_keys = [qkv_ref[1, places[half], :, lanes] for half in range(2)]
        half_values = [qkv_ref[2, places[half], :, lanes].T for half in range(2)]
        for half in range(2):
            for tile in range(tiles):
                at_rows = pl.ds(tile * TILE, TILE)
                queries = qkv_ref[0, places[half], at_rows, lanes]
                asked = stacked_heads(queries)
                spans = []
                if half == 1:
                    spans.append((0, 0, rows))
                if tile > 0:
                    spans.append((half, 0, tile * TILE))
                spans.append((half, tile * TILE, TILE))
                scores = [
                    dot(half_keys[where][start : start + size], asked, CONTRACT_COLS)
                    for where, start, size in spans
                ]
                scores[-1] = jnp.where(later, NEG, scores[-1])
                top = functools.reduce(
                    jnp.maximum, [jnp.max(part, axis=0, keepdims=True) for part in scores]
                )
                top = top * scale
                total = 0.0
                summed = 0.0
                for part, (where, start, size) in zip(scores, spans):
                    weights = jnp.exp2(part * scale - top)
                    total = total + jnp.sum(weights, axis=0, keepdims=True)
                    summed = summed + dot(
                        half_values[where][:, start : start + size], weights.astype(jnp.bfloat16)
                    )
                lse = top + jnp.log2(total)
                for head in range(2):
                    lse_ref[pair, head, half, :, at_rows] = lse[:, head * TILE : (head + 1) * TILE]
                joined = own_heads(summed / total).T
                att_ref[places[half], at_rows, lanes] = joined.astype(jnp.bfloat16)
        return carry

    lax.fori_loop(0, att_ref.shape[2] // PAIR, one_pair, 0)
    out_other_ref[...] = dot(att_ref[1], out_weight_ref[...]).astype(jnp.bfloat16)
    out_own_ref[...] = dot(att_ref[0], out_weight_ref[...])


def attend(at, own, other, weight, out_weight):
    rows, width = own.shape
    local = weight.shape[2]
    return local_call(
        attend_kernel,
        "attend",
        at,
        [own, other, weight, out_weight],
        [
            ((3, 2, rows, local), jnp.bfloat16),
            ((2, rows, local), jnp.bfloat16),
            ((local // PAIR, 2, 2, 1, rows), jnp.float32),
            ((rows, width), jnp.float32),
            ((rows, width), jnp.bfloat16),
        ],
        mebibytes=12,
    )


def renorm_kernel(at_ref, mixed_ref, own_ref, other_ref, gain_ref, middle_ref, second_ref):
    middle = mixed_ref[...] + own_ref[...] + other_ref[...].astype(jnp.float32)
    middle_ref[...] = middle
    second_ref[...] = (normalize(middle)[0] * gain_ref[...]).astype(jnp.bfloat16)


def renorm(at, mixed, own, other, gain):
    return local_call(
        renorm_kernel,
        "renorm",
        at,
        [mixed, own, other, gain[None]],
        [(mixed.shape, jnp.float32), (mixed.shape, jnp.bfloat16)],
    )


def split_halves(bit, rows, top, bottom, keep_ref, send_ref):
    shape = (keep_ref.shape[0], -1, keep_ref.shape[2])
    top = top.astype(jnp.bfloat16).reshape(shape)
    bottom = bottom.astype(jnp.bfloat16).reshape(shape)
    keep_ref[:, rows, :] = jnp.where(bit == 0, top, bottom)
    send_ref[:, rows, :] = jnp.where(bit == 0, bottom, top)


def mlp_kernel(
    slots, at_ref, second_own_ref, second_other_ref, cot_own_ref, cot_other_ref, up_ref, down_ref,
    *refs,
):
    (
        keep_a_ref, send_a_ref, keep_b_ref, send_b_ref, hidden_ref, own_ref, other_ref, grad_pre_ref
    ) = refs[-8:]
    bf16 = jnp.bfloat16
    chunks = hidden_ref.shape[2] // CHUNK
    sides = ((second_own_ref, cot_own_ref), (second_other_ref, cot_other_ref))
    unit = TILE // keep_a_ref.shape[0]
    early = keep_a_ref.shape[1] // unit

    def make(chunk):
        lanes = pl.ds(chunk * CHUNK, CHUNK)
        for side, (second_ref, cot_ref) in enumerate(sides):
            pre = dot(second_ref[...], up_ref[:, lanes])
            cdf = 0.5 * (1.0 + lax.erf(pre * SQRT_HALF))
            hidden_ref[side, :, lanes] = (pre * cdf).astype(bf16)
            slope = cdf + pre * jnp.exp(-0.5 * pre * pre) * INV_ROOT_TWO_PI
            grad_hidden = dot(cot_ref[...], down_ref[lanes, :], CONTRACT_COLS)
            grad_pre_ref[side, :, lanes] = (grad_hidden * slope).astype(bf16)

    def give(chunk):
        lanes = pl.ds(chunk * CHUNK, CHUNK)
        grad_up, grad_down = 0.0, 0.0
        for side, (second_ref, cot_ref) in enumerate(sides):
            grad_up = grad_up + dot(grad_pre_ref[side, :, lanes], second_ref[...], CONTRACT_ROWS)
            grad_down = grad_down + dot(hidden_ref[side, :, lanes], cot_ref[...], CONTRACT_ROWS)
        for part in range(CHUNK // TILE):
            tile = chunk * (CHUNK // TILE) + part
            late = tile >= early
            refs = (keep_b_ref, send_b_ref) if late else (keep_a_ref, send_a_ref)
            place = pl.ds((tile - early if late else tile) * unit, unit)
            rows = slice(part * TILE, (part + 1) * TILE)
            split_halves(at_ref[slots[late]], place, grad_up[rows], grad_down[rows], *refs)

    make(0)
    for chunk in range(1, chunks):
        make(chunk)
        give(chunk - 1)
    give(chunks - 1)
    other_ref[...] = dot(grad_pre_ref[1], up_ref[...], CONTRACT_COLS).astype(bf16)
    own_ref[...] = dot(grad_pre_ref[0], up_ref[...], CONTRACT_COLS)


def mlp(at, slots, second_own, second_other, cot_own, cot_other, up, down, after=()):
    rows, width = second_own.shape
    hidden = down.shape[0]
    blocks = 2 ** (SPLITS - 1)
    tiles = hidden // TILE
    unit = TILE // blocks
    pieces = [
        ((blocks, count * unit, width), jnp.bfloat16) for count in (EARLY, tiles - EARLY)
    ]
    return local_call(
        functools.partial(mlp_kernel, slots),
        "mlp",
        at,
        [second_own, second_other, cot_own, cot_other, up, down],
        [pieces[0], pieces[0], pieces[1], pieces[1]]
        + [
            ((2, rows, hidden), jnp.bfloat16),
            ((rows, width), jnp.float32),
            ((rows, width), jnp.bfloat16),
        ],
        after,
        [pltpu.VMEM((2, rows, hidden), jnp.bfloat16)],
    )


def rows_kernel(at_ref, rows_ref, weight_ref, *refs):
    own_ref, other_ref = refs[-2:]
    other_ref[...] = dot(rows_ref[1], weight_ref[...]).astype(jnp.bfloat16)
    own_ref[...] = dot(rows_ref[0], weight_ref[...])


def rows_times(at, rows, weight, after=()):
    shape = (rows.shape[1], weight.shape[1])
    return local_call(
        rows_kernel, "block", at, [rows, weight], [(shape, jnp.float32), (shape, jnp.bfloat16)],
        after,
    )


def norm_back_kernel(at_ref, own_ref, other_ref, middle_ref, cot_ref, gain_ref, *refs):
    grad_ref, narrow_ref, gain_grad_ref = refs[-3:]
    grad_second = own_ref[...] + other_ref[...].astype(jnp.float32)
    normed, inv_scale = normalize(middle_ref[...])
    grad = cot_ref[...].astype(jnp.float32) + norm_back(
        grad_second, gain_ref[...], normed, inv_scale
    )
    grad_ref[...] = grad
    narrow_ref[...] = grad.astype(jnp.bfloat16)
    gain_grad_ref[...] = jnp.sum(grad_second * normed, axis=0, keepdims=True)


def norm_back_rows(at, own, other, middle, cotangent, gain, after=()):
    shape = own.shape
    return local_call(
        norm_back_kernel,
        "norm_back_rows",
        at,
        [own, other, middle, cotangent, gain[None]],
        [(shape, jnp.float32), (shape, jnp.bfloat16), ((1, shape[1]), jnp.float32)],
        after,
    )


def attend_back_kernel(
    slot, pair, place, at_ref, qkv_ref, att_ref, lse_ref, grad_own_ref, grad_other_ref,
    out_weight_ref, first_own_ref, first_other_ref, *refs,
):
    keep_ref, send_ref, grad_rows_ref = refs[-3:]
    rows = grad_own_ref.shape[0]
    tiles = rows // TILE
    first = at_ref[0]
    plain = HEAD_DIM ** (-0.5)
    scale = plain * LOG2E
    places = (first, 1 - first)
    later = jnp.concatenate([future_mask()] * 2, axis=1)
    bf16 = jnp.bfloat16
    sides = (grad_own_ref, grad_other_ref)
    firsts = (first_own_ref, first_other_ref)
    unit = 4 * PAIR // (2 * keep_ref.shape[0])
    is_own = [places[half] == 0 for half in range(2)]
    chunks = [(half, tile) for half in range(2) for tile in range(tiles)]

    def plus(old, term):
        return term if old is None else old + term

    lanes = pl.ds(pair * PAIR, PAIR)
    outer = [
        dot(ref[...], out_weight_ref[lanes, :], CONTRACT_COLS).astype(bf16) for ref in sides
    ]
    grads = [jnp.where(is_own[half], outer[0], outer[1]) for half in range(2)]
    queries, keys, values = [
        [qkv_ref[c, places[half], :, lanes] for half in range(2)] for c in range(3)
    ]
    keys_t = [part.T for part in keys]
    deltas = []
    for half in range(2):
        attended = att_ref[places[half], :, lanes].astype(jnp.float32)
        product = (grads[half].astype(jnp.float32) * attended).T
        deltas.append([
            jnp.sum(product[head * HEAD_DIM : (head + 1) * HEAD_DIM], axis=0, keepdims=True)
            for head in range(2)
        ])
    key_grads = {}
    value_grads = {}
    query_grads = []
    for half, tile in chunks:
        here = slice(tile * TILE, (tile + 1) * TILE)
        asked = stacked_heads(queries[half][here])
        grad = stacked_heads(grads[half][here])
        lse = jnp.concatenate([lse_ref[pair, head, half, :, here] for head in range(2)], axis=1)
        delta = jnp.concatenate([deltas[half][head][:, here] for head in range(2)], axis=1)
        spans = []
        if half == 1:
            spans.append((0, 0, rows))
        if tile > 0:
            spans.append((half, 0, tile * TILE))
        spans.append((half, tile * TILE, TILE))
        query_grad = None
        for where, start, size in spans:
            span = slice(start, start + size)
            scores = dot(keys[where][span], asked, CONTRACT_COLS)
            probs = jnp.exp2(scores * scale - lse)
            if (where, start) == (half, tile * TILE):
                probs = jnp.where(later, 0.0, probs)
            grad_probs = dot(values[where][span], grad, CONTRACT_COLS)
            grad_scores = (probs * (grad_probs - delta)).astype(bf16)
            value_term = dot(probs.astype(bf16), grad)
            key_term = dot(grad_scores, asked)
            query_grad = plus(query_grad, dot(keys_t[where][:, span], grad_scores))
            for part in range(size // TILE):
                at_part = (where, start // TILE + part)
                cut = slice(part * TILE, (part + 1) * TILE)
                value_grads[at_part] = plus(value_grads.get(at_part), value_term[cut])
                key_grads[at_part] = plus(key_grads.get(at_part), key_term[cut])
        query_grads.append((own_heads(query_grad) * plain).astype(bf16))
    turned = []
    for half in range(2):
        at_half = [i for i, (where, _) in enumerate(chunks) if where == half]
        query_t = jnp.concatenate([query_grads[i] for i in at_half], axis=1)
        key = jnp.concatenate(
            [(key_grads[half, tile] * plain).astype(bf16) for tile in range(tiles)], axis=0
        )
        value = jnp.concatenate(
            [value_grads[half, tile].astype(bf16) for tile in range(tiles)], axis=0
        )
        turned.append([query_t, key.T, value.T, att_ref[places[half], :, lanes].T])
        for c, part in enumerate((query_t.T, key, value)):
            grad_rows_ref[c, places[half]] = part
    top, bottom = 0.0, 0.0
    for side in range(2):
        mine = [jnp.where(is_own[side], a, b) for a, b in zip(turned[0], turned[1])]
        rows_here = firsts[side][...]
        top = top + dot(jnp.concatenate(mine[:2], axis=0), rows_here)
        bottom = bottom + jnp.concatenate(
            [dot(mine[2], rows_here), dot(mine[3], sides[side][...])], axis=0
        )
    split_halves(at_ref[slot], pl.ds(place * unit, unit), top, bottom, keep_ref, send_ref)


def attend_back(at, slot, pair, place, count, qkv, att, lse, grad_own, grad_other, out_weight,
                first_own, first_other, old=(), after=()):
    rows, width = grad_own.shape
    blocks = 2 ** (SPLITS - 1)
    unit = 4 * PAIR // (2 * blocks)
    pieces = ((blocks, count * unit, width), jnp.bfloat16)
    arrays = [qkv, att, lse, grad_own, grad_other, out_weight, first_own, first_other, *old]
    return local_call(
        functools.partial(attend_back_kernel, slot, pair, place),
        "attend_back",
        at,
        arrays,
        [pieces, pieces, ((3, 2, rows, PAIR), jnp.bfloat16)],
        after,
        aliases={len(arrays) - 1: 0, len(arrays): 1} if old else {},
        mebibytes=12,
    )


def first_back_kernel(count, at_ref, weight_ref, *refs):
    own_ref, other_ref = refs[-2:]
    pieces = []
    for index, ref in enumerate(refs[:count]):
        lanes = slice(index * PAIR, (index + 1) * PAIR)
        pieces += [(ref, c, lanes) for c in range(3)]
    weight = jnp.concatenate([weight_ref[c, :, lanes] for _, c, lanes in pieces], axis=1)
    for side, out_ref in ((1, other_ref), (0, own_ref)):
        rows = jnp.concatenate([ref[c, side] for ref, c, _ in pieces], axis=1)
        out_ref[...] = dot(rows, weight, CONTRACT_COLS).astype(out_ref.dtype)


def first_back(at, weight, groups, after=()):
    shape = (groups[0].shape[2], weight.shape[1])
    return local_call(
        functools.partial(first_back_kernel, len(groups)), "first_back", at, [weight, *groups],
        [(shape, jnp.float32), (shape, jnp.bfloat16)], after,
    )


def fold_kernel(slot, at_ref, kept_ref, came_ref, *refs):
    keep_ref, send_ref = refs[-2:]
    half = keep_ref.shape[0]
    bit = at_ref[slot]
    for target, start in ((send_ref, (1 - bit) * half), (keep_ref, bit * half)):
        for index in range(half):
            total = kept_ref[start + index].astype(jnp.float32) + came_ref[
                start + index
            ].astype(jnp.float32)
            target[index] = total.astype(jnp.bfloat16)


def add_kernel(at_ref, kept_ref, came_ref, *refs):
    total = kept_ref[...].astype(jnp.float32) + came_ref[...].astype(jnp.float32)
    refs[-1][...] = total.astype(jnp.bfloat16)


def widen(pair):
    half = pair.shape[0] // 2
    pair = pair.astype(jnp.float32)
    return pair[:half] + pair[half:]


def narrow(value):
    high = value.astype(jnp.bfloat16)
    low = (value - high.astype(jnp.float32)).astype(jnp.bfloat16)
    return jnp.concatenate([high, low], axis=0)


def add_small_kernel(at_ref, kept_ref, came_ref, mine_ref, other_ref, *refs):
    total = kept_ref[0].astype(jnp.float32) + came_ref[0].astype(jnp.float32)
    refs[-1][0] = total.astype(jnp.bfloat16)
    refs[-1][1] = narrow(mine_ref[...] + other_ref[...])


def again_kernel(at_ref, mine_ref, came_ref, *refs):
    total = mine_ref[0].astype(jnp.float32) + came_ref[0].astype(jnp.float32)
    refs[-1][0] = total.astype(jnp.bfloat16)
    if mine_ref.shape[0] > 1:
        refs[-1][1] = narrow(widen(mine_ref[1]) + widen(came_ref[1]))


def join_kernel(slot, at_ref, mine_ref, came_ref, *refs):
    both_ref = refs[-1]
    half = both_ref.shape[0] // 2
    bit = at_ref[slot]
    for source, start in ((mine_ref, bit * half), (came_ref, (1 - bit) * half)):
        for index in range(half):
            both_ref[start + index] = source[index]
    if both_ref.shape[0] > 2 * half:
        both_ref[2 * half] = narrow(widen(mine_ref[half]) + widen(came_ref[half]))


def fold(at, slot, kept, came, after=()):
    blocks, rows, width = kept.shape
    outs = [((blocks // 2, rows, width), jnp.bfloat16)] * 2
    return local_call(
        functools.partial(fold_kernel, slot), "fold", at, [kept, came], outs, after
    )


def last_fold(at, kept, came, small, after=()):
    blocks, rows, width = kept.shape
    kernel = add_small_kernel if small else add_kernel
    outs = [((blocks + (1 if small else 0), rows, width), jnp.bfloat16)]
    return local_call(kernel, "add", at, [kept, came, *small], outs, after)[0]


def again(at, mine, came, after=()):
    outs = [(mine.shape, jnp.bfloat16)]
    return local_call(again_kernel, "again", at, [mine, came], outs, after)[0]


def join(at, slot, mine, came, blocks, after=()):
    _, rows, width = mine.shape
    extra = mine.shape[0] - blocks
    outs = [((2 * blocks + extra, rows, width), jnp.bfloat16)]
    return local_call(
        functools.partial(join_kernel, slot), "join", at, [mine, came], outs, after
    )[0]


def ordered_units(bit, mine_ref, came_ref, blocks, unit):
    width = mine_ref.shape[2]
    for index in range(mine_ref.shape[1] // unit):
        rows = slice(index * unit, (index + 1) * unit)
        mine = mine_ref[:blocks, rows, :].reshape(blocks * unit, width)
        came = came_ref[:blocks, rows, :].reshape(blocks * unit, width)
        yield index, jnp.where(bit == 0, mine, came), jnp.where(bit == 0, came, mine)


def finish_mlp_kernel(slot, start, blocks, at_ref, mine_ref, came_ref, *refs):
    up_ref, down_ref, token_ref, turned_ref, held_ref, up_sems, down_sems = refs[-7:]
    token_ref[...] = jnp.zeros_like(token_ref)
    copies = []
    for index, top, bottom in ordered_units(
        at_ref[slot], mine_ref, came_ref, blocks, TILE // blocks
    ):
        place = pl.ds((start + index) * TILE, TILE)
        held_ref[index] = bottom.astype(jnp.float32)
        copies.append(
            pltpu.make_async_copy(held_ref.at[index], down_ref.at[place, :], down_sems.at[index])
        )
        copies[-1].start()
        turned_ref[index] = top.T.astype(jnp.float32)
        copies.append(
            pltpu.make_async_copy(turned_ref.at[index], up_ref.at[:, place], up_sems.at[index])
        )
        copies[-1].start()
    for copy in copies:
        copy.wait()


def finish_attend_kernel(slot, start, blocks, at_ref, mine_ref, came_ref, *refs):
    qkv_ref, out_ref, token_ref, turned_ref, held_ref, qkv_sems, out_sems = refs[-7:]
    token_ref[...] = jnp.zeros_like(token_ref)
    if mine_ref.shape[0] > blocks:
        token_ref[...] = widen(mine_ref[blocks]) + widen(came_ref[blocks])
    copies = []
    for index, top, bottom in ordered_units(
        at_ref[slot], mine_ref, came_ref, blocks, 2 * PAIR // blocks
    ):
        place = pl.ds((start + index) * PAIR, PAIR)
        held_ref[index] = bottom[PAIR:].astype(jnp.float32)
        copies.append(
            pltpu.make_async_copy(held_ref.at[index], out_ref.at[place, :], out_sems.at[index])
        )
        copies[-1].start()
        for c, part in enumerate((top[:PAIR], top[PAIR:], bottom[:PAIR])):
            turned_ref[index, c] = part.T.astype(jnp.float32)
        copies.append(
            pltpu.make_async_copy(
                turned_ref.at[index], qkv_ref.at[:, :, place], qkv_sems.at[index]
            )
        )
        copies[-1].start()
    for copy in copies:
        copy.wait()


def finish(kernel, name, at, slot, start, mine, came, shapes, scratch, old=None, after=()):
    in_vmem = pl.BlockSpec(memory_space=pltpu.VMEM)
    in_hbm = pl.BlockSpec(memory_space=pltpu.HBM)
    blocks = 2 ** (SPLITS - 1)
    units = mine.shape[1] * blocks // TILE
    return pl.pallas_call(
        functools.partial(kernel, slot, start, blocks),
        in_specs=[pl.BlockSpec(memory_space=pltpu.SMEM), in_vmem, in_vmem]
        + [in_hbm] * len(old or [])
        + [pl.BlockSpec(memory_space=pl.ANY)] * len(after),
        out_specs=[in_hbm, in_hbm, in_vmem],
        out_shape=[jax.ShapeDtypeStruct(shape, jnp.float32) for shape in shapes]
        + [jax.ShapeDtypeStruct((SMALL_ROWS, mine.shape[2]), jnp.float32)],
        scratch_shapes=[pltpu.VMEM((units, *shape), jnp.float32) for shape in scratch]
        + [pltpu.SemaphoreType.DMA((units,))] * 2,
        input_output_aliases={3: 0, 4: 1} if old else {},
        compiler_params=params(12),
        cost_estimate=cost(1000, 1000),
        name=name,
    )(at, mine, came, *(old or []), *after)


def finish_mlp(at, slot, start, mine, came, width, hidden, old=None, after=()):
    shapes = [(width, hidden), (hidden, width)]
    scratch = [(width, TILE), (TILE, width)]
    return finish(
        finish_mlp_kernel, "finish_mlp", at, slot, start, mine, came, shapes, scratch, old, after
    )


def finish_attend(at, slot, start, mine, came, width, local, old=None, after=()):
    shapes = [(3, width, local), (local, width)]
    scratch = [(3, width, PAIR), (PAIR, width)]
    return finish(
        finish_attend_kernel, "finish_attend", at, slot, start, mine, came, shapes, scratch, old,
        after,
    )


def mp_swap(rows):
    return lax.ppermute(rows, "mp", [(0, 1), (1, 0)])


def dp_bits():
    return lax.axis_size("dp").bit_length() - 1


def bit_swap(rows, bits):
    size, cores = lax.axis_size("dp"), lax.axis_size("mp")
    pairs = [
        (i * cores + core, (i ^ (1 << bits[core])) * cores + core)
        for i in range(size)
        for core in range(cores)
    ]
    return lax.ppermute(rows, ("dp", "mp"), pairs)


def step_bits(kind, step):
    return [order[step] for order in KINDS[kind]]


def slot_of(kind, step):
    return 1 + kind * SPLITS + step


def where_am_i():
    core, index = lax.axis_index("mp"), lax.axis_index("dp")
    values = [core]
    for kind in range(len(KINDS)):
        for step in range(SPLITS):
            bits = step_bits(kind, step)
            values.append((index >> jnp.where(core == 0, bits[0], bits[1])) & 1)
    return jnp.stack(values).astype(jnp.int32)


class Stream:
    def __init__(self, at, kind, kept, sent, small=None):
        self.at, self.kind, self.kept, self.step, self.small = at, kind, kept, 0, small
        self.extra = dp_bits() - SPLITS
        self.came = bit_swap(sent, step_bits(kind, 0))

    def advance(self, after=()):
        step, kind, at = self.step, self.kind, self.at
        self.step += 1
        joined = step - SPLITS - self.extra
        if step < SPLITS - 1:
            self.kept, sent = fold(at, slot_of(kind, step + 1), self.kept, self.came, after)
            self.came = bit_swap(sent, step_bits(kind, step + 1))
            return self.kept
        if step == SPLITS - 1:
            small = self.small() if self.small else ()
            self.kept = last_fold(at, self.kept, self.came, small, after)
        elif joined < 0:
            self.kept = again(at, self.kept, self.came, after)
        else:
            slot = slot_of(kind, SPLITS - 1 - joined)
            self.kept = join(at, slot, self.kept, self.came, 2**joined, after)
        if joined < -1:
            bit = SPLITS + joined + 1 + self.extra
            self.came = bit_swap(self.kept, [bit, bit])
        else:
            self.came = bit_swap(self.kept, step_bits(kind, SPLITS - 2 - joined))
        return self.kept


def shards(
    history,
    depth_weights,
    gain_attn,
    gain_mlp,
    qkv_weight,
    out_weight,
    up_weight,
    down_weight,
    cotangent,
):
    width = cotangent.shape[1]
    local = out_weight.shape[0]
    hidden = down_weight.shape[0]
    pairs = local // PAIR
    at = where_am_i()

    cot_other = mp_swap(cotangent)
    mixed, first = mix(depth_weights, history, gain_attn)
    first_other = mp_swap(first)
    qkv, att, lse, out_own, out_other = attend(at, first, first_other, qkv_weight, out_weight)
    middle, second = renorm(at, mixed, out_own, mp_swap(out_other), gain_mlp)
    second_other = mp_swap(second)
    kept_a, sent_a, kept_b, sent_b, hidden_rows, grad_own, grad_other = mlp(
        at, (slot_of(KIND["Ma"], 0), slot_of(KIND["Mb"], 0)), second, second_other, cotangent, cot_other,
        up_weight, down_weight,
    )
    streams = {
        "Ma": Stream(at, KIND["Ma"], kept_a, sent_a),
        "Mb": Stream(at, KIND["Mb"], kept_b, sent_b),
    }
    grad_came = mp_swap(grad_other)
    made = {}

    def back_norm(after):
        made["middle"], made["narrow"], made["gain"] = norm_back_rows(
            at, grad_own, grad_came, middle, cotangent, gain_mlp, after
        )
        made["narrow_came"] = mp_swap(made["narrow"])
        return made["gain"]

    def back_pair(pair, after):
        late = pair == pairs - 1
        name, place = ("Ab", 0) if late else ("Aa", pair)
        old = () if late or pair == 0 else made["stack"]
        kept, sent, made[pair] = attend_back(
            at, slot_of(KIND[name], 0), pair, place, 1 if late else pairs - 1, qkv, att, lse,
            made["narrow"], made["narrow_came"], out_weight, first, first_other, old, after,
        )
        made["stack"] = (kept, sent)
        if pair >= pairs - 2:
            small = (lambda: (made["small"], made["small_came"])) if late else None
            streams[name] = Stream(at, KIND[name], kept, sent, small)
        return made[pair]

    def back_first(after):
        groups = [made[pair] for pair in range(pairs)]
        made["own"], other = first_back(at, qkv_weight, groups, after)
        made["came"] = mp_swap(other)
        return made["own"]

    def back_start(after):
        block = (middle, made["block"], made["block_came"])
        made["history"], made["out"], made["small"] = unmix(
            depth_weights, history, gain_attn, mixed, made["middle"], made["own"], made["came"],
            made["gain"], block, after,
        )
        made["small_came"] = mp_swap(made["small"])
        return made["small"]

    def block_rows(after):
        made["block"], other = rows_times(at, hidden_rows, down_weight, after)
        made["block_came"] = mp_swap(other)
        return made["block"]

    def end_mlp(name, start, after):
        stream = streams[name]
        *made["mlp"], token = finish_mlp(
            at, slot_of(KIND[name], 0), start, stream.kept, stream.came, width, hidden,
            made.get("mlp"), after,
        )
        return token

    def end_attend(name, start, after):
        stream = streams[name]
        *made["attend"], made[name] = finish_attend(
            at, slot_of(KIND[name], 0), start, stream.kept, stream.came, width, local,
            made.get("attend"), after,
        )
        return made[name]

    units = {
        "nb": back_norm,
        "fb": back_first,
        "um": back_start,
        "blk": block_rows,
        "fMa": functools.partial(end_mlp, "Ma", 0),
        "fMb": functools.partial(end_mlp, "Mb", EARLY),
        "fAa": functools.partial(end_attend, "Aa", 0),
        "fAb": functools.partial(end_attend, "Ab", pairs - 1),
    }
    for pair in range(pairs):
        units["ab" + str(pair)] = functools.partial(back_pair, pair)
    last = hidden_rows
    for name in ORDER:
        if name in streams:
            if streams[name].step == SPLITS:
                for _ in range(streams[name].extra - 1):
                    last = streams[name].advance([last])
            last = streams[name].advance([last])
        else:
            last = units[name]([last])
    small = made["Ab"]
    grad_depth = jnp.sum(small[8 : 8 + history.shape[0]], axis=1)
    block_out, grad_history = made["out"], made["history"]
    gain_grad_attn, gain_grad_mlp = small[0], small[1]
    (grad_up, grad_down), (grad_qkv, grad_out) = made["mlp"], made["attend"]
    return (
        block_out,
        grad_history,
        grad_depth,
        gain_grad_attn,
        gain_grad_mlp,
        grad_qkv,
        grad_out,
        grad_up,
        grad_down,
    )


def solution(mesh):
    in_specs = (
        P(None, ("dp", "mp"), None),
        P(),
        P(),
        P(),
        P(None, None, "mp"),
        P("mp", None),
        P(None, "mp"),
        P("mp", None),
        P(("dp", "mp"), None),
    )
    out_specs = (
        P(("dp", "mp"), None),
        P(None, ("dp", "mp"), None),
        P(),
        P(),
        P(),
        P(None, None, "mp"),
        P("mp", None),
        P(None, "mp"),
        P("mp", None),
    )
    return jax.shard_map(shards, mesh=mesh, in_specs=in_specs, out_specs=out_specs, check_vma=False)
```

```python
import functools

import jax
import jax.numpy as jnp
from jax import lax
from jax.experimental import pallas as pl
from jax.experimental.pallas import tpu as pltpu
from jax.sharding import PartitionSpec as P

HEAD_DIM = 64
EPSILON = 1e-05
SQRT_HALF = 0.7071067811865476
INV_ROOT_TWO_PI = 0.3989422804014327
LOG2E = 1.4426950408889634
NEG = -1e30
TILE = 256
ROW_BLOCK = 64
HALF_ROWS = 256
MIX_BLOCK = 128
SMALL_ROWS = 32
SPLITS = 3
PAIR = 2 * HEAD_DIM
CHUNK = 512
ORDER = (
    "nb", "ab0", "ab1", "Mb", "Ma", "Mc", "ab2", "fb", "Mb", "Ma", "Aa", "Mb", "Mc", "Ma",
    "Ab", "Aa", "Mb", "Mc", "um", "Ma", "Aa", "Mb", "Ab", "Mc", "blk", "Ma", "Aa", "Ab", "Mc",
    "Mb", "Ma", "Mc", "Ab", "Aa", "um2", "Aa", "Ab", "fMb", "fMa", "Ab", "fMc", "fAa", "fAb",
)
KINDS = (
    ((0, 1, 2), (1, 2, 0)),
    ((0, 1, 2), (2, 0, 1)),
    ((2, 1, 0), (1, 0, 2)),
    ((0, 2, 1), (2, 1, 0)),
    ((0, 1, 2), (1, 0, 2)),
)
KIND = {"Ma": 0, "Mb": 1, "Mc": 2, "Aa": 3, "Ab": 4}
MLP_UNITS = (2, 2, 2)

PLAIN = (((1,), (0,)), ((), ()))
CONTRACT_COLS = (((1,), (1,)), ((), ()))
CONTRACT_ROWS = (((0,), (0,)), ((), ()))


def dot(lhs, rhs, dims=PLAIN):
    return lax.dot_general(lhs, rhs, dims, preferred_element_type=jnp.float32)


def cost(flops, moved, exps=0):
    return pl.CostEstimate(flops=flops, bytes_accessed=moved, transcendentals=exps)


def params(mebibytes=8):
    return pltpu.CompilerParams(vmem_limit_bytes=mebibytes * 2**20)


def normalize(inputs):
    row_mean = jnp.mean(inputs, axis=-1, keepdims=True)
    centered = inputs - row_mean
    variance = jnp.mean(centered * centered, axis=-1, keepdims=True)
    inv_scale = lax.rsqrt(variance + EPSILON)
    return centered * inv_scale, inv_scale


def norm_back(grad_rows, gain_row, normed, inv_scale):
    scaled = grad_rows * gain_row
    first_mean = jnp.mean(scaled, axis=-1, keepdims=True)
    second_mean = jnp.mean(scaled * normed, axis=-1, keepdims=True)
    return inv_scale * (scaled - first_mean - normed * second_mean)


def gelu_value(inputs):
    return 0.5 * inputs * (1.0 + lax.erf(inputs * SQRT_HALF))


def gelu_slope(inputs):
    normal_cdf = 0.5 * (1.0 + lax.erf(inputs * SQRT_HALF))
    return normal_cdf + inputs * jnp.exp(-0.5 * inputs * inputs) * INV_ROOT_TWO_PI


def layer_copies(history_ref, held_ref, sems, out=False):
    copies = []
    for index in range(held_ref.shape[0]):
        rows = pl.ds(index * ROW_BLOCK, ROW_BLOCK)
        ends = (history_ref.at[:, rows, :], held_ref.at[index])
        copies.append(
            pltpu.make_async_copy(ends[out], ends[not out], sems.at[index])
        )
    return copies


def mix_kernel(weights_ref, gain_ref, history_ref, mixed_ref, first_ref):
    mixed = weights_ref[0] * history_ref[0].astype(jnp.float32)
    for layer in range(1, history_ref.shape[0]):
        mixed = mixed + weights_ref[layer] * history_ref[layer].astype(jnp.float32)
    mixed_ref[...] = mixed
    normed, _ = normalize(mixed)
    first_ref[...] = (normed * gain_ref[...]).astype(jnp.bfloat16)


def mix(weights, history, gain):
    layers, rows, width = history.shape
    row_spec = pl.BlockSpec((MIX_BLOCK, width), lambda i: (i, 0))
    return pl.pallas_call(
        mix_kernel,
        grid=(rows // MIX_BLOCK,),
        in_specs=[
            pl.BlockSpec(memory_space=pltpu.SMEM),
            pl.BlockSpec((width,), lambda i: (0,)),
            pl.BlockSpec((layers, MIX_BLOCK, width), lambda i: (0, i, 0)),
        ],
        out_specs=[row_spec, row_spec],
        out_shape=[
            jax.ShapeDtypeStruct((rows, width), jnp.float32),
            jax.ShapeDtypeStruct((rows, width), jnp.bfloat16),
        ],
        compiler_params=params(57),
        cost_estimate=cost(1000, 1000),
        name="mix",
    )(weights, gain, history)


def unmix_kernel(
    weights_ref, gain_ref, mixed_ref, middle_ref, own_ref, upper_ref, lower_ref, gain_mlp_ref,
    history_ref, *refs,
):
    grad_ref, small_ref, held_ref, sems = refs[-4:]
    copies = layer_copies(history_ref, held_ref, sems)
    for copy in copies:
        copy.start()
    layers = held_ref.shape[1]
    small_ref[...] = jnp.zeros_like(small_ref)
    small_ref[1:2] = gain_mlp_ref[...]
    for index, copy in enumerate(copies):
        rows = pl.ds(index * ROW_BLOCK, ROW_BLOCK)
        start = index * ROW_BLOCK
        part, start = (upper_ref, start) if start < HALF_ROWS else (lower_ref, start - HALF_ROWS)
        other = part[start : start + ROW_BLOCK, :].astype(jnp.float32)
        grad_first = own_ref[rows, :] + other
        normed, inv_scale = normalize(mixed_ref[rows, :])
        grad_mixed = middle_ref[rows, :] + norm_back(
            grad_first, gain_ref[...], normed, inv_scale
        )
        grad_ref[rows, :] = grad_mixed
        small_ref[0:1] += jnp.sum(grad_first * normed, axis=0, keepdims=True)
        copy.wait()
        for layer in range(layers):
            product = held_ref[index, layer].astype(jnp.float32) * grad_mixed
            small_ref[8 + layer : 9 + layer] += jnp.sum(product, axis=0, keepdims=True)


def unmix(weights, history, gain, mixed, grad_middle, own, other, gain_grad_mlp, after=()):
    layers, rows, width = history.shape
    in_vmem = pl.BlockSpec(memory_space=pltpu.VMEM)
    blocks = rows // ROW_BLOCK
    return pl.pallas_call(
        unmix_kernel,
        in_specs=[pl.BlockSpec(memory_space=pltpu.SMEM)]
        + [in_vmem] * 7
        + [pl.BlockSpec(memory_space=pltpu.HBM)]
        + [pl.BlockSpec(memory_space=pl.ANY)] * len(after),
        out_specs=[in_vmem, in_vmem],
        out_shape=[
            jax.ShapeDtypeStruct((rows, width), jnp.float32),
            jax.ShapeDtypeStruct((SMALL_ROWS, width), jnp.float32),
        ],
        scratch_shapes=[
            pltpu.VMEM((blocks, layers, ROW_BLOCK, width), jnp.bfloat16),
            pltpu.SemaphoreType.DMA((blocks,)),
        ],
        compiler_params=params(9),
        cost_estimate=cost(1000, 1000),
        name="unmix",
    )(weights, gain, mixed, grad_middle, own, *other, gain_grad_mlp, history, *after)


def outputs_kernel(
    weights_ref, grad_ref, rows_ref, block_own_ref, upper_ref, lower_ref, *refs
):
    grads_ref, out_ref, token_ref, given_ref, made_ref, sems, made_sem = refs[-7:]
    token_ref[...] = jnp.zeros_like(token_ref)
    gives = layer_copies(grads_ref, given_ref, sems, True)
    other = jnp.concatenate([upper_ref[...], lower_ref[...]], axis=0).astype(jnp.float32)
    made_ref[...] = (rows_ref[...] + block_own_ref[...] + other).astype(jnp.bfloat16)
    make = pltpu.make_async_copy(made_ref, out_ref, made_sem)
    make.start()
    for index, give in enumerate(gives):
        grad_mixed = grad_ref[pl.ds(index * ROW_BLOCK, ROW_BLOCK), :]
        for layer in range(given_ref.shape[1]):
            given_ref[index, layer] = (weights_ref[layer] * grad_mixed).astype(jnp.bfloat16)
        give.start()
    make.wait()
    for give in gives:
        give.wait()


def outputs(weights, grad_mixed, rows, block_own, block_other, after=()):
    layers = weights.shape[0]
    count, width = grad_mixed.shape
    in_vmem = pl.BlockSpec(memory_space=pltpu.VMEM)
    in_hbm = pl.BlockSpec(memory_space=pltpu.HBM)
    blocks = count // ROW_BLOCK
    return pl.pallas_call(
        outputs_kernel,
        in_specs=[pl.BlockSpec(memory_space=pltpu.SMEM)]
        + [in_vmem] * 5
        + [pl.BlockSpec(memory_space=pl.ANY)] * len(after),
        out_specs=[in_hbm, in_hbm, in_vmem],
        out_shape=[
            jax.ShapeDtypeStruct((layers, count, width), jnp.bfloat16),
            jax.ShapeDtypeStruct((count, width), jnp.bfloat16),
            jax.ShapeDtypeStruct((8, 128), jnp.float32),
        ],
        scratch_shapes=[
            pltpu.VMEM((blocks, layers, ROW_BLOCK, width), jnp.bfloat16),
            pltpu.VMEM((count, width), jnp.bfloat16),
            pltpu.SemaphoreType.DMA((blocks,)),
            pltpu.SemaphoreType.DMA,
        ],
        compiler_params=params(10),
        cost_estimate=cost(1000, 1000),
        name="outputs",
    )(weights, grad_mixed, rows, block_own, *block_other, *after)


def head_mask(head):
    lanes = lax.broadcasted_iota(jnp.int32, (1, PAIR), 1)
    return (lanes // HEAD_DIM) == head


def future_mask():
    keys = lax.broadcasted_iota(jnp.int32, (TILE, TILE), 0)
    asks = lax.broadcasted_iota(jnp.int32, (TILE, TILE), 1)
    return keys > asks


def stacked_heads(rows):
    zero = jnp.zeros_like(rows)
    return jnp.concatenate([jnp.where(head_mask(head), rows, zero) for head in range(2)], axis=0)


def own_heads(columns):
    half = columns.shape[1] // 2
    return jnp.concatenate([columns[:HEAD_DIM, :half], columns[HEAD_DIM:, half:]], axis=0)


def local_call(kernel, name, at, arrays, outs, after=(), scratch=(), aliases=None,
               mebibytes=8):
    in_vmem = pl.BlockSpec(memory_space=pltpu.VMEM)
    return pl.pallas_call(
        kernel,
        in_specs=[pl.BlockSpec(memory_space=pltpu.SMEM)]
        + [in_vmem] * len(arrays)
        + [pl.BlockSpec(memory_space=pl.ANY)] * len(after),
        out_specs=[in_vmem] * len(outs),
        out_shape=[jax.ShapeDtypeStruct(shape, dtype) for shape, dtype in outs],
        scratch_shapes=list(scratch),
        input_output_aliases=aliases or {},
        compiler_params=params(mebibytes),
        cost_estimate=cost(1000, 1000),
        name=name,
    )(at, *arrays, *after)


def attend_kernel(
    at_ref, own_ref, other_ref, weight_ref, out_weight_ref, *refs,
):
    qkv_ref, att_ref, lse_ref, out_own_ref, out_other_ref = refs[-5:]
    rows = own_ref.shape[0]
    tiles = rows // TILE
    first = at_ref[0]
    scale = HEAD_DIM ** (-0.5) * LOG2E
    places = (first, 1 - first)
    later = jnp.concatenate([future_mask()] * 2, axis=1)

    def one_pair(pair, carry):
        lanes = pl.ds(pl.multiple_of(pair * PAIR, PAIR), PAIR)
        weight = jnp.concatenate([weight_ref[c, :, lanes] for c in range(3)], axis=1)
        for side, ref in enumerate((own_ref, other_ref)):
            made = dot(ref[...], weight).astype(jnp.bfloat16)
            for c in range(3):
                qkv_ref[c, side, :, lanes] = made[:, c * PAIR : (c + 1) * PAIR]
        half_keys = [qkv_ref[1, places[half], :, lanes] for half in range(2)]
        half_values = [qkv_ref[2, places[half], :, lanes].T for half in range(2)]
        for half in range(2):
            for tile in range(tiles):
                at_rows = pl.ds(tile * TILE, TILE)
                queries = qkv_ref[0, places[half], at_rows, lanes]
                asked = stacked_heads(queries)
                spans = []
                if half == 1:
                    spans.append((0, 0, rows))
                if tile > 0:
                    spans.append((half, 0, tile * TILE))
                spans.append((half, tile * TILE, TILE))
                scores = [
                    dot(half_keys[where][start : start + size], asked, CONTRACT_COLS)
                    for where, start, size in spans
                ]
                scores[-1] = jnp.where(later, NEG, scores[-1])
                top = functools.reduce(
                    jnp.maximum, [jnp.max(part, axis=0, keepdims=True) for part in scores]
                )
                top = top * scale
                total = 0.0
                summed = 0.0
                for part, (where, start, size) in zip(scores, spans):
                    weights = jnp.exp2(part * scale - top)
                    total = total + jnp.sum(weights, axis=0, keepdims=True)
                    summed = summed + dot(
                        half_values[where][:, start : start + size], weights.astype(jnp.bfloat16)
                    )
                lse = top + jnp.log2(total)
                for head in range(2):
                    lse_ref[pair, head, half, :, at_rows] = lse[:, head * TILE : (head + 1) * TILE]
                joined = own_heads(summed / total).T
                att_ref[places[half], at_rows, lanes] = joined.astype(jnp.bfloat16)
        return carry

    lax.fori_loop(0, att_ref.shape[2] // PAIR, one_pair, 0)
    out_other_ref[...] = dot(att_ref[1], out_weight_ref[...]).astype(jnp.bfloat16)
    out_own_ref[...] = dot(att_ref[0], out_weight_ref[...])


def attend(at, own, other, weight, out_weight, after=()):
    rows, width = own.shape
    local = weight.shape[2]
    return local_call(
        attend_kernel,
        "attend",
        at,
        [own, other, weight, out_weight],
        [
            ((3, 2, rows, local), jnp.bfloat16),
            ((2, rows, local), jnp.bfloat16),
            ((local // PAIR, 2, 2, 1, rows), jnp.float32),
            ((rows, width), jnp.float32),
            ((rows, width), jnp.bfloat16),
        ],
        after,
        mebibytes=12,
    )


def renorm_kernel(at_ref, mixed_ref, own_ref, other_ref, gain_ref, *refs):
    middle_ref, second_ref = refs[-2:]
    middle = mixed_ref[...] + own_ref[...] + other_ref[...].astype(jnp.float32)
    middle_ref[...] = middle
    second_ref[...] = (normalize(middle)[0] * gain_ref[...]).astype(jnp.bfloat16)


def renorm(at, mixed, own, other, gain, after=()):
    return local_call(
        renorm_kernel,
        "renorm",
        at,
        [mixed, own, other, gain],
        [(mixed.shape, jnp.float32), (mixed.shape, jnp.bfloat16)],
        after,
    )


def hidden_back_kernel(at_ref, cot_ref, down_ref, *refs):
    refs[-1][...] = dot(cot_ref[...], down_ref[...], CONTRACT_COLS).astype(jnp.bfloat16)


def hidden_back(at, cotangent, down, after=()):
    outs = [((cotangent.shape[0], down.shape[0]), jnp.bfloat16)]
    return local_call(
        hidden_back_kernel, "hidden_back", at, [cotangent, down], outs, after
    )[0]


def split_halves(bit, rows, top, bottom, keep_ref, send_ref):
    shape = (keep_ref.shape[0], -1, keep_ref.shape[2])
    top = top.astype(jnp.bfloat16).reshape(shape)
    bottom = bottom.astype(jnp.bfloat16).reshape(shape)
    keep_ref[:, rows, :] = jnp.where(bit == 0, top, bottom)
    send_ref[:, rows, :] = jnp.where(bit == 0, bottom, top)


def give_halves(upper_ref, lower_ref, value):
    value = value.astype(jnp.bfloat16)
    upper_ref[...], lower_ref[...] = value[:HALF_ROWS], value[HALF_ROWS:]


def take_halves(upper_ref, lower_ref):
    return jnp.concatenate([upper_ref[...], lower_ref[...]], axis=0)


def mlp_kernel(
    slots, at_ref, second_own_ref, second_other_ref, cot_own_ref, cot_other_ref, back_own_ref,
    back_other_ref, up_ref, *refs,
):
    stacks = refs[-5 - 2 * len(slots) : -5]
    hidden_ref, own_ref, upper_ref, lower_ref, grad_pre_ref = refs[-5:]
    bf16 = jnp.bfloat16
    chunks = hidden_ref.shape[2] // CHUNK
    sides = ((second_own_ref, cot_own_ref), (second_other_ref, cot_other_ref))
    backs = (back_own_ref, back_other_ref)
    unit = TILE // stacks[0].shape[0]
    homes = []
    for index in range(len(slots)):
        keep_ref, send_ref = stacks[2 * index : 2 * index + 2]
        for place in range(keep_ref.shape[1] // unit):
            homes.append((slots[index], pl.ds(place * unit, unit), keep_ref, send_ref))

    def make(chunk):
        lanes = pl.ds(chunk * CHUNK, CHUNK)
        for side, (second_ref, _) in enumerate(sides):
            pre = dot(second_ref[...], up_ref[:, lanes])
            cdf = 0.5 * (1.0 + lax.erf(pre * SQRT_HALF))
            hidden_ref[side, :, lanes] = (pre * cdf).astype(bf16)
            slope = cdf + pre * jnp.exp(-0.5 * pre * pre) * INV_ROOT_TWO_PI
            grad_hidden = backs[side][:, lanes].astype(jnp.float32)
            grad_pre_ref[side, :, lanes] = (grad_hidden * slope).astype(bf16)

    def give(chunk):
        lanes = pl.ds(chunk * CHUNK, CHUNK)
        grad_up, grad_down = 0.0, 0.0
        for side, (second_ref, cot_ref) in enumerate(sides):
            grad_up = grad_up + dot(grad_pre_ref[side, :, lanes], second_ref[...], CONTRACT_ROWS)
            grad_down = grad_down + dot(hidden_ref[side, :, lanes], cot_ref[...], CONTRACT_ROWS)
        for part in range(CHUNK // TILE):
            slot, place, *home = homes[chunk * (CHUNK // TILE) + part]
            rows = slice(part * TILE, (part + 1) * TILE)
            split_halves(at_ref[slot], place, grad_up[rows], grad_down[rows], *home)

    make(0)
    for chunk in range(1, chunks):
        make(chunk)
        give(chunk - 1)
    give(chunks - 1)
    give_halves(upper_ref, lower_ref, dot(grad_pre_ref[1], up_ref[...], CONTRACT_COLS))
    own_ref[...] = dot(grad_pre_ref[0], up_ref[...], CONTRACT_COLS)


def mlp(at, slots, second_own, second_other, cot_own, cot_other, back_own, back_other, up,
        after=()):
    rows, width = second_own.shape
    hidden = up.shape[1]
    blocks = 2 ** (SPLITS - 1)
    unit = TILE // blocks
    stacks = []
    for count in MLP_UNITS:
        stacks += [((blocks, count * unit, width), jnp.bfloat16)] * 2
    half = ((HALF_ROWS, width), jnp.bfloat16)
    return local_call(
        functools.partial(mlp_kernel, slots),
        "mlp",
        at,
        [second_own, second_other, cot_own, cot_other, back_own, back_other, up],
        stacks
        + [((2, rows, hidden), jnp.bfloat16), ((rows, width), jnp.float32), half, half],
        after,
        [pltpu.VMEM((2, rows, hidden), jnp.bfloat16)],
    )


def rows_kernel(at_ref, rows_ref, weight_ref, *refs):
    own_ref, upper_ref, lower_ref = refs[-3:]
    give_halves(upper_ref, lower_ref, dot(rows_ref[1], weight_ref[...]))
    own_ref[...] = dot(rows_ref[0], weight_ref[...])


def rows_times(at, rows, weight, after=()):
    shape = (rows.shape[1], weight.shape[1])
    half = ((HALF_ROWS, weight.shape[1]), jnp.bfloat16)
    return local_call(
        rows_kernel, "block", at, [rows, weight], [(shape, jnp.float32), half, half], after
    )


def norm_back_kernel(
    at_ref, own_ref, up_other_ref, low_other_ref, middle_ref, cot_ref, gain_ref, *refs
):
    grad_ref, upper_ref, lower_ref, gain_grad_ref = refs[-4:]
    grad_second = own_ref[...] + take_halves(up_other_ref, low_other_ref).astype(jnp.float32)
    normed, inv_scale = normalize(middle_ref[...])
    grad = cot_ref[...].astype(jnp.float32) + norm_back(
        grad_second, gain_ref[...], normed, inv_scale
    )
    grad_ref[...] = grad
    give_halves(upper_ref, lower_ref, grad)
    gain_grad_ref[...] = jnp.sum(grad_second * normed, axis=0, keepdims=True)


def norm_back_rows(at, own, other, middle, cotangent, gain, after=()):
    shape = own.shape
    half = ((HALF_ROWS, shape[1]), jnp.bfloat16)
    return local_call(
        norm_back_kernel,
        "norm_back_rows",
        at,
        [own, *other, middle, cotangent, gain],
        [(shape, jnp.float32), half, half, ((1, shape[1]), jnp.float32)],
        after,
    )


def attend_back_kernel(
    slot, pair, place, at_ref, qkv_ref, att_ref, lse_ref, up_own_ref, low_own_ref, up_other_ref,
    low_other_ref, out_weight_ref, first_own_ref, first_other_ref, *refs,
):
    keep_ref, send_ref, grad_rows_ref = refs[-3:]
    rows = first_own_ref.shape[0]
    tiles = rows // TILE
    first = at_ref[0]
    plain = HEAD_DIM ** (-0.5)
    scale = plain * LOG2E
    places = (first, 1 - first)
    later = jnp.concatenate([future_mask()] * 2, axis=1)
    bf16 = jnp.bfloat16
    sides = (take_halves(up_own_ref, low_own_ref), take_halves(up_other_ref, low_other_ref))
    firsts = (first_own_ref, first_other_ref)
    unit = 4 * PAIR // (2 * keep_ref.shape[0])
    is_own = [places[half] == 0 for half in range(2)]
    chunks = [(half, tile) for half in range(2) for tile in range(tiles)]

    def plus(old, term):
        return term if old is None else old + term

    lanes = pl.ds(pair * PAIR, PAIR)
    outer = [
        dot(rows_here, out_weight_ref[lanes, :], CONTRACT_COLS).astype(bf16)
        for rows_here in sides
    ]
    grads = [jnp.where(is_own[half], outer[0], outer[1]) for half in range(2)]
    queries, keys, values = [
        [qkv_ref[c, places[half], :, lanes] for half in range(2)] for c in range(3)
    ]
    keys_t = [part.T for part in keys]
    deltas = []
    for half in range(2):
        attended = att_ref[places[half], :, lanes].astype(jnp.float32)
        product = (grads[half].astype(jnp.float32) * attended).T
        deltas.append([
            jnp.sum(product[head * HEAD_DIM : (head + 1) * HEAD_DIM], axis=0, keepdims=True)
            for head in range(2)
        ])
    key_grads = {}
    value_grads = {}
    query_grads = []
    for half, tile in chunks:
        here = slice(tile * TILE, (tile + 1) * TILE)
        asked = stacked_heads(queries[half][here])
        grad = stacked_heads(grads[half][here])
        lse = jnp.concatenate([lse_ref[pair, head, half, :, here] for head in range(2)], axis=1)
        delta = jnp.concatenate([deltas[half][head][:, here] for head in range(2)], axis=1)
        spans = []
        if half == 1:
            spans.append((0, 0, rows))
        if tile > 0:
            spans.append((half, 0, tile * TILE))
        spans.append((half, tile * TILE, TILE))
        query_grad = None
        for where, start, size in spans:
            span = slice(start, start + size)
            scores = dot(keys[where][span], asked, CONTRACT_COLS)
            probs = jnp.exp2(scores * scale - lse)
            if (where, start) == (half, tile * TILE):
                probs = jnp.where(later, 0.0, probs)
            grad_probs = dot(values[where][span], grad, CONTRACT_COLS)
            grad_scores = (probs * (grad_probs - delta)).astype(bf16)
            value_term = dot(probs.astype(bf16), grad)
            key_term = dot(grad_scores, asked)
            query_grad = plus(query_grad, dot(keys_t[where][:, span], grad_scores))
            for part in range(size // TILE):
                at_part = (where, start // TILE + part)
                cut = slice(part * TILE, (part + 1) * TILE)
                value_grads[at_part] = plus(value_grads.get(at_part), value_term[cut])
                key_grads[at_part] = plus(key_grads.get(at_part), key_term[cut])
        query_grads.append((own_heads(query_grad) * plain).astype(bf16))
    turned = []
    for half in range(2):
        at_half = [i for i, (where, _) in enumerate(chunks) if where == half]
        query_t = jnp.concatenate([query_grads[i] for i in at_half], axis=1)
        key = jnp.concatenate(
            [(key_grads[half, tile] * plain).astype(bf16) for tile in range(tiles)], axis=0
        )
        value = jnp.concatenate(
            [value_grads[half, tile].astype(bf16) for tile in range(tiles)], axis=0
        )
        turned.append([query_t, key.T, value.T, att_ref[places[half], :, lanes].T])
        for c, part in enumerate((query_t.T, key, value)):
            grad_rows_ref[c, places[half]] = part
    top, bottom = 0.0, 0.0
    for side in range(2):
        mine = [jnp.where(is_own[side], a, b) for a, b in zip(turned[0], turned[1])]
        rows_here = firsts[side][...]
        top = top + dot(jnp.concatenate(mine[:2], axis=0), rows_here)
        bottom = bottom + jnp.concatenate(
            [dot(mine[2], rows_here), dot(mine[3], sides[side])], axis=0
        )
    split_halves(at_ref[slot], pl.ds(place * unit, unit), top, bottom, keep_ref, send_ref)


def attend_back(at, slot, pair, place, count, qkv, att, lse, grad_own, grad_other, out_weight,
                first_own, first_other, old=(), after=()):
    rows, width = first_own.shape
    blocks = 2 ** (SPLITS - 1)
    unit = 4 * PAIR // (2 * blocks)
    pieces = ((blocks, count * unit, width), jnp.bfloat16)
    arrays = [qkv, att, lse, *grad_own, *grad_other, out_weight, first_own, first_other, *old]
    return local_call(
        functools.partial(attend_back_kernel, slot, pair, place),
        "attend_back",
        at,
        arrays,
        [pieces, pieces, ((3, 2, rows, PAIR), jnp.bfloat16)],
        after,
        aliases={len(arrays) - 1: 0, len(arrays): 1} if old else {},
        mebibytes=12,
    )


def first_back_kernel(count, at_ref, weight_ref, *refs):
    own_ref, upper_ref, lower_ref = refs[-3:]
    pieces = []
    for index, ref in enumerate(refs[:count]):
        lanes = slice(index * PAIR, (index + 1) * PAIR)
        pieces += [(ref, c, lanes) for c in range(3)]
    weight = jnp.concatenate([weight_ref[c, :, lanes] for _, c, lanes in pieces], axis=1)
    own, other = [
        jnp.concatenate([ref[c, side] for ref, c, _ in pieces], axis=1) for side in range(2)
    ]
    give_halves(upper_ref, lower_ref, dot(other, weight, CONTRACT_COLS))
    own_ref[...] = dot(own, weight, CONTRACT_COLS)


def first_back(at, weight, groups, after=()):
    shape = (groups[0].shape[2], weight.shape[1])
    half = ((HALF_ROWS, weight.shape[1]), jnp.bfloat16)
    return local_call(
        functools.partial(first_back_kernel, len(groups)), "first_back", at, [weight, *groups],
        [(shape, jnp.float32), half, half], after,
    )


def fold_kernel(slot, at_ref, kept_ref, came_ref, *refs):
    keep_ref, send_ref = refs[-2:]
    half = keep_ref.shape[0]
    bit = at_ref[slot]
    for target, start in ((send_ref, (1 - bit) * half), (keep_ref, bit * half)):
        for index in range(half):
            total = kept_ref[start + index].astype(jnp.float32) + came_ref[
                start + index
            ].astype(jnp.float32)
            target[index] = total.astype(jnp.bfloat16)


def add_kernel(at_ref, kept_ref, came_ref, *refs):
    total = kept_ref[...].astype(jnp.float32) + came_ref[...].astype(jnp.float32)
    refs[-1][...] = total.astype(jnp.bfloat16)


def widen(pair):
    half = pair.shape[0] // 2
    pair = pair.astype(jnp.float32)
    return pair[:half] + pair[half:]


def narrow(value):
    high = value.astype(jnp.bfloat16)
    low = (value - high.astype(jnp.float32)).astype(jnp.bfloat16)
    return jnp.concatenate([high, low], axis=0)


def add_small_kernel(at_ref, kept_ref, came_ref, mine_ref, other_ref, *refs):
    total = kept_ref[0].astype(jnp.float32) + came_ref[0].astype(jnp.float32)
    refs[-1][0] = total.astype(jnp.bfloat16)
    refs[-1][1] = narrow(mine_ref[...] + other_ref[...])


def again_kernel(at_ref, mine_ref, came_ref, *refs):
    total = mine_ref[0].astype(jnp.float32) + came_ref[0].astype(jnp.float32)
    refs[-1][0] = total.astype(jnp.bfloat16)
    if mine_ref.shape[0] > 1:
        refs[-1][1] = narrow(widen(mine_ref[1]) + widen(came_ref[1]))


def join_kernel(slot, at_ref, mine_ref, came_ref, *refs):
    both_ref = refs[-1]
    half = both_ref.shape[0] // 2
    bit = at_ref[slot]
    for source, start in ((mine_ref, bit * half), (came_ref, (1 - bit) * half)):
        for index in range(half):
            both_ref[start + index] = source[index]
    if both_ref.shape[0] > 2 * half:
        both_ref[2 * half] = narrow(widen(mine_ref[half]) + widen(came_ref[half]))


def fold(at, slot, kept, came, after=()):
    blocks, rows, width = kept.shape
    outs = [((blocks // 2, rows, width), jnp.bfloat16)] * 2
    return local_call(
        functools.partial(fold_kernel, slot), "fold", at, [kept, came], outs, after
    )


def last_fold(at, kept, came, small, after=()):
    blocks, rows, width = kept.shape
    kernel = add_small_kernel if small else add_kernel
    outs = [((blocks + (1 if small else 0), rows, width), jnp.bfloat16)]
    return local_call(kernel, "add", at, [kept, came, *small], outs, after)[0]


def again(at, mine, came, after=()):
    outs = [(mine.shape, jnp.bfloat16)]
    return local_call(again_kernel, "again", at, [mine, came], outs, after)[0]


def join(at, slot, mine, came, blocks, after=()):
    _, rows, width = mine.shape
    extra = mine.shape[0] - blocks
    outs = [((2 * blocks + extra, rows, width), jnp.bfloat16)]
    return local_call(
        functools.partial(join_kernel, slot), "join", at, [mine, came], outs, after
    )[0]


def ordered_units(bit, mine_ref, came_ref, blocks, unit):
    width = mine_ref.shape[2]
    for index in range(mine_ref.shape[1] // unit):
        rows = slice(index * unit, (index + 1) * unit)
        mine = mine_ref[:blocks, rows, :].reshape(blocks * unit, width)
        came = came_ref[:blocks, rows, :].reshape(blocks * unit, width)
        yield index, jnp.where(bit == 0, mine, came), jnp.where(bit == 0, came, mine)


def finish_mlp_kernel(slot, start, blocks, at_ref, mine_ref, came_ref, *refs):
    up_ref, down_ref, token_ref, turned_ref, held_ref, up_sems, down_sems = refs[-7:]
    token_ref[...] = jnp.zeros_like(token_ref)
    copies = []
    for index, top, bottom in ordered_units(
        at_ref[slot], mine_ref, came_ref, blocks, TILE // blocks
    ):
        place = pl.ds((start + index) * TILE, TILE)
        held_ref[index] = bottom.astype(jnp.float32)
        copies.append(
            pltpu.make_async_copy(held_ref.at[index], down_ref.at[place, :], down_sems.at[index])
        )
        copies[-1].start()
        turned_ref[index] = top.T.astype(jnp.float32)
        copies.append(
            pltpu.make_async_copy(turned_ref.at[index], up_ref.at[:, place], up_sems.at[index])
        )
        copies[-1].start()
    for copy in copies:
        copy.wait()


def finish_attend_kernel(slot, start, blocks, at_ref, mine_ref, came_ref, *refs):
    qkv_ref, out_ref, token_ref, turned_ref, held_ref, qkv_sems, out_sems = refs[-7:]
    token_ref[...] = jnp.zeros_like(token_ref)
    if mine_ref.shape[0] > blocks:
        token_ref[...] = widen(mine_ref[blocks]) + widen(came_ref[blocks])
    copies = []
    for index, top, bottom in ordered_units(
        at_ref[slot], mine_ref, came_ref, blocks, 2 * PAIR // blocks
    ):
        place = pl.ds((start + index) * PAIR, PAIR)
        held_ref[index] = bottom[PAIR:].astype(jnp.float32)
        copies.append(
            pltpu.make_async_copy(held_ref.at[index], out_ref.at[place, :], out_sems.at[index])
        )
        copies[-1].start()
        for c, part in enumerate((top[:PAIR], top[PAIR:], bottom[:PAIR])):
            turned_ref[index, c] = part.T.astype(jnp.float32)
        copies.append(
            pltpu.make_async_copy(
                turned_ref.at[index], qkv_ref.at[:, :, place], qkv_sems.at[index]
            )
        )
        copies[-1].start()
    for copy in copies:
        copy.wait()


def finish(kernel, name, at, slot, start, mine, came, shapes, scratch, old=None, after=()):
    in_vmem = pl.BlockSpec(memory_space=pltpu.VMEM)
    in_hbm = pl.BlockSpec(memory_space=pltpu.HBM)
    blocks = 2 ** (SPLITS - 1)
    units = mine.shape[1] * blocks // TILE
    return pl.pallas_call(
        functools.partial(kernel, slot, start, blocks),
        in_specs=[pl.BlockSpec(memory_space=pltpu.SMEM), in_vmem, in_vmem]
        + [in_hbm] * len(old or [])
        + [pl.BlockSpec(memory_space=pl.ANY)] * len(after),
        out_specs=[in_hbm, in_hbm, in_vmem],
        out_shape=[jax.ShapeDtypeStruct(shape, jnp.float32) for shape in shapes]
        + [jax.ShapeDtypeStruct((SMALL_ROWS, mine.shape[2]), jnp.float32)],
        scratch_shapes=[pltpu.VMEM((units, *shape), jnp.float32) for shape in scratch]
        + [pltpu.SemaphoreType.DMA((units,))] * 2,
        input_output_aliases={3: 0, 4: 1} if old else {},
        compiler_params=params(12),
        cost_estimate=cost(1000, 1000),
        name=name,
    )(at, mine, came, *(old or []), *after)


def finish_mlp(at, slot, start, mine, came, width, hidden, old=None, after=()):
    shapes = [(width, hidden), (hidden, width)]
    scratch = [(width, TILE), (TILE, width)]
    return finish(
        finish_mlp_kernel, "finish_mlp", at, slot, start, mine, came, shapes, scratch, old, after
    )


def finish_attend(at, slot, start, mine, came, width, local, old=None, after=()):
    shapes = [(3, width, local), (local, width)]
    scratch = [(3, width, PAIR), (PAIR, width)]
    return finish(
        finish_attend_kernel, "finish_attend", at, slot, start, mine, came, shapes, scratch, old,
        after,
    )


def mp_swap(rows):
    return lax.ppermute(rows, "mp", [(0, 1), (1, 0)])


def dp_bits():
    return lax.axis_size("dp").bit_length() - 1


def bit_swap(rows, bits):
    size, cores = lax.axis_size("dp"), lax.axis_size("mp")
    pairs = [
        (i * cores + core, (i ^ (1 << bits[core])) * cores + core)
        for i in range(size)
        for core in range(cores)
    ]
    return lax.ppermute(rows, ("dp", "mp"), pairs)


def step_bits(kind, step):
    return [order[step] for order in KINDS[kind]]


def slot_of(kind, step):
    return 1 + kind * SPLITS + step


def where_am_i():
    core, index = lax.axis_index("mp"), lax.axis_index("dp")
    values = [core]
    for kind in range(len(KINDS)):
        for step in range(SPLITS):
            bits = step_bits(kind, step)
            values.append((index >> jnp.where(core == 0, bits[0], bits[1])) & 1)
    return jnp.stack(values).astype(jnp.int32)


class Stream:
    def __init__(self, at, kind, kept, sent, small=None):
        self.at, self.kind, self.kept, self.step, self.small = at, kind, kept, 0, small
        self.extra = dp_bits() - SPLITS
        self.came = bit_swap(sent, step_bits(kind, 0))

    def advance(self, after=()):
        step, kind, at = self.step, self.kind, self.at
        self.step += 1
        joined = step - SPLITS - self.extra
        if step < SPLITS - 1:
            self.kept, sent = fold(at, slot_of(kind, step + 1), self.kept, self.came, after)
            self.came = bit_swap(sent, step_bits(kind, step + 1))
            return self.kept
        if step == SPLITS - 1:
            small = self.small() if self.small else ()
            self.kept = last_fold(at, self.kept, self.came, small, after)
        elif joined < 0:
            self.kept = again(at, self.kept, self.came, after)
        else:
            slot = slot_of(kind, SPLITS - 1 - joined)
            self.kept = join(at, slot, self.kept, self.came, 2**joined, after)
        if joined < -1:
            bit = SPLITS + joined + 1 + self.extra
            self.came = bit_swap(self.kept, [bit, bit])
        else:
            self.came = bit_swap(self.kept, step_bits(kind, SPLITS - 2 - joined))
        return self.kept


def shards(
    history,
    depth_weights,
    gain_attn,
    gain_mlp,
    qkv_weight,
    out_weight,
    up_weight,
    down_weight,
    cotangent,
):
    width = cotangent.shape[1]
    local = out_weight.shape[0]
    hidden = down_weight.shape[0]
    pairs = local // PAIR
    at = where_am_i()

    cot_other = mp_swap(cotangent)
    mixed, first = mix(depth_weights, history, gain_attn)
    first_other = mp_swap(first)
    back_own = hidden_back(at, cotangent, down_weight, [first])
    qkv, att, lse, out_own, out_other = attend(
        at, first, first_other, qkv_weight, out_weight, [back_own]
    )
    middle, second = renorm(at, mixed, out_own, mp_swap(out_other), gain_mlp)
    back_other = hidden_back(at, cot_other, down_weight, [second])
    second_other = mp_swap(second)
    mlp_names = [name for name in KIND if name[0] == "M"]
    *stacks, hidden_rows, grad_own, grad_upper, grad_lower = mlp(
        at, tuple(slot_of(KIND[name], 0) for name in mlp_names), second, second_other, cotangent,
        cot_other, back_own, back_other, up_weight,
    )
    streams = {
        name: Stream(at, KIND[name], *stacks[2 * i : 2 * i + 2])
        for i, name in enumerate(mlp_names)
    }
    grad_came = [mp_swap(part) for part in (grad_upper, grad_lower)]
    made = {}

    def back_norm(after):
        made["middle"], *made["narrow"], made["gain"] = norm_back_rows(
            at, grad_own, grad_came, middle, cotangent, gain_mlp, after
        )
        made["narrow_came"] = [mp_swap(part) for part in made["narrow"]]
        return made["gain"]

    def back_pair(pair, after):
        late = pair == pairs - 1
        name, place = ("Ab", 0) if late else ("Aa", pair)
        old = () if late or pair == 0 else made["stack"]
        kept, sent, made[pair] = attend_back(
            at, slot_of(KIND[name], 0), pair, place, 1 if late else pairs - 1, qkv, att, lse,
            made["narrow"], made["narrow_came"], out_weight, first, first_other, old, after,
        )
        made["stack"] = (kept, sent)
        if pair >= pairs - 2:
            small = (lambda: (made["small"], made["small_came"])) if late else None
            streams[name] = Stream(at, KIND[name], kept, sent, small)
        return made[pair]

    def back_first(after):
        groups = [made[pair] for pair in range(pairs)]
        made["own"], *other = first_back(at, qkv_weight, groups, after)
        made["came"] = [mp_swap(part) for part in other]
        return made["own"]

    def back_start(after):
        made["mixed"], made["small"] = unmix(
            depth_weights, history, gain_attn, mixed, made["middle"], made["own"], made["came"],
            made["gain"], after,
        )
        made["small_came"] = mp_swap(made["small"])
        return made["small"]

    def give_outputs(after):
        made["history"], made["out"], token = outputs(
            depth_weights, made["mixed"], middle, made["block"], made["block_came"], after
        )
        return token

    def block_rows(after):
        made["block"], *other = rows_times(at, hidden_rows, down_weight, after)
        made["block_came"] = [mp_swap(part) for part in other]
        return made["block"]

    def end_mlp(name, start, after):
        stream = streams[name]
        *made["mlp"], token = finish_mlp(
            at, slot_of(KIND[name], 0), start, stream.kept, stream.came, width, hidden,
            made.get("mlp"), after,
        )
        return token

    def end_attend(name, start, after):
        stream = streams[name]
        *made["attend"], made[name] = finish_attend(
            at, slot_of(KIND[name], 0), start, stream.kept, stream.came, width, local,
            made.get("attend"), after,
        )
        return made[name]

    units = {
        "nb": back_norm,
        "fb": back_first,
        "um": back_start,
        "um2": give_outputs,
        "blk": block_rows,
        "fAa": functools.partial(end_attend, "Aa", 0),
        "fAb": functools.partial(end_attend, "Ab", pairs - 1),
    }
    start = 0
    for name, count in zip(mlp_names, MLP_UNITS):
        units["f" + name] = functools.partial(end_mlp, name, start)
        start += count
    for pair in range(pairs):
        units["ab" + str(pair)] = functools.partial(back_pair, pair)
    last = hidden_rows
    for name in ORDER:
        if name in streams:
            if streams[name].step == SPLITS:
                for _ in range(streams[name].extra - 1):
                    last = streams[name].advance([last])
            last = streams[name].advance([last])
        else:
            last = units[name]([last])
    small = made["Ab"]
    grad_depth = jnp.sum(small[8 : 8 + history.shape[0]], axis=1)
    block_out, grad_history = made["out"], made["history"]
    gain_grad_attn, gain_grad_mlp = small[0], small[1]
    (grad_up, grad_down), (grad_qkv, grad_out) = made["mlp"], made["attend"]
    return (
        block_out,
        grad_history,
        grad_depth,
        gain_grad_attn,
        gain_grad_mlp,
        grad_qkv,
        grad_out,
        grad_up,
        grad_down,
    )


def solution(mesh):
    in_specs = (
        P(None, ("dp", "mp"), None),
        P(),
        P(),
        P(),
        P(None, None, "mp"),
        P("mp", None),
        P(None, "mp"),
        P("mp", None),
        P(("dp", "mp"), None),
    )
    out_specs = (
        P(("dp", "mp"), None),
        P(None, ("dp", "mp"), None),
        P(),
        P(),
        P(),
        P(None, None, "mp"),
        P("mp", None),
        P(None, "mp"),
        P("mp", None),
    )
    return jax.shard_map(shards, mesh=mesh, in_specs=in_specs, out_specs=out_specs, check_vma=False)
```

```python
import functools

import jax
import jax.numpy as jnp
from jax import lax
from jax.experimental import pallas as pl
from jax.experimental.pallas import tpu as pltpu
from jax.sharding import PartitionSpec as P

HEAD_DIM = 64
EPSILON = 1e-05
SQRT_HALF = 0.7071067811865476
INV_ROOT_TWO_PI = 0.3989422804014327
LOG2E = 1.4426950408889634
NEG = -1e30
TILE = 256
ROW_BLOCK = 64
HALF_ROWS = 256
MIX_BLOCK = 128
SMALL_ROWS = 32
SPLITS = 3
PAIR = 2 * HEAD_DIM
CHUNK = 512
ORDER = (
    "nb", "ab0", "ab1", "Mb", "Ma", "Mc", "ab2", "fb", "Mb", "Ma", "Aa", "Mb", "Mc", "Ma",
    "Aa", "Mb", "Ab", "Mc", "um", "Ma", "Aa", "Mb", "Ab", "Mc", "blk", "Ma", "Aa", "Ab", "Mc",
    "Mb", "Ma", "Mc", "Ab", "Aa", "um2", "Aa", "Ab", "fMb", "fMa", "Ab", "fMc", "fAa", "fAb",
)
KINDS = (
    ((0, 1, 2), (1, 2, 0)),
    ((0, 1, 2), (2, 0, 1)),
    ((2, 1, 0), (1, 0, 2)),
    ((0, 2, 1), (2, 1, 0)),
    ((0, 1, 2), (1, 0, 2)),
)
KIND = {"Ma": 0, "Mb": 1, "Mc": 2, "Aa": 3, "Ab": 4}
MLP_UNITS = (2, 2, 2)

PLAIN = (((1,), (0,)), ((), ()))
CONTRACT_COLS = (((1,), (1,)), ((), ()))
CONTRACT_ROWS = (((0,), (0,)), ((), ()))


def dot(lhs, rhs, dims=PLAIN):
    return lax.dot_general(lhs, rhs, dims, preferred_element_type=jnp.float32)


def cost(flops, moved, exps=0):
    return pl.CostEstimate(flops=flops, bytes_accessed=moved, transcendentals=exps)


def params(mebibytes=8):
    return pltpu.CompilerParams(vmem_limit_bytes=mebibytes * 2**20)


def normalize(inputs):
    row_mean = jnp.mean(inputs, axis=-1, keepdims=True)
    centered = inputs - row_mean
    variance = jnp.mean(centered * centered, axis=-1, keepdims=True)
    inv_scale = lax.rsqrt(variance + EPSILON)
    return centered * inv_scale, inv_scale


def norm_back(grad_rows, gain_row, normed, inv_scale):
    scaled = grad_rows * gain_row
    first_mean = jnp.mean(scaled, axis=-1, keepdims=True)
    second_mean = jnp.mean(scaled * normed, axis=-1, keepdims=True)
    return inv_scale * (scaled - first_mean - normed * second_mean)


def gelu_value(inputs):
    return 0.5 * inputs * (1.0 + lax.erf(inputs * SQRT_HALF))


def gelu_slope(inputs):
    normal_cdf = 0.5 * (1.0 + lax.erf(inputs * SQRT_HALF))
    return normal_cdf + inputs * jnp.exp(-0.5 * inputs * inputs) * INV_ROOT_TWO_PI


def layer_copies(history_ref, held_ref, sems, out=False):
    copies = []
    for index in range(held_ref.shape[0]):
        rows = pl.ds(index * ROW_BLOCK, ROW_BLOCK)
        ends = (history_ref.at[:, rows, :], held_ref.at[index])
        copies.append(
            pltpu.make_async_copy(ends[out], ends[not out], sems.at[index])
        )
    return copies


def mix_kernel(weights_ref, gain_ref, history_ref, mixed_ref, first_ref):
    mixed = weights_ref[0] * history_ref[0].astype(jnp.float32)
    for layer in range(1, history_ref.shape[0]):
        mixed = mixed + weights_ref[layer] * history_ref[layer].astype(jnp.float32)
    mixed_ref[...] = mixed
    normed, _ = normalize(mixed)
    first_ref[...] = (normed * gain_ref[...]).astype(jnp.bfloat16)


def mix(weights, history, gain):
    layers, rows, width = history.shape
    row_spec = pl.BlockSpec((MIX_BLOCK, width), lambda i: (i, 0))
    return pl.pallas_call(
        mix_kernel,
        grid=(rows // MIX_BLOCK,),
        in_specs=[
            pl.BlockSpec(memory_space=pltpu.SMEM),
            pl.BlockSpec((width,), lambda i: (0,)),
            pl.BlockSpec((layers, MIX_BLOCK, width), lambda i: (0, i, 0)),
        ],
        out_specs=[row_spec, row_spec],
        out_shape=[
            jax.ShapeDtypeStruct((rows, width), jnp.float32),
            jax.ShapeDtypeStruct((rows, width), jnp.bfloat16),
        ],
        compiler_params=params(57),
        cost_estimate=cost(1000, 1000),
        name="mix",
    )(weights, gain, history)


def unmix_kernel(
    weights_ref, gain_ref, mixed_ref, middle_ref, own_ref, upper_ref, lower_ref, gain_mlp_ref,
    history_ref, *refs,
):
    grad_ref, small_ref, held_ref, sems = refs[-4:]
    copies = layer_copies(history_ref, held_ref, sems)
    for copy in copies:
        copy.start()
    layers = held_ref.shape[1]
    small_ref[...] = jnp.zeros_like(small_ref)
    small_ref[1:2] = gain_mlp_ref[...]
    for index, copy in enumerate(copies):
        rows = pl.ds(index * ROW_BLOCK, ROW_BLOCK)
        start = index * ROW_BLOCK
        part, start = (upper_ref, start) if start < HALF_ROWS else (lower_ref, start - HALF_ROWS)
        other = part[start : start + ROW_BLOCK, :].astype(jnp.float32)
        grad_first = own_ref[rows, :] + other
        normed, inv_scale = normalize(mixed_ref[rows, :])
        grad_mixed = middle_ref[rows, :] + norm_back(
            grad_first, gain_ref[...], normed, inv_scale
        )
        grad_ref[rows, :] = grad_mixed
        small_ref[0:1] += jnp.sum(grad_first * normed, axis=0, keepdims=True)
        copy.wait()
        for layer in range(layers):
            product = held_ref[index, layer].astype(jnp.float32) * grad_mixed
            small_ref[8 + layer : 9 + layer] += jnp.sum(product, axis=0, keepdims=True)


def unmix(weights, history, gain, mixed, grad_middle, own, other, gain_grad_mlp, after=()):
    layers, rows, width = history.shape
    in_vmem = pl.BlockSpec(memory_space=pltpu.VMEM)
    blocks = rows // ROW_BLOCK
    return pl.pallas_call(
        unmix_kernel,
        in_specs=[pl.BlockSpec(memory_space=pltpu.SMEM)]
        + [in_vmem] * 7
        + [pl.BlockSpec(memory_space=pltpu.HBM)]
        + [pl.BlockSpec(memory_space=pl.ANY)] * len(after),
        out_specs=[in_vmem, in_vmem],
        out_shape=[
            jax.ShapeDtypeStruct((rows, width), jnp.float32),
            jax.ShapeDtypeStruct((SMALL_ROWS, width), jnp.float32),
        ],
        scratch_shapes=[
            pltpu.VMEM((blocks, layers, ROW_BLOCK, width), jnp.bfloat16),
            pltpu.SemaphoreType.DMA((blocks,)),
        ],
        compiler_params=params(9),
        cost_estimate=cost(1000, 1000),
        name="unmix",
    )(weights, gain, mixed, grad_middle, own, *other, gain_grad_mlp, history, *after)


def outputs_kernel(
    weights_ref, grad_ref, rows_ref, block_own_ref, upper_ref, lower_ref, *refs
):
    grads_ref, out_ref, token_ref, given_ref, made_ref, sems, made_sem = refs[-7:]
    token_ref[...] = jnp.zeros_like(token_ref)
    gives = layer_copies(grads_ref, given_ref, sems, True)
    other = jnp.concatenate([upper_ref[...], lower_ref[...]], axis=0).astype(jnp.float32)
    made_ref[...] = (rows_ref[...] + block_own_ref[...] + other).astype(jnp.bfloat16)
    make = pltpu.make_async_copy(made_ref, out_ref, made_sem)
    make.start()
    for index, give in enumerate(gives):
        grad_mixed = grad_ref[pl.ds(index * ROW_BLOCK, ROW_BLOCK), :]
        for layer in range(given_ref.shape[1]):
            given_ref[index, layer] = (weights_ref[layer] * grad_mixed).astype(jnp.bfloat16)
        give.start()
    make.wait()
    for give in gives:
        give.wait()


def outputs(weights, grad_mixed, rows, block_own, block_other, after=()):
    layers = weights.shape[0]
    count, width = grad_mixed.shape
    in_vmem = pl.BlockSpec(memory_space=pltpu.VMEM)
    in_hbm = pl.BlockSpec(memory_space=pltpu.HBM)
    blocks = count // ROW_BLOCK
    return pl.pallas_call(
        outputs_kernel,
        in_specs=[pl.BlockSpec(memory_space=pltpu.SMEM)]
        + [in_vmem] * 5
        + [pl.BlockSpec(memory_space=pl.ANY)] * len(after),
        out_specs=[in_hbm, in_hbm, in_vmem],
        out_shape=[
            jax.ShapeDtypeStruct((layers, count, width), jnp.bfloat16),
            jax.ShapeDtypeStruct((count, width), jnp.bfloat16),
            jax.ShapeDtypeStruct((8, 128), jnp.float32),
        ],
        scratch_shapes=[
            pltpu.VMEM((blocks, layers, ROW_BLOCK, width), jnp.bfloat16),
            pltpu.VMEM((count, width), jnp.bfloat16),
            pltpu.SemaphoreType.DMA((blocks,)),
            pltpu.SemaphoreType.DMA,
        ],
        compiler_params=params(10),
        cost_estimate=cost(1000, 1000),
        name="outputs",
    )(weights, grad_mixed, rows, block_own, *block_other, *after)


def head_mask(head):
    lanes = lax.broadcasted_iota(jnp.int32, (1, PAIR), 1)
    return (lanes // HEAD_DIM) == head


def future_mask():
    keys = lax.broadcasted_iota(jnp.int32, (TILE, TILE), 0)
    asks = lax.broadcasted_iota(jnp.int32, (TILE, TILE), 1)
    return keys > asks


def stacked_heads(rows):
    zero = jnp.zeros_like(rows)
    return jnp.concatenate([jnp.where(head_mask(head), rows, zero) for head in range(2)], axis=0)


def own_heads(columns):
    half = columns.shape[1] // 2
    return jnp.concatenate([columns[:HEAD_DIM, :half], columns[HEAD_DIM:, half:]], axis=0)


def local_call(kernel, name, at, arrays, outs, after=(), scratch=(), aliases=None,
               mebibytes=8):
    in_vmem = pl.BlockSpec(memory_space=pltpu.VMEM)
    return pl.pallas_call(
        kernel,
        in_specs=[pl.BlockSpec(memory_space=pltpu.SMEM)]
        + [in_vmem] * len(arrays)
        + [pl.BlockSpec(memory_space=pl.ANY)] * len(after),
        out_specs=[in_vmem] * len(outs),
        out_shape=[jax.ShapeDtypeStruct(shape, dtype) for shape, dtype in outs],
        scratch_shapes=list(scratch),
        input_output_aliases=aliases or {},
        compiler_params=params(mebibytes),
        cost_estimate=cost(1000, 1000),
        name=name,
    )(at, *arrays, *after)


def attend_kernel(
    at_ref, own_ref, other_ref, weight_ref, out_weight_ref, *refs,
):
    qkv_ref, att_ref, lse_ref, out_own_ref, out_other_ref = refs[-5:]
    rows = own_ref.shape[0]
    tiles = rows // TILE
    first = at_ref[0]
    scale = HEAD_DIM ** (-0.5) * LOG2E
    places = (first, 1 - first)
    later = jnp.concatenate([future_mask()] * 2, axis=1)

    def one_pair(pair, carry):
        lanes = pl.ds(pl.multiple_of(pair * PAIR, PAIR), PAIR)
        weight = jnp.concatenate([weight_ref[c, :, lanes] for c in range(3)], axis=1)
        for side, ref in enumerate((own_ref, other_ref)):
            made = dot(ref[...], weight).astype(jnp.bfloat16)
            for c in range(3):
                qkv_ref[c, side, :, lanes] = made[:, c * PAIR : (c + 1) * PAIR]
        half_keys = [qkv_ref[1, places[half], :, lanes] for half in range(2)]
        half_values = [qkv_ref[2, places[half], :, lanes].T for half in range(2)]
        for half in range(2):
            for tile in range(tiles):
                at_rows = pl.ds(tile * TILE, TILE)
                queries = qkv_ref[0, places[half], at_rows, lanes]
                asked = stacked_heads(queries)
                spans = []
                if half == 1:
                    spans.append((0, 0, rows))
                if tile > 0:
                    spans.append((half, 0, tile * TILE))
                spans.append((half, tile * TILE, TILE))
                scores = [
                    dot(half_keys[where][start : start + size], asked, CONTRACT_COLS)
                    for where, start, size in spans
                ]
                scores[-1] = jnp.where(later, NEG, scores[-1])
                top = functools.reduce(
                    jnp.maximum, [jnp.max(part, axis=0, keepdims=True) for part in scores]
                )
                top = top * scale
                total = 0.0
                summed = 0.0
                for part, (where, start, size) in zip(scores, spans):
                    weights = jnp.exp2(part * scale - top)
                    total = total + jnp.sum(weights, axis=0, keepdims=True)
                    summed = summed + dot(
                        half_values[where][:, start : start + size], weights.astype(jnp.bfloat16)
                    )
                lse = top + jnp.log2(total)
                for head in range(2):
                    lse_ref[pair, head, half, :, at_rows] = lse[:, head * TILE : (head + 1) * TILE]
                joined = own_heads(summed / total).T
                att_ref[places[half], at_rows, lanes] = joined.astype(jnp.bfloat16)
        return carry

    lax.fori_loop(0, att_ref.shape[2] // PAIR, one_pair, 0)
    out_other_ref[...] = dot(att_ref[1], out_weight_ref[...]).astype(jnp.bfloat16)
    out_own_ref[...] = dot(att_ref[0], out_weight_ref[...])


def attend(at, own, other, weight, out_weight, after=()):
    rows, width = own.shape
    local = weight.shape[2]
    return local_call(
        attend_kernel,
        "attend",
        at,
        [own, other, weight, out_weight],
        [
            ((3, 2, rows, local), jnp.bfloat16),
            ((2, rows, local), jnp.bfloat16),
            ((local // PAIR, 2, 2, 1, rows), jnp.float32),
            ((rows, width), jnp.float32),
            ((rows, width), jnp.bfloat16),
        ],
        after,
        mebibytes=12,
    )


def renorm_kernel(at_ref, mixed_ref, own_ref, other_ref, gain_ref, *refs):
    middle_ref, second_ref = refs[-2:]
    middle = mixed_ref[...] + own_ref[...] + other_ref[...].astype(jnp.float32)
    middle_ref[...] = middle
    second_ref[...] = (normalize(middle)[0] * gain_ref[...]).astype(jnp.bfloat16)


def renorm(at, mixed, own, other, gain, after=()):
    return local_call(
        renorm_kernel,
        "renorm",
        at,
        [mixed, own, other, gain],
        [(mixed.shape, jnp.float32), (mixed.shape, jnp.bfloat16)],
        after,
    )


def hidden_back_kernel(at_ref, cot_ref, down_ref, *refs):
    refs[-1][...] = dot(cot_ref[...], down_ref[...], CONTRACT_COLS).astype(jnp.bfloat16)


def hidden_back(at, cotangent, down, after=()):
    outs = [((cotangent.shape[0], down.shape[0]), jnp.bfloat16)]
    return local_call(
        hidden_back_kernel, "hidden_back", at, [cotangent, down], outs, after
    )[0]


def split_halves(bit, rows, top, bottom, keep_ref, send_ref):
    shape = (keep_ref.shape[0], -1, keep_ref.shape[2])
    top = top.astype(jnp.bfloat16).reshape(shape)
    bottom = bottom.astype(jnp.bfloat16).reshape(shape)
    keep_ref[:, rows, :] = jnp.where(bit == 0, top, bottom)
    send_ref[:, rows, :] = jnp.where(bit == 0, bottom, top)


def give_halves(upper_ref, lower_ref, value):
    value = value.astype(jnp.bfloat16)
    upper_ref[...], lower_ref[...] = value[:HALF_ROWS], value[HALF_ROWS:]


def take_halves(upper_ref, lower_ref):
    return jnp.concatenate([upper_ref[...], lower_ref[...]], axis=0)


def mlp_kernel(
    slots, at_ref, second_own_ref, second_other_ref, cot_own_ref, cot_other_ref, back_own_ref,
    back_other_ref, up_ref, *refs,
):
    stacks = refs[-5 - 2 * len(slots) : -5]
    hidden_ref, own_ref, upper_ref, lower_ref, grad_pre_ref = refs[-5:]
    bf16 = jnp.bfloat16
    chunks = hidden_ref.shape[2] // CHUNK
    sides = ((second_own_ref, cot_own_ref), (second_other_ref, cot_other_ref))
    backs = (back_own_ref, back_other_ref)
    unit = TILE // stacks[0].shape[0]
    homes = []
    for index in range(len(slots)):
        keep_ref, send_ref = stacks[2 * index : 2 * index + 2]
        for place in range(keep_ref.shape[1] // unit):
            homes.append((slots[index], pl.ds(place * unit, unit), keep_ref, send_ref))

    def make(chunk):
        lanes = pl.ds(chunk * CHUNK, CHUNK)
        for side, (second_ref, _) in enumerate(sides):
            pre = dot(second_ref[...], up_ref[:, lanes])
            cdf = 0.5 * (1.0 + lax.erf(pre * SQRT_HALF))
            hidden_ref[side, :, lanes] = (pre * cdf).astype(bf16)
            slope = cdf + pre * jnp.exp(-0.5 * pre * pre) * INV_ROOT_TWO_PI
            grad_hidden = backs[side][:, lanes].astype(jnp.float32)
            grad_pre_ref[side, :, lanes] = (grad_hidden * slope).astype(bf16)

    def give(chunk):
        lanes = pl.ds(chunk * CHUNK, CHUNK)
        grad_up, grad_down = 0.0, 0.0
        for side, (second_ref, cot_ref) in enumerate(sides):
            grad_up = grad_up + dot(grad_pre_ref[side, :, lanes], second_ref[...], CONTRACT_ROWS)
            grad_down = grad_down + dot(hidden_ref[side, :, lanes], cot_ref[...], CONTRACT_ROWS)
        for part in range(CHUNK // TILE):
            slot, place, *home = homes[chunk * (CHUNK // TILE) + part]
            rows = slice(part * TILE, (part + 1) * TILE)
            split_halves(at_ref[slot], place, grad_up[rows], grad_down[rows], *home)

    make(0)
    for chunk in range(1, chunks):
        make(chunk)
        give(chunk - 1)
    give(chunks - 1)
    give_halves(upper_ref, lower_ref, dot(grad_pre_ref[1], up_ref[...], CONTRACT_COLS))
    own_ref[...] = dot(grad_pre_ref[0], up_ref[...], CONTRACT_COLS)


def mlp(at, slots, second_own, second_other, cot_own, cot_other, back_own, back_other, up,
        after=()):
    rows, width = second_own.shape
    hidden = up.shape[1]
    blocks = 2 ** (SPLITS - 1)
    unit = TILE // blocks
    stacks = []
    for count in MLP_UNITS:
        stacks += [((blocks, count * unit, width), jnp.bfloat16)] * 2
    half = ((HALF_ROWS, width), jnp.bfloat16)
    return local_call(
        functools.partial(mlp_kernel, slots),
        "mlp",
        at,
        [second_own, second_other, cot_own, cot_other, back_own, back_other, up],
        stacks
        + [((2, rows, hidden), jnp.bfloat16), ((rows, width), jnp.float32), half, half],
        after,
        [pltpu.VMEM((2, rows, hidden), jnp.bfloat16)],
    )


def rows_kernel(at_ref, rows_ref, weight_ref, *refs):
    own_ref, upper_ref, lower_ref = refs[-3:]
    give_halves(upper_ref, lower_ref, dot(rows_ref[1], weight_ref[...]))
    own_ref[...] = dot(rows_ref[0], weight_ref[...])


def rows_times(at, rows, weight, after=()):
    shape = (rows.shape[1], weight.shape[1])
    half = ((HALF_ROWS, weight.shape[1]), jnp.bfloat16)
    return local_call(
        rows_kernel, "block", at, [rows, weight], [(shape, jnp.float32), half, half], after
    )


def norm_back_kernel(
    at_ref, own_ref, up_other_ref, low_other_ref, middle_ref, cot_ref, gain_ref, *refs
):
    grad_ref, upper_ref, lower_ref, gain_grad_ref = refs[-4:]
    grad_second = own_ref[...] + take_halves(up_other_ref, low_other_ref).astype(jnp.float32)
    normed, inv_scale = normalize(middle_ref[...])
    grad = cot_ref[...].astype(jnp.float32) + norm_back(
        grad_second, gain_ref[...], normed, inv_scale
    )
    grad_ref[...] = grad
    give_halves(upper_ref, lower_ref, grad)
    gain_grad_ref[...] = jnp.sum(grad_second * normed, axis=0, keepdims=True)


def norm_back_rows(at, own, other, middle, cotangent, gain, after=()):
    shape = own.shape
    half = ((HALF_ROWS, shape[1]), jnp.bfloat16)
    return local_call(
        norm_back_kernel,
        "norm_back_rows",
        at,
        [own, *other, middle, cotangent, gain],
        [(shape, jnp.float32), half, half, ((1, shape[1]), jnp.float32)],
        after,
    )


def attend_back_kernel(
    slot, pair, place, at_ref, qkv_ref, att_ref, lse_ref, up_own_ref, low_own_ref, up_other_ref,
    low_other_ref, out_weight_ref, first_own_ref, first_other_ref, *refs,
):
    keep_ref, send_ref, grad_rows_ref = refs[-3:]
    rows = first_own_ref.shape[0]
    tiles = rows // TILE
    first = at_ref[0]
    plain = HEAD_DIM ** (-0.5)
    scale = plain * LOG2E
    places = (first, 1 - first)
    later = jnp.concatenate([future_mask()] * 2, axis=1)
    bf16 = jnp.bfloat16
    sides = (take_halves(up_own_ref, low_own_ref), take_halves(up_other_ref, low_other_ref))
    firsts = (first_own_ref, first_other_ref)
    unit = 4 * PAIR // (2 * keep_ref.shape[0])
    is_own = [places[half] == 0 for half in range(2)]
    chunks = [(half, tile) for half in range(2) for tile in range(tiles)]

    def plus(old, term):
        return term if old is None else old + term

    lanes = pl.ds(pair * PAIR, PAIR)
    outer = [
        dot(rows_here, out_weight_ref[lanes, :], CONTRACT_COLS).astype(bf16)
        for rows_here in sides
    ]
    grads = [jnp.where(is_own[half], outer[0], outer[1]) for half in range(2)]
    queries, keys, values = [
        [qkv_ref[c, places[half], :, lanes] for half in range(2)] for c in range(3)
    ]
    keys_t = [part.T for part in keys]
    deltas = []
    for half in range(2):
        attended = att_ref[places[half], :, lanes].astype(jnp.float32)
        product = (grads[half].astype(jnp.float32) * attended).T
        deltas.append([
            jnp.sum(product[head * HEAD_DIM : (head + 1) * HEAD_DIM], axis=0, keepdims=True)
            for head in range(2)
        ])
    key_grads = {}
    value_grads = {}
    query_grads = []
    for half, tile in chunks:
        here = slice(tile * TILE, (tile + 1) * TILE)
        asked = stacked_heads(queries[half][here])
        grad = stacked_heads(grads[half][here])
        lse = jnp.concatenate([lse_ref[pair, head, half, :, here] for head in range(2)], axis=1)
        delta = jnp.concatenate([deltas[half][head][:, here] for head in range(2)], axis=1)
        spans = []
        if half == 1:
            spans.append((0, 0, rows))
        if tile > 0:
            spans.append((half, 0, tile * TILE))
        spans.append((half, tile * TILE, TILE))
        query_grad = None
        for where, start, size in spans:
            span = slice(start, start + size)
            scores = dot(keys[where][span], asked, CONTRACT_COLS)
            probs = jnp.exp2(scores * scale - lse)
            if (where, start) == (half, tile * TILE):
                probs = jnp.where(later, 0.0, probs)
            grad_probs = dot(values[where][span], grad, CONTRACT_COLS)
            grad_scores = (probs * (grad_probs - delta)).astype(bf16)
            value_term = dot(probs.astype(bf16), grad)
            key_term = dot(grad_scores, asked)
            query_grad = plus(query_grad, dot(keys_t[where][:, span], grad_scores))
            for part in range(size // TILE):
                at_part = (where, start // TILE + part)
                cut = slice(part * TILE, (part + 1) * TILE)
                value_grads[at_part] = plus(value_grads.get(at_part), value_term[cut])
                key_grads[at_part] = plus(key_grads.get(at_part), key_term[cut])
        query_grads.append((own_heads(query_grad) * plain).astype(bf16))
    turned = []
    for half in range(2):
        at_half = [i for i, (where, _) in enumerate(chunks) if where == half]
        query_t = jnp.concatenate([query_grads[i] for i in at_half], axis=1)
        key = jnp.concatenate(
            [(key_grads[half, tile] * plain).astype(bf16) for tile in range(tiles)], axis=0
        )
        value = jnp.concatenate(
            [value_grads[half, tile].astype(bf16) for tile in range(tiles)], axis=0
        )
        turned.append([query_t, key.T, value.T, att_ref[places[half], :, lanes].T])
        for c, part in enumerate((query_t.T, key, value)):
            grad_rows_ref[c, places[half]] = part
    top, bottom = 0.0, 0.0
    for side in range(2):
        mine = [jnp.where(is_own[side], a, b) for a, b in zip(turned[0], turned[1])]
        rows_here = firsts[side][...]
        top = top + dot(jnp.concatenate(mine[:2], axis=0), rows_here)
        bottom = bottom + jnp.concatenate(
            [dot(mine[2], rows_here), dot(mine[3], sides[side])], axis=0
        )
    split_halves(at_ref[slot], pl.ds(place * unit, unit), top, bottom, keep_ref, send_ref)


def attend_back(at, slot, pair, place, count, qkv, att, lse, grad_own, grad_other, out_weight,
                first_own, first_other, old=(), after=()):
    rows, width = first_own.shape
    blocks = 2 ** (SPLITS - 1)
    unit = 4 * PAIR // (2 * blocks)
    pieces = ((blocks, count * unit, width), jnp.bfloat16)
    arrays = [qkv, att, lse, *grad_own, *grad_other, out_weight, first_own, first_other, *old]
    return local_call(
        functools.partial(attend_back_kernel, slot, pair, place),
        "attend_back",
        at,
        arrays,
        [pieces, pieces, ((3, 2, rows, PAIR), jnp.bfloat16)],
        after,
        aliases={len(arrays) - 1: 0, len(arrays): 1} if old else {},
        mebibytes=12,
    )


def first_back_kernel(count, at_ref, weight_ref, *refs):
    own_ref, upper_ref, lower_ref = refs[-3:]
    pieces = []
    for index, ref in enumerate(refs[:count]):
        lanes = slice(index * PAIR, (index + 1) * PAIR)
        pieces += [(ref, c, lanes) for c in range(3)]
    weight = jnp.concatenate([weight_ref[c, :, lanes] for _, c, lanes in pieces], axis=1)
    own, other = [
        jnp.concatenate([ref[c, side] for ref, c, _ in pieces], axis=1) for side in range(2)
    ]
    give_halves(upper_ref, lower_ref, dot(other, weight, CONTRACT_COLS))
    own_ref[...] = dot(own, weight, CONTRACT_COLS)


def first_back(at, weight, groups, after=()):
    shape = (groups[0].shape[2], weight.shape[1])
    half = ((HALF_ROWS, weight.shape[1]), jnp.bfloat16)
    return local_call(
        functools.partial(first_back_kernel, len(groups)), "first_back", at, [weight, *groups],
        [(shape, jnp.float32), half, half], after,
    )


def fold_kernel(slot, at_ref, kept_ref, came_ref, *refs):
    keep_ref, send_ref = refs[-2:]
    half = keep_ref.shape[0]
    bit = at_ref[slot]
    for target, start in ((send_ref, (1 - bit) * half), (keep_ref, bit * half)):
        for index in range(half):
            total = kept_ref[start + index].astype(jnp.float32) + came_ref[
                start + index
            ].astype(jnp.float32)
            target[index] = total.astype(jnp.bfloat16)


def add_kernel(at_ref, kept_ref, came_ref, *refs):
    total = kept_ref[...].astype(jnp.float32) + came_ref[...].astype(jnp.float32)
    refs[-1][...] = total.astype(jnp.bfloat16)


def widen(pair):
    half = pair.shape[0] // 2
    pair = pair.astype(jnp.float32)
    return pair[:half] + pair[half:]


def narrow(value):
    high = value.astype(jnp.bfloat16)
    low = (value - high.astype(jnp.float32)).astype(jnp.bfloat16)
    return jnp.concatenate([high, low], axis=0)


def add_small_kernel(at_ref, kept_ref, came_ref, mine_ref, other_ref, *refs):
    total = kept_ref[0].astype(jnp.float32) + came_ref[0].astype(jnp.float32)
    refs[-1][0] = total.astype(jnp.bfloat16)
    refs[-1][1] = narrow(mine_ref[...] + other_ref[...])


def again_kernel(at_ref, mine_ref, came_ref, *refs):
    total = mine_ref[0].astype(jnp.float32) + came_ref[0].astype(jnp.float32)
    refs[-1][0] = total.astype(jnp.bfloat16)
    if mine_ref.shape[0] > 1:
        refs[-1][1] = narrow(widen(mine_ref[1]) + widen(came_ref[1]))


def join_kernel(slot, at_ref, mine_ref, came_ref, *refs):
    both_ref = refs[-1]
    half = both_ref.shape[0] // 2
    bit = at_ref[slot]
    for source, start in ((mine_ref, bit * half), (came_ref, (1 - bit) * half)):
        for index in range(half):
            both_ref[start + index] = source[index]
    if both_ref.shape[0] > 2 * half:
        both_ref[2 * half] = narrow(widen(mine_ref[half]) + widen(came_ref[half]))


def fold(at, slot, kept, came, after=()):
    blocks, rows, width = kept.shape
    outs = [((blocks // 2, rows, width), jnp.bfloat16)] * 2
    return local_call(
        functools.partial(fold_kernel, slot), "fold", at, [kept, came], outs, after
    )


def last_fold(at, kept, came, small, after=()):
    blocks, rows, width = kept.shape
    kernel = add_small_kernel if small else add_kernel
    outs = [((blocks + (1 if small else 0), rows, width), jnp.bfloat16)]
    return local_call(kernel, "add", at, [kept, came, *small], outs, after)[0]


def again(at, mine, came, after=()):
    outs = [(mine.shape, jnp.bfloat16)]
    return local_call(again_kernel, "again", at, [mine, came], outs, after)[0]


def join(at, slot, mine, came, blocks, after=()):
    _, rows, width = mine.shape
    extra = mine.shape[0] - blocks
    outs = [((2 * blocks + extra, rows, width), jnp.bfloat16)]
    return local_call(
        functools.partial(join_kernel, slot), "join", at, [mine, came], outs, after
    )[0]


def ordered_units(bit, mine_ref, came_ref, blocks, unit):
    width = mine_ref.shape[2]
    for index in range(mine_ref.shape[1] // unit):
        rows = slice(index * unit, (index + 1) * unit)
        mine = mine_ref[:blocks, rows, :].reshape(blocks * unit, width)
        came = came_ref[:blocks, rows, :].reshape(blocks * unit, width)
        yield index, jnp.where(bit == 0, mine, came), jnp.where(bit == 0, came, mine)


def finish_mlp_kernel(slot, start, blocks, at_ref, mine_ref, came_ref, *refs):
    up_ref, down_ref, token_ref, turned_ref, held_ref, up_sems, down_sems = refs[-7:]
    token_ref[...] = jnp.zeros_like(token_ref)
    copies = []
    for index, top, bottom in ordered_units(
        at_ref[slot], mine_ref, came_ref, blocks, TILE // blocks
    ):
        place = pl.ds((start + index) * TILE, TILE)
        held_ref[index] = bottom.astype(jnp.float32)
        copies.append(
            pltpu.make_async_copy(held_ref.at[index], down_ref.at[place, :], down_sems.at[index])
        )
        copies[-1].start()
        turned_ref[index] = top.T.astype(jnp.float32)
        copies.append(
            pltpu.make_async_copy(turned_ref.at[index], up_ref.at[:, place], up_sems.at[index])
        )
        copies[-1].start()
    for copy in copies:
        copy.wait()


def finish_attend_kernel(slot, start, blocks, at_ref, mine_ref, came_ref, *refs):
    qkv_ref, out_ref, token_ref, turned_ref, held_ref, qkv_sems, out_sems = refs[-7:]
    token_ref[...] = jnp.zeros_like(token_ref)
    if mine_ref.shape[0] > blocks:
        token_ref[...] = widen(mine_ref[blocks]) + widen(came_ref[blocks])
    copies = []
    for index, top, bottom in ordered_units(
        at_ref[slot], mine_ref, came_ref, blocks, 2 * PAIR // blocks
    ):
        place = pl.ds((start + index) * PAIR, PAIR)
        held_ref[index] = bottom[PAIR:].astype(jnp.float32)
        copies.append(
            pltpu.make_async_copy(held_ref.at[index], out_ref.at[place, :], out_sems.at[index])
        )
        copies[-1].start()
        for c, part in enumerate((top[:PAIR], top[PAIR:], bottom[:PAIR])):
            turned_ref[index, c] = part.T.astype(jnp.float32)
        copies.append(
            pltpu.make_async_copy(
                turned_ref.at[index], qkv_ref.at[:, :, place], qkv_sems.at[index]
            )
        )
        copies[-1].start()
    for copy in copies:
        copy.wait()


def finish(kernel, name, at, slot, start, mine, came, shapes, scratch, old=None, after=()):
    in_vmem = pl.BlockSpec(memory_space=pltpu.VMEM)
    in_hbm = pl.BlockSpec(memory_space=pltpu.HBM)
    blocks = 2 ** (SPLITS - 1)
    units = mine.shape[1] * blocks // TILE
    return pl.pallas_call(
        functools.partial(kernel, slot, start, blocks),
        in_specs=[pl.BlockSpec(memory_space=pltpu.SMEM), in_vmem, in_vmem]
        + [in_hbm] * len(old or [])
        + [pl.BlockSpec(memory_space=pl.ANY)] * len(after),
        out_specs=[in_hbm, in_hbm, in_vmem],
        out_shape=[jax.ShapeDtypeStruct(shape, jnp.float32) for shape in shapes]
        + [jax.ShapeDtypeStruct((SMALL_ROWS, mine.shape[2]), jnp.float32)],
        scratch_shapes=[pltpu.VMEM((units, *shape), jnp.float32) for shape in scratch]
        + [pltpu.SemaphoreType.DMA((units,))] * 2,
        input_output_aliases={3: 0, 4: 1} if old else {},
        compiler_params=params(12),
        cost_estimate=cost(1000, 1000),
        name=name,
    )(at, mine, came, *(old or []), *after)


def finish_mlp(at, slot, start, mine, came, width, hidden, old=None, after=()):
    shapes = [(width, hidden), (hidden, width)]
    scratch = [(width, TILE), (TILE, width)]
    return finish(
        finish_mlp_kernel, "finish_mlp", at, slot, start, mine, came, shapes, scratch, old, after
    )


def finish_attend(at, slot, start, mine, came, width, local, old=None, after=()):
    shapes = [(3, width, local), (local, width)]
    scratch = [(3, width, PAIR), (PAIR, width)]
    return finish(
        finish_attend_kernel, "finish_attend", at, slot, start, mine, came, shapes, scratch, old,
        after,
    )


def mp_swap(rows):
    return lax.ppermute(rows, "mp", [(0, 1), (1, 0)])


def dp_bits():
    return lax.axis_size("dp").bit_length() - 1


def bit_swap(rows, bits):
    size, cores = lax.axis_size("dp"), lax.axis_size("mp")
    pairs = [
        (i * cores + core, (i ^ (1 << bits[core])) * cores + core)
        for i in range(size)
        for core in range(cores)
    ]
    return lax.ppermute(rows, ("dp", "mp"), pairs)


def step_bits(kind, step):
    return [order[step] for order in KINDS[kind]]


def slot_of(kind, step):
    return 1 + kind * SPLITS + step


def where_am_i():
    core, index = lax.axis_index("mp"), lax.axis_index("dp")
    values = [core]
    for kind in range(len(KINDS)):
        for step in range(SPLITS):
            bits = step_bits(kind, step)
            values.append((index >> jnp.where(core == 0, bits[0], bits[1])) & 1)
    return jnp.stack(values).astype(jnp.int32)


class Stream:
    def __init__(self, at, kind, kept, sent, small=None):
        self.at, self.kind, self.kept, self.step, self.small = at, kind, kept, 0, small
        self.extra = dp_bits() - SPLITS
        self.came = bit_swap(sent, step_bits(kind, 0))

    def advance(self, after=()):
        step, kind, at = self.step, self.kind, self.at
        self.step += 1
        joined = step - SPLITS - self.extra
        if step < SPLITS - 1:
            self.kept, sent = fold(at, slot_of(kind, step + 1), self.kept, self.came, after)
            self.came = bit_swap(sent, step_bits(kind, step + 1))
            return self.kept
        if step == SPLITS - 1:
            small = self.small() if self.small else ()
            self.kept = last_fold(at, self.kept, self.came, small, after)
        elif joined < 0:
            self.kept = again(at, self.kept, self.came, after)
        else:
            slot = slot_of(kind, SPLITS - 1 - joined)
            self.kept = join(at, slot, self.kept, self.came, 2**joined, after)
        if joined < -1:
            bit = SPLITS + joined + 1 + self.extra
            self.came = bit_swap(self.kept, [bit, bit])
        else:
            self.came = bit_swap(self.kept, step_bits(kind, SPLITS - 2 - joined))
        return self.kept


def shards(
    history,
    depth_weights,
    gain_attn,
    gain_mlp,
    qkv_weight,
    out_weight,
    up_weight,
    down_weight,
    cotangent,
):
    width = cotangent.shape[1]
    local = out_weight.shape[0]
    hidden = down_weight.shape[0]
    pairs = local // PAIR
    at = where_am_i()

    cot_other = mp_swap(cotangent)
    mixed, first = mix(depth_weights, history, gain_attn)
    first_other = mp_swap(first)
    back_own = hidden_back(at, cotangent, down_weight)
    qkv, att, lse, out_own, out_other = attend(
        at, first, first_other, qkv_weight, out_weight, [back_own]
    )
    middle, second = renorm(at, mixed, out_own, mp_swap(out_other), gain_mlp)
    back_other = hidden_back(at, cot_other, down_weight, [second])
    second_other = mp_swap(second)
    mlp_names = [name for name in KIND if name[0] == "M"]
    *stacks, hidden_rows, grad_own, grad_upper, grad_lower = mlp(
        at, tuple(slot_of(KIND[name], 0) for name in mlp_names), second, second_other, cotangent,
        cot_other, back_own, back_other, up_weight,
    )
    streams = {
        name: Stream(at, KIND[name], *stacks[2 * i : 2 * i + 2])
        for i, name in enumerate(mlp_names)
    }
    grad_came = [mp_swap(part) for part in (grad_upper, grad_lower)]
    made = {}

    def back_norm(after):
        made["middle"], *made["narrow"], made["gain"] = norm_back_rows(
            at, grad_own, grad_came, middle, cotangent, gain_mlp, after
        )
        made["narrow_came"] = [mp_swap(part) for part in made["narrow"]]
        return made["gain"]

    def back_pair(pair, after):
        late = pair == pairs - 1
        name, place = ("Ab", 0) if late else ("Aa", pair)
        old = () if late or pair == 0 else made["stack"]
        kept, sent, made[pair] = attend_back(
            at, slot_of(KIND[name], 0), pair, place, 1 if late else pairs - 1, qkv, att, lse,
            made["narrow"], made["narrow_came"], out_weight, first, first_other, old, after,
        )
        made["stack"] = (kept, sent)
        if pair >= pairs - 2:
            small = (lambda: (made["small"], made["small_came"])) if late else None
            streams[name] = Stream(at, KIND[name], kept, sent, small)
        return made[pair]

    def back_first(after):
        groups = [made[pair] for pair in range(pairs)]
        made["own"], *other = first_back(at, qkv_weight, groups, after)
        made["came"] = [mp_swap(part) for part in other]
        return made["own"]

    def back_start(after):
        made["mixed"], made["small"] = unmix(
            depth_weights, history, gain_attn, mixed, made["middle"], made["own"], made["came"],
            made["gain"], after,
        )
        made["small_came"] = mp_swap(made["small"])
        return made["small"]

    def give_outputs(after):
        made["history"], made["out"], token = outputs(
            depth_weights, made["mixed"], middle, made["block"], made["block_came"], after
        )
        return token

    def block_rows(after):
        made["block"], *other = rows_times(at, hidden_rows, down_weight, after)
        made["block_came"] = [mp_swap(part) for part in other]
        return made["block"]

    def end_mlp(name, start, after):
        stream = streams[name]
        *made["mlp"], token = finish_mlp(
            at, slot_of(KIND[name], 0), start, stream.kept, stream.came, width, hidden,
            made.get("mlp"), after,
        )
        return token

    def end_attend(name, start, after):
        stream = streams[name]
        *made["attend"], made[name] = finish_attend(
            at, slot_of(KIND[name], 0), start, stream.kept, stream.came, width, local,
            made.get("attend"), after,
        )
        return made[name]

    units = {
        "nb": back_norm,
        "fb": back_first,
        "um": back_start,
        "um2": give_outputs,
        "blk": block_rows,
        "fAa": functools.partial(end_attend, "Aa", 0),
        "fAb": functools.partial(end_attend, "Ab", pairs - 1),
    }
    start = 0
    for name, count in zip(mlp_names, MLP_UNITS):
        units["f" + name] = functools.partial(end_mlp, name, start)
        start += count
    for pair in range(pairs):
        units["ab" + str(pair)] = functools.partial(back_pair, pair)
    last = hidden_rows
    for name in ORDER:
        if name in streams:
            if streams[name].step == SPLITS:
                for _ in range(streams[name].extra - 1):
                    last = streams[name].advance([last])
            last = streams[name].advance([last])
        else:
            last = units[name]([last])
    small = made["Ab"]
    grad_depth = jnp.sum(small[8 : 8 + history.shape[0]], axis=1)
    block_out, grad_history = made["out"], made["history"]
    gain_grad_attn, gain_grad_mlp = small[0], small[1]
    (grad_up, grad_down), (grad_qkv, grad_out) = made["mlp"], made["attend"]
    return (
        block_out,
        grad_history,
        grad_depth,
        gain_grad_attn,
        gain_grad_mlp,
        grad_qkv,
        grad_out,
        grad_up,
        grad_down,
    )


def solution(mesh):
    in_specs = (
        P(None, ("dp", "mp"), None),
        P(),
        P(),
        P(),
        P(None, None, "mp"),
        P("mp", None),
        P(None, "mp"),
        P("mp", None),
        P(("dp", "mp"), None),
    )
    out_specs = (
        P(("dp", "mp"), None),
        P(None, ("dp", "mp"), None),
        P(),
        P(),
        P(),
        P(None, None, "mp"),
        P("mp", None),
        P(None, "mp"),
        P("mp", None),
    )
    return jax.shard_map(shards, mesh=mesh, in_specs=in_specs, out_specs=out_specs, check_vma=False)
```

```python
import functools

import jax
import jax.numpy as jnp
from jax import lax
from jax.experimental import pallas as pl
from jax.experimental.pallas import tpu as pltpu
from jax.sharding import PartitionSpec as P

HEAD_DIM = 64
EPSILON = 1e-05
SQRT_HALF = 0.7071067811865476
INV_ROOT_TWO_PI = 0.3989422804014327
LOG2E = 1.4426950408889634
NEG = -1e30
TILE = 256
ROW_BLOCK = 64
HALF_ROWS = 256
MIX_BLOCK = 128
SMALL_ROWS = 32
SPLITS = 3
PAIR = 2 * HEAD_DIM
CHUNK = 256
ORDER = (
    "nb", "ab0", "ab1", "Mb", "Ma", "Mc", "ab2", "fb", "Mb", "Ma", "Aa", "Mb", "Mc", "Ma",
    "Aa", "Mb", "Ab", "Mc", "um", "Ma", "Aa", "Mb", "Ab", "Mc", "Ma", "blk", "Aa", "Ab", "Mc",
    "Mb", "Ma", "Mc", "Ab", "Aa", "um2", "Aa", "Ab", "fMb", "fMa", "Ab", "fMc", "fAa", "fAb",
)
KINDS = (
    ((0, 1, 2), (1, 2, 0)),
    ((0, 1, 2), (2, 0, 1)),
    ((2, 1, 0), (1, 0, 2)),
    ((0, 2, 1), (2, 1, 0)),
    ((0, 1, 2), (1, 0, 2)),
)
KIND = {"Ma": 0, "Mb": 1, "Mc": 2, "Aa": 3, "Ab": 4}
MLP_UNITS = (2, 2, 2)

PLAIN = (((1,), (0,)), ((), ()))
CONTRACT_COLS = (((1,), (1,)), ((), ()))
CONTRACT_ROWS = (((0,), (0,)), ((), ()))


def dot(lhs, rhs, dims=PLAIN):
    return lax.dot_general(lhs, rhs, dims, preferred_element_type=jnp.float32)


def cost(flops, moved, exps=0):
    return pl.CostEstimate(flops=flops, bytes_accessed=moved, transcendentals=exps)


def params(mebibytes=8):
    return pltpu.CompilerParams(vmem_limit_bytes=mebibytes * 2**20)


def normalize(inputs):
    row_mean = jnp.mean(inputs, axis=-1, keepdims=True)
    centered = inputs - row_mean
    variance = jnp.mean(centered * centered, axis=-1, keepdims=True)
    inv_scale = lax.rsqrt(variance + EPSILON)
    return centered * inv_scale, inv_scale


def norm_back(grad_rows, gain_row, normed, inv_scale):
    scaled = grad_rows * gain_row
    first_mean = jnp.mean(scaled, axis=-1, keepdims=True)
    second_mean = jnp.mean(scaled * normed, axis=-1, keepdims=True)
    return inv_scale * (scaled - first_mean - normed * second_mean)


def gelu_value(inputs):
    return 0.5 * inputs * (1.0 + lax.erf(inputs * SQRT_HALF))


def gelu_slope(inputs):
    normal_cdf = 0.5 * (1.0 + lax.erf(inputs * SQRT_HALF))
    return normal_cdf + inputs * jnp.exp(-0.5 * inputs * inputs) * INV_ROOT_TWO_PI


def layer_copies(history_ref, held_ref, sems, out=False):
    copies = []
    for index in range(held_ref.shape[0]):
        rows = pl.ds(index * ROW_BLOCK, ROW_BLOCK)
        ends = (history_ref.at[:, rows, :], held_ref.at[index])
        copies.append(
            pltpu.make_async_copy(ends[out], ends[not out], sems.at[index])
        )
    return copies


def mix_kernel(weights_ref, gain_ref, history_ref, mixed_ref, first_ref):
    mixed = weights_ref[0] * history_ref[0].astype(jnp.float32)
    for layer in range(1, history_ref.shape[0]):
        mixed = mixed + weights_ref[layer] * history_ref[layer].astype(jnp.float32)
    mixed_ref[...] = mixed
    normed, _ = normalize(mixed)
    first_ref[...] = (normed * gain_ref[...]).astype(jnp.bfloat16)


def mix(weights, history, gain):
    layers, rows, width = history.shape
    row_spec = pl.BlockSpec((MIX_BLOCK, width), lambda i: (i, 0))
    return pl.pallas_call(
        mix_kernel,
        grid=(rows // MIX_BLOCK,),
        in_specs=[
            pl.BlockSpec(memory_space=pltpu.SMEM),
            pl.BlockSpec((width,), lambda i: (0,)),
            pl.BlockSpec((layers, MIX_BLOCK, width), lambda i: (0, i, 0)),
        ],
        out_specs=[row_spec, row_spec],
        out_shape=[
            jax.ShapeDtypeStruct((rows, width), jnp.float32),
            jax.ShapeDtypeStruct((rows, width), jnp.bfloat16),
        ],
        compiler_params=params(57),
        cost_estimate=cost(1000, 1000),
        name="mix",
    )(weights, gain, history)


def unmix_kernel(
    weights_ref, gain_ref, mixed_ref, middle_ref, own_ref, upper_ref, lower_ref, gain_mlp_ref,
    history_ref, *refs,
):
    grad_ref, small_ref = refs[-2:]
    small_ref[...] = jnp.zeros_like(small_ref)
    small_ref[1:2] = gain_mlp_ref[...]
    for index in range(grad_ref.shape[0] // ROW_BLOCK):
        rows = pl.ds(index * ROW_BLOCK, ROW_BLOCK)
        start = index * ROW_BLOCK
        part, start = (upper_ref, start) if start < HALF_ROWS else (lower_ref, start - HALF_ROWS)
        other = part[start : start + ROW_BLOCK, :].astype(jnp.float32)
        grad_first = own_ref[rows, :] + other
        normed, inv_scale = normalize(mixed_ref[rows, :])
        grad_mixed = middle_ref[rows, :] + norm_back(
            grad_first, gain_ref[...], normed, inv_scale
        )
        grad_ref[rows, :] = grad_mixed
        small_ref[0:1] += jnp.sum(grad_first * normed, axis=0, keepdims=True)
        for layer in range(history_ref.shape[0]):
            product = history_ref[layer, rows, :].astype(jnp.float32) * grad_mixed
            small_ref[8 + layer : 9 + layer] += jnp.sum(product, axis=0, keepdims=True)


def unmix(weights, history, gain, mixed, grad_middle, own, other, gain_grad_mlp, after=()):
    _, rows, width = history.shape
    in_vmem = pl.BlockSpec(memory_space=pltpu.VMEM)
    return pl.pallas_call(
        unmix_kernel,
        in_specs=[pl.BlockSpec(memory_space=pltpu.SMEM)]
        + [in_vmem] * 8
        + [pl.BlockSpec(memory_space=pl.ANY)] * len(after),
        out_specs=[in_vmem, in_vmem],
        out_shape=[
            jax.ShapeDtypeStruct((rows, width), jnp.float32),
            jax.ShapeDtypeStruct((SMALL_ROWS, width), jnp.float32),
        ],
        compiler_params=params(),
        cost_estimate=cost(1000, 1000),
        name="unmix",
    )(weights, gain, mixed, grad_middle, own, *other, gain_grad_mlp, history, *after)


def outputs_kernel(
    weights_ref, grad_ref, rows_ref, block_own_ref, upper_ref, lower_ref, *refs
):
    grads_ref, out_ref, token_ref, given_ref, made_ref, sems, made_sem = refs[-7:]
    token_ref[...] = jnp.zeros_like(token_ref)
    gives = layer_copies(grads_ref, given_ref, sems, True)
    other = jnp.concatenate([upper_ref[...], lower_ref[...]], axis=0).astype(jnp.float32)
    made_ref[...] = (rows_ref[...] + block_own_ref[...] + other).astype(jnp.bfloat16)
    make = pltpu.make_async_copy(made_ref, out_ref, made_sem)
    make.start()
    for index, give in enumerate(gives):
        grad_mixed = grad_ref[pl.ds(index * ROW_BLOCK, ROW_BLOCK), :]
        for layer in range(given_ref.shape[1]):
            given_ref[index, layer] = (weights_ref[layer] * grad_mixed).astype(jnp.bfloat16)
        give.start()
    make.wait()
    for give in gives:
        give.wait()


def outputs(weights, grad_mixed, rows, block_own, block_other, after=()):
    layers = weights.shape[0]
    count, width = grad_mixed.shape
    in_vmem = pl.BlockSpec(memory_space=pltpu.VMEM)
    in_hbm = pl.BlockSpec(memory_space=pltpu.HBM)
    blocks = count // ROW_BLOCK
    return pl.pallas_call(
        outputs_kernel,
        in_specs=[pl.BlockSpec(memory_space=pltpu.SMEM)]
        + [in_vmem] * 5
        + [pl.BlockSpec(memory_space=pl.ANY)] * len(after),
        out_specs=[in_hbm, in_hbm, in_vmem],
        out_shape=[
            jax.ShapeDtypeStruct((layers, count, width), jnp.bfloat16),
            jax.ShapeDtypeStruct((count, width), jnp.bfloat16),
            jax.ShapeDtypeStruct((8, 128), jnp.float32),
        ],
        scratch_shapes=[
            pltpu.VMEM((blocks, layers, ROW_BLOCK, width), jnp.bfloat16),
            pltpu.VMEM((count, width), jnp.bfloat16),
            pltpu.SemaphoreType.DMA((blocks,)),
            pltpu.SemaphoreType.DMA,
        ],
        compiler_params=params(10),
        cost_estimate=cost(1000, 1000),
        name="outputs",
    )(weights, grad_mixed, rows, block_own, *block_other, *after)


def head_mask(head):
    lanes = lax.broadcasted_iota(jnp.int32, (1, PAIR), 1)
    return (lanes // HEAD_DIM) == head


def future_mask():
    keys = lax.broadcasted_iota(jnp.int32, (TILE, TILE), 0)
    asks = lax.broadcasted_iota(jnp.int32, (TILE, TILE), 1)
    return keys > asks


def stacked_heads(rows):
    zero = jnp.zeros_like(rows)
    return jnp.concatenate([jnp.where(head_mask(head), rows, zero) for head in range(2)], axis=0)


def own_heads(columns):
    half = columns.shape[1] // 2
    return jnp.concatenate([columns[:HEAD_DIM, :half], columns[HEAD_DIM:, half:]], axis=0)


def local_call(kernel, name, at, arrays, outs, after=(), scratch=(), aliases=None,
               mebibytes=8):
    in_vmem = pl.BlockSpec(memory_space=pltpu.VMEM)
    return pl.pallas_call(
        kernel,
        in_specs=[pl.BlockSpec(memory_space=pltpu.SMEM)]
        + [in_vmem] * len(arrays)
        + [pl.BlockSpec(memory_space=pl.ANY)] * len(after),
        out_specs=[in_vmem] * len(outs),
        out_shape=[jax.ShapeDtypeStruct(shape, dtype) for shape, dtype in outs],
        scratch_shapes=list(scratch),
        input_output_aliases=aliases or {},
        compiler_params=params(mebibytes),
        cost_estimate=cost(1000, 1000),
        name=name,
    )(at, *arrays, *after)


def attend_kernel(
    at_ref, own_ref, other_ref, weight_ref, out_weight_ref, *refs,
):
    qkv_ref, att_ref, lse_ref, out_own_ref, out_other_ref = refs[-5:]
    rows = own_ref.shape[0]
    tiles = rows // TILE
    first = at_ref[0]
    scale = HEAD_DIM ** (-0.5) * LOG2E
    places = (first, 1 - first)
    later = jnp.concatenate([future_mask()] * 2, axis=1)

    def one_pair(pair, carry):
        lanes = pl.ds(pl.multiple_of(pair * PAIR, PAIR), PAIR)
        weight = jnp.concatenate([weight_ref[c, :, lanes] for c in range(3)], axis=1)
        for side, ref in enumerate((own_ref, other_ref)):
            made = dot(ref[...], weight).astype(jnp.bfloat16)
            for c in range(3):
                qkv_ref[c, side, :, lanes] = made[:, c * PAIR : (c + 1) * PAIR]
        half_keys = [qkv_ref[1, places[half], :, lanes] for half in range(2)]
        half_values = [qkv_ref[2, places[half], :, lanes].T for half in range(2)]
        for half in range(2):
            for tile in range(tiles):
                at_rows = pl.ds(tile * TILE, TILE)
                queries = qkv_ref[0, places[half], at_rows, lanes]
                asked = stacked_heads(queries)
                spans = []
                if half == 1:
                    spans.append((0, 0, rows))
                if tile > 0:
                    spans.append((half, 0, tile * TILE))
                spans.append((half, tile * TILE, TILE))
                scores = [
                    dot(half_keys[where][start : start + size], asked, CONTRACT_COLS)
                    for where, start, size in spans
                ]
                scores[-1] = jnp.where(later, NEG, scores[-1])
                top = functools.reduce(
                    jnp.maximum, [jnp.max(part, axis=0, keepdims=True) for part in scores]
                )
                top = top * scale
                total = 0.0
                summed = 0.0
                for part, (where, start, size) in zip(scores, spans):
                    weights = jnp.exp2(part * scale - top)
                    total = total + jnp.sum(weights, axis=0, keepdims=True)
                    summed = summed + dot(
                        half_values[where][:, start : start + size], weights.astype(jnp.bfloat16)
                    )
                lse = top + jnp.log2(total)
                for head in range(2):
                    lse_ref[pair, head, half, :, at_rows] = lse[:, head * TILE : (head + 1) * TILE]
                joined = own_heads(summed / total).T
                att_ref[places[half], at_rows, lanes] = joined.astype(jnp.bfloat16)
        return carry

    lax.fori_loop(0, att_ref.shape[2] // PAIR, one_pair, 0)
    out_other_ref[...] = dot(att_ref[1], out_weight_ref[...]).astype(jnp.bfloat16)
    out_own_ref[...] = dot(att_ref[0], out_weight_ref[...])


def attend(at, own, other, weight, out_weight, after=()):
    rows, width = own.shape
    local = weight.shape[2]
    return local_call(
        attend_kernel,
        "attend",
        at,
        [own, other, weight, out_weight],
        [
            ((3, 2, rows, local), jnp.bfloat16),
            ((2, rows, local), jnp.bfloat16),
            ((local // PAIR, 2, 2, 1, rows), jnp.float32),
            ((rows, width), jnp.float32),
            ((rows, width), jnp.bfloat16),
        ],
        after,
        mebibytes=12,
    )


def renorm_kernel(at_ref, mixed_ref, own_ref, other_ref, gain_ref, *refs):
    middle_ref, second_ref = refs[-2:]
    middle = mixed_ref[...] + own_ref[...] + other_ref[...].astype(jnp.float32)
    middle_ref[...] = middle
    second_ref[...] = (normalize(middle)[0] * gain_ref[...]).astype(jnp.bfloat16)


def renorm(at, mixed, own, other, gain, after=()):
    return local_call(
        renorm_kernel,
        "renorm",
        at,
        [mixed, own, other, gain],
        [(mixed.shape, jnp.float32), (mixed.shape, jnp.bfloat16)],
        after,
    )


def hidden_back_kernel(at_ref, cot_ref, down_ref, *refs):
    refs[-1][...] = dot(cot_ref[...], down_ref[...], CONTRACT_COLS).astype(jnp.bfloat16)


def hidden_back(at, cotangent, down, after=()):
    outs = [((cotangent.shape[0], down.shape[0]), jnp.bfloat16)]
    return local_call(
        hidden_back_kernel, "hidden_back", at, [cotangent, down], outs, after
    )[0]


def split_halves(bit, rows, top, bottom, keep_ref, send_ref):
    shape = (keep_ref.shape[0], -1, keep_ref.shape[2])
    top = top.astype(jnp.bfloat16).reshape(shape)
    bottom = bottom.astype(jnp.bfloat16).reshape(shape)
    keep_ref[:, rows, :] = jnp.where(bit == 0, top, bottom)
    send_ref[:, rows, :] = jnp.where(bit == 0, bottom, top)


def give_halves(upper_ref, lower_ref, value):
    value = value.astype(jnp.bfloat16)
    upper_ref[...], lower_ref[...] = value[:HALF_ROWS], value[HALF_ROWS:]


def take_halves(upper_ref, lower_ref):
    return jnp.concatenate([upper_ref[...], lower_ref[...]], axis=0)


def mlp_kernel(
    slots, at_ref, second_own_ref, second_other_ref, cot_own_ref, cot_other_ref, back_own_ref,
    back_other_ref, up_ref, *refs,
):
    stacks = refs[-5 - 2 * len(slots) : -5]
    hidden_ref, own_ref, upper_ref, lower_ref, grad_pre_ref = refs[-5:]
    bf16 = jnp.bfloat16
    chunks = hidden_ref.shape[2] // CHUNK
    sides = ((second_own_ref, cot_own_ref), (second_other_ref, cot_other_ref))
    backs = (back_own_ref, back_other_ref)
    unit = TILE // stacks[0].shape[0]
    homes = []
    for index in range(len(slots)):
        keep_ref, send_ref = stacks[2 * index : 2 * index + 2]
        for place in range(keep_ref.shape[1] // unit):
            homes.append((slots[index], pl.ds(place * unit, unit), keep_ref, send_ref))

    def make(chunk):
        lanes = pl.ds(chunk * CHUNK, CHUNK)
        for side, (second_ref, _) in enumerate(sides):
            pre = dot(second_ref[...], up_ref[:, lanes])
            cdf = 0.5 * (1.0 + lax.erf(pre * SQRT_HALF))
            hidden_ref[side, :, lanes] = (pre * cdf).astype(bf16)
            slope = cdf + pre * jnp.exp(-0.5 * pre * pre) * INV_ROOT_TWO_PI
            grad_hidden = backs[side][:, lanes].astype(jnp.float32)
            grad_pre_ref[side, :, lanes] = (grad_hidden * slope).astype(bf16)

    def give(chunk):
        lanes = pl.ds(chunk * CHUNK, CHUNK)
        grad_up, grad_down = 0.0, 0.0
        for side, (second_ref, cot_ref) in enumerate(sides):
            grad_up = grad_up + dot(grad_pre_ref[side, :, lanes], second_ref[...], CONTRACT_ROWS)
            grad_down = grad_down + dot(hidden_ref[side, :, lanes], cot_ref[...], CONTRACT_ROWS)
        for part in range(CHUNK // TILE):
            slot, place, *home = homes[chunk * (CHUNK // TILE) + part]
            rows = slice(part * TILE, (part + 1) * TILE)
            split_halves(at_ref[slot], place, grad_up[rows], grad_down[rows], *home)

    make(0)
    for chunk in range(1, chunks):
        make(chunk)
        give(chunk - 1)
    give(chunks - 1)
    give_halves(upper_ref, lower_ref, dot(grad_pre_ref[1], up_ref[...], CONTRACT_COLS))
    own_ref[...] = dot(grad_pre_ref[0], up_ref[...], CONTRACT_COLS)


def mlp(at, slots, second_own, second_other, cot_own, cot_other, back_own, back_other, up,
        after=()):
    rows, width = second_own.shape
    hidden = up.shape[1]
    blocks = 2 ** (SPLITS - 1)
    unit = TILE // blocks
    stacks = []
    for count in MLP_UNITS:
        stacks += [((blocks, count * unit, width), jnp.bfloat16)] * 2
    half = ((HALF_ROWS, width), jnp.bfloat16)
    return local_call(
        functools.partial(mlp_kernel, slots),
        "mlp",
        at,
        [second_own, second_other, cot_own, cot_other, back_own, back_other, up],
        stacks
        + [((2, rows, hidden), jnp.bfloat16), ((rows, width), jnp.float32), half, half],
        after,
        [pltpu.VMEM((2, rows, hidden), jnp.bfloat16)],
    )


def rows_kernel(at_ref, rows_ref, weight_ref, *refs):
    own_ref, upper_ref, lower_ref = refs[-3:]
    give_halves(upper_ref, lower_ref, dot(rows_ref[1], weight_ref[...]))
    own_ref[...] = dot(rows_ref[0], weight_ref[...])


def rows_times(at, rows, weight, after=()):
    shape = (rows.shape[1], weight.shape[1])
    half = ((HALF_ROWS, weight.shape[1]), jnp.bfloat16)
    return local_call(
        rows_kernel, "block", at, [rows, weight], [(shape, jnp.float32), half, half], after
    )


def norm_back_kernel(
    at_ref, own_ref, up_other_ref, low_other_ref, middle_ref, cot_ref, gain_ref, *refs
):
    grad_ref, upper_ref, lower_ref, gain_grad_ref = refs[-4:]
    grad_second = own_ref[...] + take_halves(up_other_ref, low_other_ref).astype(jnp.float32)
    normed, inv_scale = normalize(middle_ref[...])
    grad = cot_ref[...].astype(jnp.float32) + norm_back(
        grad_second, gain_ref[...], normed, inv_scale
    )
    grad_ref[...] = grad
    give_halves(upper_ref, lower_ref, grad)
    gain_grad_ref[...] = jnp.sum(grad_second * normed, axis=0, keepdims=True)


def norm_back_rows(at, own, other, middle, cotangent, gain, after=()):
    shape = own.shape
    half = ((HALF_ROWS, shape[1]), jnp.bfloat16)
    return local_call(
        norm_back_kernel,
        "norm_back_rows",
        at,
        [own, *other, middle, cotangent, gain],
        [(shape, jnp.float32), half, half, ((1, shape[1]), jnp.float32)],
        after,
    )


def attend_back_kernel(
    slot, pair, place, at_ref, qkv_ref, att_ref, lse_ref, up_own_ref, low_own_ref, up_other_ref,
    low_other_ref, out_weight_ref, first_own_ref, first_other_ref, *refs,
):
    keep_ref, send_ref, grad_rows_ref = refs[-3:]
    rows = first_own_ref.shape[0]
    tiles = rows // TILE
    first = at_ref[0]
    plain = HEAD_DIM ** (-0.5)
    scale = plain * LOG2E
    places = (first, 1 - first)
    later = jnp.concatenate([future_mask()] * 2, axis=1)
    bf16 = jnp.bfloat16
    sides = (take_halves(up_own_ref, low_own_ref), take_halves(up_other_ref, low_other_ref))
    firsts = (first_own_ref, first_other_ref)
    unit = 4 * PAIR // (2 * keep_ref.shape[0])
    is_own = [places[half] == 0 for half in range(2)]
    chunks = [(half, tile) for half in range(2) for tile in range(tiles)]

    def plus(old, term):
        return term if old is None else old + term

    lanes = pl.ds(pair * PAIR, PAIR)
    outer = [
        dot(rows_here, out_weight_ref[lanes, :], CONTRACT_COLS).astype(bf16)
        for rows_here in sides
    ]
    grads = [jnp.where(is_own[half], outer[0], outer[1]) for half in range(2)]
    queries, keys, values = [
        [qkv_ref[c, places[half], :, lanes] for half in range(2)] for c in range(3)
    ]
    keys_t = [part.T for part in keys]
    deltas = []
    for half in range(2):
        attended = att_ref[places[half], :, lanes].astype(jnp.float32)
        product = (grads[half].astype(jnp.float32) * attended).T
        deltas.append([
            jnp.sum(product[head * HEAD_DIM : (head + 1) * HEAD_DIM], axis=0, keepdims=True)
            for head in range(2)
        ])
    key_grads = {}
    value_grads = {}
    query_grads = []
    for half, tile in chunks:
        here = slice(tile * TILE, (tile + 1) * TILE)
        asked = stacked_heads(queries[half][here])
        grad = stacked_heads(grads[half][here])
        lse = jnp.concatenate([lse_ref[pair, head, half, :, here] for head in range(2)], axis=1)
        delta = jnp.concatenate([deltas[half][head][:, here] for head in range(2)], axis=1)
        spans = []
        if half == 1:
            spans.append((0, 0, rows))
        if tile > 0:
            spans.append((half, 0, tile * TILE))
        spans.append((half, tile * TILE, TILE))
        query_grad = None
        for where, start, size in spans:
            span = slice(start, start + size)
            scores = dot(keys[where][span], asked, CONTRACT_COLS)
            probs = jnp.exp2(scores * scale - lse)
            if (where, start) == (half, tile * TILE):
                probs = jnp.where(later, 0.0, probs)
            grad_probs = dot(values[where][span], grad, CONTRACT_COLS)
            grad_scores = (probs * (grad_probs - delta)).astype(bf16)
            value_term = dot(probs.astype(bf16), grad)
            key_term = dot(grad_scores, asked)
            query_grad = plus(query_grad, dot(keys_t[where][:, span], grad_scores))
            for part in range(size // TILE):
                at_part = (where, start // TILE + part)
                cut = slice(part * TILE, (part + 1) * TILE)
                value_grads[at_part] = plus(value_grads.get(at_part), value_term[cut])
                key_grads[at_part] = plus(key_grads.get(at_part), key_term[cut])
        query_grads.append((own_heads(query_grad) * plain).astype(bf16))
    turned = []
    for half in range(2):
        at_half = [i for i, (where, _) in enumerate(chunks) if where == half]
        query_t = jnp.concatenate([query_grads[i] for i in at_half], axis=1)
        key = jnp.concatenate(
            [(key_grads[half, tile] * plain).astype(bf16) for tile in range(tiles)], axis=0
        )
        value = jnp.concatenate(
            [value_grads[half, tile].astype(bf16) for tile in range(tiles)], axis=0
        )
        turned.append([query_t, key.T, value.T, att_ref[places[half], :, lanes].T])
        for c, part in enumerate((query_t.T, key, value)):
            grad_rows_ref[c, places[half]] = part
    top, bottom = 0.0, 0.0
    for side in range(2):
        mine = [jnp.where(is_own[side], a, b) for a, b in zip(turned[0], turned[1])]
        rows_here = firsts[side][...]
        top = top + dot(jnp.concatenate(mine[:2], axis=0), rows_here)
        bottom = bottom + jnp.concatenate(
            [dot(mine[2], rows_here), dot(mine[3], sides[side])], axis=0
        )
    split_halves(at_ref[slot], pl.ds(place * unit, unit), top, bottom, keep_ref, send_ref)


def attend_back(at, slot, pair, place, count, qkv, att, lse, grad_own, grad_other, out_weight,
                first_own, first_other, old=(), after=()):
    rows, width = first_own.shape
    blocks = 2 ** (SPLITS - 1)
    unit = 4 * PAIR // (2 * blocks)
    pieces = ((blocks, count * unit, width), jnp.bfloat16)
    arrays = [qkv, att, lse, *grad_own, *grad_other, out_weight, first_own, first_other, *old]
    return local_call(
        functools.partial(attend_back_kernel, slot, pair, place),
        "attend_back",
        at,
        arrays,
        [pieces, pieces, ((3, 2, rows, PAIR), jnp.bfloat16)],
        after,
        aliases={len(arrays) - 1: 0, len(arrays): 1} if old else {},
        mebibytes=12,
    )


def first_back_kernel(count, at_ref, weight_ref, *refs):
    own_ref, upper_ref, lower_ref = refs[-3:]
    pieces = []
    for index, ref in enumerate(refs[:count]):
        lanes = slice(index * PAIR, (index + 1) * PAIR)
        pieces += [(ref, c, lanes) for c in range(3)]
    weight = jnp.concatenate([weight_ref[c, :, lanes] for _, c, lanes in pieces], axis=1)
    own, other = [
        jnp.concatenate([ref[c, side] for ref, c, _ in pieces], axis=1) for side in range(2)
    ]
    give_halves(upper_ref, lower_ref, dot(other, weight, CONTRACT_COLS))
    own_ref[...] = dot(own, weight, CONTRACT_COLS)


def first_back(at, weight, groups, after=()):
    shape = (groups[0].shape[2], weight.shape[1])
    half = ((HALF_ROWS, weight.shape[1]), jnp.bfloat16)
    return local_call(
        functools.partial(first_back_kernel, len(groups)), "first_back", at, [weight, *groups],
        [(shape, jnp.float32), half, half], after,
    )


def fold_kernel(slot, at_ref, kept_ref, came_ref, *refs):
    keep_ref, send_ref = refs[-2:]
    half = keep_ref.shape[0]
    bit = at_ref[slot]
    for target, start in ((send_ref, (1 - bit) * half), (keep_ref, bit * half)):
        for index in range(half):
            total = kept_ref[start + index].astype(jnp.float32) + came_ref[
                start + index
            ].astype(jnp.float32)
            target[index] = total.astype(jnp.bfloat16)


def add_kernel(at_ref, kept_ref, came_ref, *refs):
    total = kept_ref[...].astype(jnp.float32) + came_ref[...].astype(jnp.float32)
    refs[-1][...] = total.astype(jnp.bfloat16)


def widen(pair):
    half = pair.shape[0] // 2
    pair = pair.astype(jnp.float32)
    return pair[:half] + pair[half:]


def narrow(value):
    high = value.astype(jnp.bfloat16)
    low = (value - high.astype(jnp.float32)).astype(jnp.bfloat16)
    return jnp.concatenate([high, low], axis=0)


def add_small_kernel(at_ref, kept_ref, came_ref, mine_ref, other_ref, *refs):
    total = kept_ref[0].astype(jnp.float32) + came_ref[0].astype(jnp.float32)
    refs[-1][0] = total.astype(jnp.bfloat16)
    refs[-1][1] = narrow(mine_ref[...] + other_ref[...])


def again_kernel(at_ref, mine_ref, came_ref, *refs):
    total = mine_ref[0].astype(jnp.float32) + came_ref[0].astype(jnp.float32)
    refs[-1][0] = total.astype(jnp.bfloat16)
    if mine_ref.shape[0] > 1:
        refs[-1][1] = narrow(widen(mine_ref[1]) + widen(came_ref[1]))


def join_kernel(slot, at_ref, mine_ref, came_ref, *refs):
    both_ref = refs[-1]
    half = both_ref.shape[0] // 2
    bit = at_ref[slot]
    for source, start in ((mine_ref, bit * half), (came_ref, (1 - bit) * half)):
        for index in range(half):
            both_ref[start + index] = source[index]
    if both_ref.shape[0] > 2 * half:
        both_ref[2 * half] = narrow(widen(mine_ref[half]) + widen(came_ref[half]))


def fold(at, slot, kept, came, after=()):
    blocks, rows, width = kept.shape
    outs = [((blocks // 2, rows, width), jnp.bfloat16)] * 2
    return local_call(
        functools.partial(fold_kernel, slot), "fold", at, [kept, came], outs, after
    )


def last_fold(at, kept, came, small, after=()):
    blocks, rows, width = kept.shape
    kernel = add_small_kernel if small else add_kernel
    outs = [((blocks + (1 if small else 0), rows, width), jnp.bfloat16)]
    return local_call(kernel, "add", at, [kept, came, *small], outs, after)[0]


def again(at, mine, came, after=()):
    outs = [(mine.shape, jnp.bfloat16)]
    return local_call(again_kernel, "again", at, [mine, came], outs, after)[0]


def join(at, slot, mine, came, blocks, after=()):
    _, rows, width = mine.shape
    extra = mine.shape[0] - blocks
    outs = [((2 * blocks + extra, rows, width), jnp.bfloat16)]
    return local_call(
        functools.partial(join_kernel, slot), "join", at, [mine, came], outs, after
    )[0]


def ordered_units(bit, mine_ref, came_ref, blocks, unit):
    width = mine_ref.shape[2]
    for index in range(mine_ref.shape[1] // unit):
        rows = slice(index * unit, (index + 1) * unit)
        mine = mine_ref[:blocks, rows, :].reshape(blocks * unit, width)
        came = came_ref[:blocks, rows, :].reshape(blocks * unit, width)
        yield index, jnp.where(bit == 0, mine, came), jnp.where(bit == 0, came, mine)


def finish_mlp_kernel(slot, start, blocks, at_ref, mine_ref, came_ref, *refs):
    up_ref, down_ref, token_ref, turned_ref, held_ref, up_sems, down_sems = refs[-7:]
    token_ref[...] = jnp.zeros_like(token_ref)
    copies = []
    for index, top, bottom in ordered_units(
        at_ref[slot], mine_ref, came_ref, blocks, TILE // blocks
    ):
        place = pl.ds((start + index) * TILE, TILE)
        held_ref[index] = bottom.astype(jnp.float32)
        copies.append(
            pltpu.make_async_copy(held_ref.at[index], down_ref.at[place, :], down_sems.at[index])
        )
        copies[-1].start()
        turned_ref[index] = top.T.astype(jnp.float32)
        copies.append(
            pltpu.make_async_copy(turned_ref.at[index], up_ref.at[:, place], up_sems.at[index])
        )
        copies[-1].start()
    for copy in copies:
        copy.wait()


def finish_attend_kernel(slot, start, blocks, at_ref, mine_ref, came_ref, *refs):
    token_ref, turned_ref, held_ref, qkv_sems, out_sems = refs[-5:]
    smalls = 3 if mine_ref.shape[0] > blocks else 0
    qkv_ref, out_ref = refs[-7 - smalls : -5 - smalls]
    if mine_ref.shape[0] > blocks:
        small = widen(mine_ref[blocks]) + widen(came_ref[blocks])
        attn_ref, mlp_ref, depth_ref = refs[-8:-5]
        attn_ref[...] = small[0]
        mlp_ref[...] = small[1]
        depth_ref[...] = jnp.sum(small[8 : 8 + depth_ref.shape[0]], axis=1)
    token_ref[...] = jnp.zeros_like(token_ref)
    copies = []
    for index, top, bottom in ordered_units(
        at_ref[slot], mine_ref, came_ref, blocks, 2 * PAIR // blocks
    ):
        place = pl.ds((start + index) * PAIR, PAIR)
        held_ref[index] = bottom[PAIR:].astype(jnp.float32)
        copies.append(
            pltpu.make_async_copy(held_ref.at[index], out_ref.at[place, :], out_sems.at[index])
        )
        copies[-1].start()
        for c, part in enumerate((top[:PAIR], top[PAIR:], bottom[:PAIR])):
            turned_ref[index, c] = part.T.astype(jnp.float32)
        copies.append(
            pltpu.make_async_copy(
                turned_ref.at[index], qkv_ref.at[:, :, place], qkv_sems.at[index]
            )
        )
        copies[-1].start()
    for copy in copies:
        copy.wait()


def finish(kernel, name, at, slot, start, mine, came, shapes, scratch, old=None, after=(),
           smalls=()):
    in_vmem = pl.BlockSpec(memory_space=pltpu.VMEM)
    in_hbm = pl.BlockSpec(memory_space=pltpu.HBM)
    blocks = 2 ** (SPLITS - 1)
    units = mine.shape[1] * blocks // TILE
    return pl.pallas_call(
        functools.partial(kernel, slot, start, blocks),
        in_specs=[pl.BlockSpec(memory_space=pltpu.SMEM), in_vmem, in_vmem]
        + [in_hbm] * len(old or [])
        + [pl.BlockSpec(memory_space=pl.ANY)] * len(after),
        out_specs=[in_hbm, in_hbm] + [in_vmem] * (len(smalls) + 1),
        out_shape=[
            jax.ShapeDtypeStruct(shape, jnp.float32) for shape in [*shapes, *smalls, (8, 128)]
        ],
        scratch_shapes=[pltpu.VMEM((units, *shape), jnp.float32) for shape in scratch]
        + [pltpu.SemaphoreType.DMA((units,))] * 2,
        input_output_aliases={3: 0, 4: 1} if old else {},
        compiler_params=params(12),
        cost_estimate=cost(1000, 1000),
        name=name,
    )(at, mine, came, *(old or []), *after)


def finish_mlp(at, slot, start, mine, came, width, hidden, old=None, after=()):
    shapes = [(width, hidden), (hidden, width)]
    scratch = [(width, TILE), (TILE, width)]
    return finish(
        finish_mlp_kernel, "finish_mlp", at, slot, start, mine, came, shapes, scratch, old, after
    )


def finish_attend(at, slot, start, mine, came, width, local, layers, old=None, after=()):
    shapes = [(3, width, local), (local, width)]
    scratch = [(3, width, PAIR), (PAIR, width)]
    smalls = [(width,), (width,), (layers,)] if mine.shape[0] > 2 ** (SPLITS - 1) else []
    return finish(
        finish_attend_kernel, "finish_attend", at, slot, start, mine, came, shapes, scratch, old,
        after, smalls,
    )


def mp_swap(rows):
    return lax.ppermute(rows, "mp", [(0, 1), (1, 0)])


def dp_bits():
    return lax.axis_size("dp").bit_length() - 1


def bit_swap(rows, bits):
    size, cores = lax.axis_size("dp"), lax.axis_size("mp")
    pairs = [
        (i * cores + core, (i ^ (1 << bits[core])) * cores + core)
        for i in range(size)
        for core in range(cores)
    ]
    return lax.ppermute(rows, ("dp", "mp"), pairs)


def step_bits(kind, step):
    return [order[step] for order in KINDS[kind]]


def slot_of(kind, step):
    return 1 + kind * SPLITS + step


def where_am_i():
    core, index = lax.axis_index("mp"), lax.axis_index("dp")
    values = [core]
    for kind in range(len(KINDS)):
        for step in range(SPLITS):
            bits = step_bits(kind, step)
            values.append((index >> jnp.where(core == 0, bits[0], bits[1])) & 1)
    return jnp.stack(values).astype(jnp.int32)


class Stream:
    def __init__(self, at, kind, kept, sent, small=None):
        self.at, self.kind, self.kept, self.step, self.small = at, kind, kept, 0, small
        self.extra = dp_bits() - SPLITS
        self.came = bit_swap(sent, step_bits(kind, 0))

    def advance(self, after=()):
        step, kind, at = self.step, self.kind, self.at
        self.step += 1
        joined = step - SPLITS - self.extra
        if step < SPLITS - 1:
            self.kept, sent = fold(at, slot_of(kind, step + 1), self.kept, self.came, after)
            self.came = bit_swap(sent, step_bits(kind, step + 1))
            return self.kept
        if step == SPLITS - 1:
            small = self.small() if self.small else ()
            self.kept = last_fold(at, self.kept, self.came, small, after)
        elif joined < 0:
            self.kept = again(at, self.kept, self.came, after)
        else:
            slot = slot_of(kind, SPLITS - 1 - joined)
            self.kept = join(at, slot, self.kept, self.came, 2**joined, after)
        if joined < -1:
            bit = SPLITS + joined + 1 + self.extra
            self.came = bit_swap(self.kept, [bit, bit])
        else:
            self.came = bit_swap(self.kept, step_bits(kind, SPLITS - 2 - joined))
        return self.kept


def shards(
    history,
    depth_weights,
    gain_attn,
    gain_mlp,
    qkv_weight,
    out_weight,
    up_weight,
    down_weight,
    cotangent,
):
    width = cotangent.shape[1]
    local = out_weight.shape[0]
    hidden = down_weight.shape[0]
    pairs = local // PAIR
    at = where_am_i()

    cot_other = mp_swap(cotangent)
    mixed, first = mix(depth_weights, history, gain_attn)
    first_other = mp_swap(first)
    back_own = hidden_back(at, cotangent, down_weight)
    qkv, att, lse, out_own, out_other = attend(
        at, first, first_other, qkv_weight, out_weight, [back_own]
    )
    middle, second = renorm(at, mixed, out_own, mp_swap(out_other), gain_mlp)
    back_other = hidden_back(at, cot_other, down_weight, [second])
    second_other = mp_swap(second)
    mlp_names = [name for name in KIND if name[0] == "M"]
    *stacks, hidden_rows, grad_own, grad_upper, grad_lower = mlp(
        at, tuple(slot_of(KIND[name], 0) for name in mlp_names), second, second_other, cotangent,
        cot_other, back_own, back_other, up_weight,
    )
    streams = {
        name: Stream(at, KIND[name], *stacks[2 * i : 2 * i + 2])
        for i, name in enumerate(mlp_names)
    }
    grad_came = [mp_swap(part) for part in (grad_upper, grad_lower)]
    made = {}

    def back_norm(after):
        made["middle"], *made["narrow"], made["gain"] = norm_back_rows(
            at, grad_own, grad_came, middle, cotangent, gain_mlp, after
        )
        made["narrow_came"] = [mp_swap(part) for part in made["narrow"]]
        return made["gain"]

    def back_pair(pair, after):
        late = pair == pairs - 1
        name, place = ("Ab", 0) if late else ("Aa", pair)
        old = () if late or pair == 0 else made["stack"]
        kept, sent, made[pair] = attend_back(
            at, slot_of(KIND[name], 0), pair, place, 1 if late else pairs - 1, qkv, att, lse,
            made["narrow"], made["narrow_came"], out_weight, first, first_other, old, after,
        )
        made["stack"] = (kept, sent)
        if pair >= pairs - 2:
            small = (lambda: (made["small"], made["small_came"])) if late else None
            streams[name] = Stream(at, KIND[name], kept, sent, small)
        return made[pair]

    def back_first(after):
        groups = [made[pair] for pair in range(pairs)]
        made["own"], *other = first_back(at, qkv_weight, groups, after)
        made["came"] = [mp_swap(part) for part in other]
        return made["own"]

    def back_start(after):
        made["mixed"], made["small"] = unmix(
            depth_weights, history, gain_attn, mixed, made["middle"], made["own"], made["came"],
            made["gain"], after,
        )
        made["small_came"] = mp_swap(made["small"])
        return made["small"]

    def give_outputs(after):
        made["history"], made["out"], token = outputs(
            depth_weights, made["mixed"], middle, made["block"], made["block_came"], after
        )
        return token

    def block_rows(after):
        made["block"], *other = rows_times(at, hidden_rows, down_weight, after)
        made["block_came"] = [mp_swap(part) for part in other]
        return made["block"]

    def end_mlp(name, start, after):
        stream = streams[name]
        *made["mlp"], token = finish_mlp(
            at, slot_of(KIND[name], 0), start, stream.kept, stream.came, width, hidden,
            made.get("mlp"), after,
        )
        return token

    def end_attend(name, start, after):
        stream = streams[name]
        grad_qkv, grad_out, *made[name], token = finish_attend(
            at, slot_of(KIND[name], 0), start, stream.kept, stream.came, width, local,
            history.shape[0], made.get("attend"), after,
        )
        made["attend"] = grad_qkv, grad_out
        return token

    units = {
        "nb": back_norm,
        "fb": back_first,
        "um": back_start,
        "um2": give_outputs,
        "blk": block_rows,
        "fAa": functools.partial(end_attend, "Aa", 0),
        "fAb": functools.partial(end_attend, "Ab", pairs - 1),
    }
    start = 0
    for name, count in zip(mlp_names, MLP_UNITS):
        units["f" + name] = functools.partial(end_mlp, name, start)
        start += count
    for pair in range(pairs):
        units["ab" + str(pair)] = functools.partial(back_pair, pair)
    last = hidden_rows
    for name in ORDER:
        if name in streams:
            if streams[name].step == SPLITS:
                for _ in range(streams[name].extra - 1):
                    last = streams[name].advance([last])
            last = streams[name].advance([last])
        else:
            last = units[name]([last])
    gain_grad_attn, gain_grad_mlp, grad_depth = made["Ab"]
    block_out, grad_history = made["out"], made["history"]
    (grad_up, grad_down), (grad_qkv, grad_out) = made["mlp"], made["attend"]
    return (
        block_out,
        grad_history,
        grad_depth,
        gain_grad_attn,
        gain_grad_mlp,
        grad_qkv,
        grad_out,
        grad_up,
        grad_down,
    )


def solution(mesh):
    in_specs = (
        P(None, ("dp", "mp"), None),
        P(),
        P(),
        P(),
        P(None, None, "mp"),
        P("mp", None),
        P(None, "mp"),
        P("mp", None),
        P(("dp", "mp"), None),
    )
    out_specs = (
        P(("dp", "mp"), None),
        P(None, ("dp", "mp"), None),
        P(),
        P(),
        P(),
        P(None, None, "mp"),
        P("mp", None),
        P(None, "mp"),
        P("mp", None),
    )
    return jax.shard_map(shards, mesh=mesh, in_specs=in_specs, out_specs=out_specs, check_vma=False)
```

```python
import functools

import jax
import jax.numpy as jnp
from jax import lax
from jax.experimental import pallas as pl
from jax.experimental.pallas import tpu as pltpu
from jax.sharding import PartitionSpec as P

HEAD_DIM = 64
EPSILON = 1e-05
SQRT_HALF = 0.7071067811865476
INV_ROOT_TWO_PI = 0.3989422804014327
LOG2E = 1.4426950408889634
NEG = -1e30
TILE = 256
ROW_BLOCK = 64
HALF_ROWS = 256
MIX_BLOCK = 128
SMALL_ROWS = 32
SPLITS = 3
PAIR = 2 * HEAD_DIM
CHUNK = 256
ORDER = (
    "nb", "ab0", "ab1", "Mb", "Ma", "Mc", "ab2", "fb", "Mb", "Ma", "Aa", "Mb", "Mc", "Ma",
    "Aa", "Mb", "Ab", "Mc", "um", "Ma", "Aa", "Mb", "Ab", "Mc", "Ma", "blk", "Aa", "Ab", "Mc",
    "Mb", "Ma", "Mc", "Ab", "Aa", "um2", "Aa", "Ab", "fMb", "fMa", "Ab", "fMc", "fAa", "fAb",
)
KINDS = (
    ((0, 1, 2), (1, 2, 0)),
    ((0, 1, 2), (2, 0, 1)),
    ((2, 1, 0), (1, 0, 2)),
    ((0, 2, 1), (2, 1, 0)),
    ((0, 1, 2), (1, 0, 2)),
)
KIND = {"Ma": 0, "Mb": 1, "Mc": 2, "Aa": 3, "Ab": 4}
MLP_UNITS = (2, 2, 2)

PLAIN = (((1,), (0,)), ((), ()))
CONTRACT_COLS = (((1,), (1,)), ((), ()))
CONTRACT_ROWS = (((0,), (0,)), ((), ()))


def dot(lhs, rhs, dims=PLAIN):
    return lax.dot_general(lhs, rhs, dims, preferred_element_type=jnp.float32)


def cost(flops, moved, exps=0):
    return pl.CostEstimate(flops=flops, bytes_accessed=moved, transcendentals=exps)


def params(mebibytes=8):
    return pltpu.CompilerParams(vmem_limit_bytes=mebibytes * 2**20)


def normalize(inputs):
    row_mean = jnp.mean(inputs, axis=-1, keepdims=True)
    centered = inputs - row_mean
    variance = jnp.mean(centered * centered, axis=-1, keepdims=True)
    inv_scale = lax.rsqrt(variance + EPSILON)
    return centered * inv_scale, inv_scale


def norm_back(grad_rows, gain_row, normed, inv_scale):
    scaled = grad_rows * gain_row
    first_mean = jnp.mean(scaled, axis=-1, keepdims=True)
    second_mean = jnp.mean(scaled * normed, axis=-1, keepdims=True)
    return inv_scale * (scaled - first_mean - normed * second_mean)


def gelu_value(inputs):
    return 0.5 * inputs * (1.0 + lax.erf(inputs * SQRT_HALF))


def gelu_slope(inputs):
    normal_cdf = 0.5 * (1.0 + lax.erf(inputs * SQRT_HALF))
    return normal_cdf + inputs * jnp.exp(-0.5 * inputs * inputs) * INV_ROOT_TWO_PI


def layer_copies(history_ref, held_ref, sems, out=False):
    copies = []
    for index in range(held_ref.shape[0]):
        rows = pl.ds(index * ROW_BLOCK, ROW_BLOCK)
        ends = (history_ref.at[:, rows, :], held_ref.at[index])
        copies.append(
            pltpu.make_async_copy(ends[out], ends[not out], sems.at[index])
        )
    return copies


def mix_kernel(weights_ref, gain_ref, history_ref, mixed_ref, first_ref):
    mixed = weights_ref[0] * history_ref[0].astype(jnp.float32)
    for layer in range(1, history_ref.shape[0]):
        mixed = mixed + weights_ref[layer] * history_ref[layer].astype(jnp.float32)
    mixed_ref[...] = mixed
    normed, _ = normalize(mixed)
    first_ref[...] = (normed * gain_ref[...]).astype(jnp.bfloat16)


def mix(weights, history, gain):
    layers, rows, width = history.shape
    row_spec = pl.BlockSpec((MIX_BLOCK, width), lambda i: (i, 0))
    return pl.pallas_call(
        mix_kernel,
        grid=(rows // MIX_BLOCK,),
        in_specs=[
            pl.BlockSpec(memory_space=pltpu.SMEM),
            pl.BlockSpec((width,), lambda i: (0,)),
            pl.BlockSpec((layers, MIX_BLOCK, width), lambda i: (0, i, 0)),
        ],
        out_specs=[row_spec, row_spec],
        out_shape=[
            jax.ShapeDtypeStruct((rows, width), jnp.float32),
            jax.ShapeDtypeStruct((rows, width), jnp.bfloat16),
        ],
        compiler_params=params(57),
        cost_estimate=cost(1000, 1000),
        name="mix",
    )(weights, gain, history)


def unmix_kernel(
    weights_ref, gain_ref, mixed_ref, middle_ref, own_ref, upper_ref, lower_ref, gain_mlp_ref,
    history_ref, *refs,
):
    grad_ref, small_ref = refs[-2:]
    small_ref[...] = jnp.zeros_like(small_ref)
    small_ref[1:2] = gain_mlp_ref[...]
    for index in range(grad_ref.shape[0] // ROW_BLOCK):
        rows = pl.ds(index * ROW_BLOCK, ROW_BLOCK)
        start = index * ROW_BLOCK
        part, start = (upper_ref, start) if start < HALF_ROWS else (lower_ref, start - HALF_ROWS)
        other = part[start : start + ROW_BLOCK, :].astype(jnp.float32)
        grad_first = own_ref[rows, :] + other
        normed, inv_scale = normalize(mixed_ref[rows, :])
        grad_mixed = middle_ref[rows, :] + norm_back(
            grad_first, gain_ref[...], normed, inv_scale
        )
        grad_ref[rows, :] = grad_mixed
        small_ref[0:1] += jnp.sum(grad_first * normed, axis=0, keepdims=True)
        for layer in range(history_ref.shape[0]):
            product = history_ref[layer, rows, :].astype(jnp.float32) * grad_mixed
            small_ref[8 + layer : 9 + layer] += jnp.sum(product, axis=0, keepdims=True)


def unmix(weights, history, gain, mixed, grad_middle, own, other, gain_grad_mlp, after=()):
    _, rows, width = history.shape
    in_vmem = pl.BlockSpec(memory_space=pltpu.VMEM)
    return pl.pallas_call(
        unmix_kernel,
        in_specs=[pl.BlockSpec(memory_space=pltpu.SMEM)]
        + [in_vmem] * 8
        + [pl.BlockSpec(memory_space=pl.ANY)] * len(after),
        out_specs=[in_vmem, in_vmem],
        out_shape=[
            jax.ShapeDtypeStruct((rows, width), jnp.float32),
            jax.ShapeDtypeStruct((SMALL_ROWS, width), jnp.float32),
        ],
        compiler_params=params(),
        cost_estimate=cost(1000, 1000),
        name="unmix",
    )(weights, gain, mixed, grad_middle, own, *other, gain_grad_mlp, history, *after)


def outputs_kernel(
    weights_ref, grad_ref, rows_ref, block_own_ref, upper_ref, lower_ref, *refs
):
    grads_ref, out_ref, token_ref, given_ref, made_ref, sems, made_sem = refs[-7:]
    token_ref[...] = jnp.zeros_like(token_ref)
    gives = layer_copies(grads_ref, given_ref, sems, True)
    other = jnp.concatenate([upper_ref[...], lower_ref[...]], axis=0).astype(jnp.float32)
    made_ref[...] = (rows_ref[...] + block_own_ref[...] + other).astype(jnp.bfloat16)
    make = pltpu.make_async_copy(made_ref, out_ref, made_sem)
    make.start()
    for index, give in enumerate(gives):
        grad_mixed = grad_ref[pl.ds(index * ROW_BLOCK, ROW_BLOCK), :]
        for layer in range(given_ref.shape[1]):
            given_ref[index, layer] = (weights_ref[layer] * grad_mixed).astype(jnp.bfloat16)
        give.start()
    make.wait()
    for give in gives:
        give.wait()


def outputs(weights, grad_mixed, rows, block_own, block_other, after=()):
    layers = weights.shape[0]
    count, width = grad_mixed.shape
    in_vmem = pl.BlockSpec(memory_space=pltpu.VMEM)
    in_hbm = pl.BlockSpec(memory_space=pltpu.HBM)
    blocks = count // ROW_BLOCK
    return pl.pallas_call(
        outputs_kernel,
        in_specs=[pl.BlockSpec(memory_space=pltpu.SMEM)]
        + [in_vmem] * 5
        + [pl.BlockSpec(memory_space=pl.ANY)] * len(after),
        out_specs=[in_hbm, in_hbm, in_vmem],
        out_shape=[
            jax.ShapeDtypeStruct((layers, count, width), jnp.bfloat16),
            jax.ShapeDtypeStruct((count, width), jnp.bfloat16),
            jax.ShapeDtypeStruct((8, 128), jnp.float32),
        ],
        scratch_shapes=[
            pltpu.VMEM((blocks, layers, ROW_BLOCK, width), jnp.bfloat16),
            pltpu.VMEM((count, width), jnp.bfloat16),
            pltpu.SemaphoreType.DMA((blocks,)),
            pltpu.SemaphoreType.DMA,
        ],
        compiler_params=params(10),
        cost_estimate=cost(1000, 1000),
        name="outputs",
    )(weights, grad_mixed, rows, block_own, *block_other, *after)


def head_mask(head):
    lanes = lax.broadcasted_iota(jnp.int32, (1, PAIR), 1)
    return (lanes // HEAD_DIM) == head


def future_mask():
    keys = lax.broadcasted_iota(jnp.int32, (TILE, TILE), 0)
    asks = lax.broadcasted_iota(jnp.int32, (TILE, TILE), 1)
    return keys > asks


def stacked_heads(rows):
    zero = jnp.zeros_like(rows)
    return jnp.concatenate([jnp.where(head_mask(head), rows, zero) for head in range(2)], axis=0)


def own_heads(columns):
    half = columns.shape[1] // 2
    return jnp.concatenate([columns[:HEAD_DIM, :half], columns[HEAD_DIM:, half:]], axis=0)


def local_call(kernel, name, at, arrays, outs, after=(), scratch=(), aliases=None,
               mebibytes=8):
    in_vmem = pl.BlockSpec(memory_space=pltpu.VMEM)
    return pl.pallas_call(
        kernel,
        in_specs=[pl.BlockSpec(memory_space=pltpu.SMEM)]
        + [in_vmem] * len(arrays)
        + [pl.BlockSpec(memory_space=pl.ANY)] * len(after),
        out_specs=[in_vmem] * len(outs),
        out_shape=[jax.ShapeDtypeStruct(shape, dtype) for shape, dtype in outs],
        scratch_shapes=list(scratch),
        input_output_aliases=aliases or {},
        compiler_params=params(mebibytes),
        cost_estimate=cost(1000, 1000),
        name=name,
    )(at, *arrays, *after)


def attend_kernel(
    at_ref, own_ref, other_ref, weight_ref, out_weight_ref, *refs,
):
    qkv_ref, att_ref, lse_ref, out_own_ref, out_other_ref = refs[-5:]
    rows = own_ref.shape[0]
    tiles = rows // TILE
    first = at_ref[0]
    scale = HEAD_DIM ** (-0.5) * LOG2E
    places = (first, 1 - first)
    later = jnp.concatenate([future_mask()] * 2, axis=1)

    def one_pair(pair, carry):
        lanes = pl.ds(pl.multiple_of(pair * PAIR, PAIR), PAIR)
        weight = jnp.concatenate([weight_ref[c, :, lanes] for c in range(3)], axis=1)
        for side, ref in enumerate((own_ref, other_ref)):
            made = dot(ref[...], weight).astype(jnp.bfloat16)
            for c in range(3):
                qkv_ref[c, side, :, lanes] = made[:, c * PAIR : (c + 1) * PAIR]
        half_keys = [qkv_ref[1, places[half], :, lanes] for half in range(2)]
        half_values = [qkv_ref[2, places[half], :, lanes].T for half in range(2)]
        for half in range(2):
            for tile in range(tiles):
                at_rows = pl.ds(tile * TILE, TILE)
                queries = qkv_ref[0, places[half], at_rows, lanes]
                asked = stacked_heads(queries)
                spans = []
                if half == 1:
                    spans.append((0, 0, rows))
                if tile > 0:
                    spans.append((half, 0, tile * TILE))
                spans.append((half, tile * TILE, TILE))
                scores = [
                    dot(half_keys[where][start : start + size], asked, CONTRACT_COLS)
                    for where, start, size in spans
                ]
                scores[-1] = jnp.where(later, NEG, scores[-1])
                top = functools.reduce(
                    jnp.maximum, [jnp.max(part, axis=0, keepdims=True) for part in scores]
                )
                top = top * scale
                total = 0.0
                summed = 0.0
                for part, (where, start, size) in zip(scores, spans):
                    weights = jnp.exp2(part * scale - top)
                    total = total + jnp.sum(weights, axis=0, keepdims=True)
                    summed = summed + dot(
                        half_values[where][:, start : start + size], weights.astype(jnp.bfloat16)
                    )
                lse = top + jnp.log2(total)
                for head in range(2):
                    lse_ref[pair, head, half, :, at_rows] = lse[:, head * TILE : (head + 1) * TILE]
                joined = own_heads(summed / total).T
                att_ref[places[half], at_rows, lanes] = joined.astype(jnp.bfloat16)
        return carry

    lax.fori_loop(0, att_ref.shape[2] // PAIR, one_pair, 0)
    out_other_ref[...] = dot(att_ref[1], out_weight_ref[...]).astype(jnp.bfloat16)
    out_own_ref[...] = dot(att_ref[0], out_weight_ref[...])


def attend(at, own, other, weight, out_weight, after=()):
    rows, width = own.shape
    local = weight.shape[2]
    return local_call(
        attend_kernel,
        "attend",
        at,
        [own, other, weight, out_weight],
        [
            ((3, 2, rows, local), jnp.bfloat16),
            ((2, rows, local), jnp.bfloat16),
            ((local // PAIR, 2, 2, 1, rows), jnp.float32),
            ((rows, width), jnp.float32),
            ((rows, width), jnp.bfloat16),
        ],
        after,
        mebibytes=12,
    )


def renorm_kernel(at_ref, mixed_ref, own_ref, other_ref, gain_ref, *refs):
    middle_ref, second_ref = refs[-2:]
    middle = mixed_ref[...] + own_ref[...] + other_ref[...].astype(jnp.float32)
    middle_ref[...] = middle
    second_ref[...] = (normalize(middle)[0] * gain_ref[...]).astype(jnp.bfloat16)


def renorm(at, mixed, own, other, gain, after=()):
    return local_call(
        renorm_kernel,
        "renorm",
        at,
        [mixed, own, other, gain],
        [(mixed.shape, jnp.float32), (mixed.shape, jnp.bfloat16)],
        after,
    )


def hidden_back_kernel(start, at_ref, cot_ref, down_ref, *refs):
    rows = cot_ref[start : start + refs[-1].shape[0], :]
    refs[-1][...] = dot(rows, down_ref[...], CONTRACT_COLS).astype(jnp.bfloat16)


def hidden_back(at, cotangent, down, start, count, after=()):
    outs = [((count, down.shape[0]), jnp.bfloat16)]
    return local_call(
        functools.partial(hidden_back_kernel, start), "hidden_back", at, [cotangent, down], outs, after
    )[0]


def split_halves(bit, rows, top, bottom, keep_ref, send_ref):
    shape = (keep_ref.shape[0], -1, keep_ref.shape[2])
    top = top.astype(jnp.bfloat16).reshape(shape)
    bottom = bottom.astype(jnp.bfloat16).reshape(shape)
    keep_ref[:, rows, :] = jnp.where(bit == 0, top, bottom)
    send_ref[:, rows, :] = jnp.where(bit == 0, bottom, top)


def give_halves(upper_ref, lower_ref, value):
    value = value.astype(jnp.bfloat16)
    upper_ref[...], lower_ref[...] = value[:HALF_ROWS], value[HALF_ROWS:]


def take_halves(upper_ref, lower_ref):
    return jnp.concatenate([upper_ref[...], lower_ref[...]], axis=0)


def mlp_kernel(
    slots, at_ref, second_own_ref, second_other_ref, cot_own_ref, cot_other_ref, back_up_ref,
    back_low_ref, back_other_ref, up_ref, *refs,
):
    stacks = refs[-5 - 2 * len(slots) : -5]
    hidden_ref, own_ref, upper_ref, lower_ref, grad_pre_ref = refs[-5:]
    bf16 = jnp.bfloat16
    chunks = hidden_ref.shape[2] // CHUNK
    sides = ((second_own_ref, cot_own_ref), (second_other_ref, cot_other_ref))
    backs = ((back_up_ref, back_low_ref), (back_other_ref,))
    unit = TILE // stacks[0].shape[0]
    homes = []
    for index in range(len(slots)):
        keep_ref, send_ref = stacks[2 * index : 2 * index + 2]
        for place in range(keep_ref.shape[1] // unit):
            homes.append((slots[index], pl.ds(place * unit, unit), keep_ref, send_ref))

    def make(chunk):
        lanes = pl.ds(chunk * CHUNK, CHUNK)
        for side, (second_ref, _) in enumerate(sides):
            pre = dot(second_ref[...], up_ref[:, lanes])
            cdf = 0.5 * (1.0 + lax.erf(pre * SQRT_HALF))
            hidden_ref[side, :, lanes] = (pre * cdf).astype(bf16)
            slope = cdf + pre * jnp.exp(-0.5 * pre * pre) * INV_ROOT_TWO_PI
            back = jnp.concatenate([ref[:, lanes] for ref in backs[side]], axis=0)
            grad_hidden = back.astype(jnp.float32)
            grad_pre_ref[side, :, lanes] = (grad_hidden * slope).astype(bf16)

    def give(chunk):
        lanes = pl.ds(chunk * CHUNK, CHUNK)
        grad_up, grad_down = 0.0, 0.0
        for side, (second_ref, cot_ref) in enumerate(sides):
            grad_up = grad_up + dot(grad_pre_ref[side, :, lanes], second_ref[...], CONTRACT_ROWS)
            grad_down = grad_down + dot(hidden_ref[side, :, lanes], cot_ref[...], CONTRACT_ROWS)
        for part in range(CHUNK // TILE):
            slot, place, *home = homes[chunk * (CHUNK // TILE) + part]
            rows = slice(part * TILE, (part + 1) * TILE)
            split_halves(at_ref[slot], place, grad_up[rows], grad_down[rows], *home)

    make(0)
    for chunk in range(1, chunks):
        make(chunk)
        give(chunk - 1)
    give(chunks - 1)
    give_halves(upper_ref, lower_ref, dot(grad_pre_ref[1], up_ref[...], CONTRACT_COLS))
    own_ref[...] = dot(grad_pre_ref[0], up_ref[...], CONTRACT_COLS)


def mlp(at, slots, second_own, second_other, cot_own, cot_other, back_own, back_other, up,
        after=()):
    rows, width = second_own.shape
    hidden = up.shape[1]
    blocks = 2 ** (SPLITS - 1)
    unit = TILE // blocks
    stacks = []
    for count in MLP_UNITS:
        stacks += [((blocks, count * unit, width), jnp.bfloat16)] * 2
    half = ((HALF_ROWS, width), jnp.bfloat16)
    return local_call(
        functools.partial(mlp_kernel, slots),
        "mlp",
        at,
        [second_own, second_other, cot_own, cot_other, *back_own, back_other, up],
        stacks
        + [((2, rows, hidden), jnp.bfloat16), ((rows, width), jnp.float32), half, half],
        after,
        [pltpu.VMEM((2, rows, hidden), jnp.bfloat16)],
    )


def rows_kernel(at_ref, rows_ref, weight_ref, *refs):
    own_ref, upper_ref, lower_ref = refs[-3:]
    give_halves(upper_ref, lower_ref, dot(rows_ref[1], weight_ref[...]))
    own_ref[...] = dot(rows_ref[0], weight_ref[...])


def rows_times(at, rows, weight, after=()):
    shape = (rows.shape[1], weight.shape[1])
    half = ((HALF_ROWS, weight.shape[1]), jnp.bfloat16)
    return local_call(
        rows_kernel, "block", at, [rows, weight], [(shape, jnp.float32), half, half], after
    )


def norm_back_kernel(
    at_ref, own_ref, up_other_ref, low_other_ref, middle_ref, cot_ref, gain_ref, *refs
):
    grad_ref, upper_ref, lower_ref, gain_grad_ref = refs[-4:]
    grad_second = own_ref[...] + take_halves(up_other_ref, low_other_ref).astype(jnp.float32)
    normed, inv_scale = normalize(middle_ref[...])
    grad = cot_ref[...].astype(jnp.float32) + norm_back(
        grad_second, gain_ref[...], normed, inv_scale
    )
    grad_ref[...] = grad
    give_halves(upper_ref, lower_ref, grad)
    gain_grad_ref[...] = jnp.sum(grad_second * normed, axis=0, keepdims=True)


def norm_back_rows(at, own, other, middle, cotangent, gain, after=()):
    shape = own.shape
    half = ((HALF_ROWS, shape[1]), jnp.bfloat16)
    return local_call(
        norm_back_kernel,
        "norm_back_rows",
        at,
        [own, *other, middle, cotangent, gain],
        [(shape, jnp.float32), half, half, ((1, shape[1]), jnp.float32)],
        after,
    )


def attend_back_kernel(
    slot, pair, place, at_ref, qkv_ref, att_ref, lse_ref, up_own_ref, low_own_ref, up_other_ref,
    low_other_ref, out_weight_ref, first_own_ref, first_other_ref, *refs,
):
    keep_ref, send_ref, grad_rows_ref = refs[-3:]
    rows = first_own_ref.shape[0]
    tiles = rows // TILE
    first = at_ref[0]
    plain = HEAD_DIM ** (-0.5)
    scale = plain * LOG2E
    places = (first, 1 - first)
    later = jnp.concatenate([future_mask()] * 2, axis=1)
    bf16 = jnp.bfloat16
    sides = (take_halves(up_own_ref, low_own_ref), take_halves(up_other_ref, low_other_ref))
    firsts = (first_own_ref, first_other_ref)
    unit = 4 * PAIR // (2 * keep_ref.shape[0])
    is_own = [places[half] == 0 for half in range(2)]
    chunks = [(half, tile) for half in range(2) for tile in range(tiles)]

    def plus(old, term):
        return term if old is None else old + term

    lanes = pl.ds(pair * PAIR, PAIR)
    outer = [
        dot(rows_here, out_weight_ref[lanes, :], CONTRACT_COLS).astype(bf16)
        for rows_here in sides
    ]
    grads = [jnp.where(is_own[half], outer[0], outer[1]) for half in range(2)]
    queries, keys, values = [
        [qkv_ref[c, places[half], :, lanes] for half in range(2)] for c in range(3)
    ]
    keys_t = [part.T for part in keys]
    deltas = []
    for half in range(2):
        attended = att_ref[places[half], :, lanes].astype(jnp.float32)
        product = (grads[half].astype(jnp.float32) * attended).T
        deltas.append([
            jnp.sum(product[head * HEAD_DIM : (head + 1) * HEAD_DIM], axis=0, keepdims=True)
            for head in range(2)
        ])
    key_grads = {}
    value_grads = {}
    query_grads = []
    for half, tile in chunks:
        here = slice(tile * TILE, (tile + 1) * TILE)
        asked = stacked_heads(queries[half][here])
        grad = stacked_heads(grads[half][here])
        lse = jnp.concatenate([lse_ref[pair, head, half, :, here] for head in range(2)], axis=1)
        delta = jnp.concatenate([deltas[half][head][:, here] for head in range(2)], axis=1)
        spans = []
        if half == 1:
            spans.append((0, 0, rows))
        if tile > 0:
            spans.append((half, 0, tile * TILE))
        spans.append((half, tile * TILE, TILE))
        query_grad = None
        for where, start, size in spans:
            span = slice(start, start + size)
            scores = dot(keys[where][span], asked, CONTRACT_COLS)
            probs = jnp.exp2(scores * scale - lse)
            if (where, start) == (half, tile * TILE):
                probs = jnp.where(later, 0.0, probs)
            grad_probs = dot(values[where][span], grad, CONTRACT_COLS)
            grad_scores = (probs * (grad_probs - delta)).astype(bf16)
            value_term = dot(probs.astype(bf16), grad)
            key_term = dot(grad_scores, asked)
            query_grad = plus(query_grad, dot(keys_t[where][:, span], grad_scores))
            for part in range(size // TILE):
                at_part = (where, start // TILE + part)
                cut = slice(part * TILE, (part + 1) * TILE)
                value_grads[at_part] = plus(value_grads.get(at_part), value_term[cut])
                key_grads[at_part] = plus(key_grads.get(at_part), key_term[cut])
        query_grads.append((own_heads(query_grad) * plain).astype(bf16))
    turned = []
    for half in range(2):
        at_half = [i for i, (where, _) in enumerate(chunks) if where == half]
        query_t = jnp.concatenate([query_grads[i] for i in at_half], axis=1)
        key = jnp.concatenate(
            [(key_grads[half, tile] * plain).astype(bf16) for tile in range(tiles)], axis=0
        )
        value = jnp.concatenate(
            [value_grads[half, tile].astype(bf16) for tile in range(tiles)], axis=0
        )
        turned.append([query_t, key.T, value.T, att_ref[places[half], :, lanes].T])
        for c, part in enumerate((query_t.T, key, value)):
            grad_rows_ref[c, places[half]] = part
    top, bottom = 0.0, 0.0
    for side in range(2):
        mine = [jnp.where(is_own[side], a, b) for a, b in zip(turned[0], turned[1])]
        rows_here = firsts[side][...]
        top = top + dot(jnp.concatenate(mine[:2], axis=0), rows_here)
        bottom = bottom + jnp.concatenate(
            [dot(mine[2], rows_here), dot(mine[3], sides[side])], axis=0
        )
    split_halves(at_ref[slot], pl.ds(place * unit, unit), top, bottom, keep_ref, send_ref)


def attend_back(at, slot, pair, place, count, qkv, att, lse, grad_own, grad_other, out_weight,
                first_own, first_other, old=(), after=()):
    rows, width = first_own.shape
    blocks = 2 ** (SPLITS - 1)
    unit = 4 * PAIR // (2 * blocks)
    pieces = ((blocks, count * unit, width), jnp.bfloat16)
    arrays = [qkv, att, lse, *grad_own, *grad_other, out_weight, first_own, first_other, *old]
    return local_call(
        functools.partial(attend_back_kernel, slot, pair, place),
        "attend_back",
        at,
        arrays,
        [pieces, pieces, ((3, 2, rows, PAIR), jnp.bfloat16)],
        after,
        aliases={len(arrays) - 1: 0, len(arrays): 1} if old else {},
        mebibytes=12,
    )


def first_back_kernel(count, at_ref, weight_ref, *refs):
    own_ref, upper_ref, lower_ref = refs[-3:]
    pieces = []
    for index, ref in enumerate(refs[:count]):
        lanes = slice(index * PAIR, (index + 1) * PAIR)
        pieces += [(ref, c, lanes) for c in range(3)]
    weight = jnp.concatenate([weight_ref[c, :, lanes] for _, c, lanes in pieces], axis=1)
    own, other = [
        jnp.concatenate([ref[c, side] for ref, c, _ in pieces], axis=1) for side in range(2)
    ]
    give_halves(upper_ref, lower_ref, dot(other, weight, CONTRACT_COLS))
    own_ref[...] = dot(own, weight, CONTRACT_COLS)


def first_back(at, weight, groups, after=()):
    shape = (groups[0].shape[2], weight.shape[1])
    half = ((HALF_ROWS, weight.shape[1]), jnp.bfloat16)
    return local_call(
        functools.partial(first_back_kernel, len(groups)), "first_back", at, [weight, *groups],
        [(shape, jnp.float32), half, half], after,
    )


def fold_kernel(slot, at_ref, kept_ref, came_ref, *refs):
    keep_ref, send_ref = refs[-2:]
    half = keep_ref.shape[0]
    bit = at_ref[slot]
    for target, start in ((send_ref, (1 - bit) * half), (keep_ref, bit * half)):
        for index in range(half):
            total = kept_ref[start + index].astype(jnp.float32) + came_ref[
                start + index
            ].astype(jnp.float32)
            target[index] = total.astype(jnp.bfloat16)


def add_kernel(at_ref, kept_ref, came_ref, *refs):
    total = kept_ref[...].astype(jnp.float32) + came_ref[...].astype(jnp.float32)
    refs[-1][...] = total.astype(jnp.bfloat16)


def widen(pair):
    half = pair.shape[0] // 2
    pair = pair.astype(jnp.float32)
    return pair[:half] + pair[half:]


def narrow(value):
    high = value.astype(jnp.bfloat16)
    low = (value - high.astype(jnp.float32)).astype(jnp.bfloat16)
    return jnp.concatenate([high, low], axis=0)


def add_small_kernel(at_ref, kept_ref, came_ref, mine_ref, other_ref, *refs):
    total = kept_ref[0].astype(jnp.float32) + came_ref[0].astype(jnp.float32)
    refs[-1][0] = total.astype(jnp.bfloat16)
    refs[-1][1] = narrow(mine_ref[...] + other_ref[...])


def again_kernel(at_ref, mine_ref, came_ref, *refs):
    total = mine_ref[0].astype(jnp.float32) + came_ref[0].astype(jnp.float32)
    refs[-1][0] = total.astype(jnp.bfloat16)
    if mine_ref.shape[0] > 1:
        refs[-1][1] = narrow(widen(mine_ref[1]) + widen(came_ref[1]))


def join_kernel(slot, at_ref, mine_ref, came_ref, *refs):
    both_ref = refs[-1]
    half = both_ref.shape[0] // 2
    bit = at_ref[slot]
    for source, start in ((mine_ref, bit * half), (came_ref, (1 - bit) * half)):
        for index in range(half):
            both_ref[start + index] = source[index]
    if both_ref.shape[0] > 2 * half:
        both_ref[2 * half] = narrow(widen(mine_ref[half]) + widen(came_ref[half]))


def fold(at, slot, kept, came, after=()):
    blocks, rows, width = kept.shape
    outs = [((blocks // 2, rows, width), jnp.bfloat16)] * 2
    return local_call(
        functools.partial(fold_kernel, slot), "fold", at, [kept, came], outs, after
    )


def last_fold(at, kept, came, small, after=()):
    blocks, rows, width = kept.shape
    kernel = add_small_kernel if small else add_kernel
    outs = [((blocks + (1 if small else 0), rows, width), jnp.bfloat16)]
    return local_call(kernel, "add", at, [kept, came, *small], outs, after)[0]


def again(at, mine, came, after=()):
    outs = [(mine.shape, jnp.bfloat16)]
    return local_call(again_kernel, "again", at, [mine, came], outs, after)[0]


def join(at, slot, mine, came, blocks, after=()):
    _, rows, width = mine.shape
    extra = mine.shape[0] - blocks
    outs = [((2 * blocks + extra, rows, width), jnp.bfloat16)]
    return local_call(
        functools.partial(join_kernel, slot), "join", at, [mine, came], outs, after
    )[0]


def ordered_units(bit, mine_ref, came_ref, blocks, unit):
    width = mine_ref.shape[2]
    for index in range(mine_ref.shape[1] // unit):
        rows = slice(index * unit, (index + 1) * unit)
        mine = mine_ref[:blocks, rows, :].reshape(blocks * unit, width)
        came = came_ref[:blocks, rows, :].reshape(blocks * unit, width)
        yield index, jnp.where(bit == 0, mine, came), jnp.where(bit == 0, came, mine)


def finish_mlp_kernel(slot, start, blocks, at_ref, mine_ref, came_ref, *refs):
    up_ref, down_ref, token_ref, turned_ref, held_ref, up_sems, down_sems = refs[-7:]
    token_ref[...] = jnp.zeros_like(token_ref)
    copies = []
    for index, top, bottom in ordered_units(
        at_ref[slot], mine_ref, came_ref, blocks, TILE // blocks
    ):
        place = pl.ds((start + index) * TILE, TILE)
        held_ref[index] = bottom.astype(jnp.float32)
        copies.append(
            pltpu.make_async_copy(held_ref.at[index], down_ref.at[place, :], down_sems.at[index])
        )
        copies[-1].start()
        turned_ref[index] = top.T.astype(jnp.float32)
        copies.append(
            pltpu.make_async_copy(turned_ref.at[index], up_ref.at[:, place], up_sems.at[index])
        )
        copies[-1].start()
    for copy in copies:
        copy.wait()


def finish_attend_kernel(slot, start, blocks, at_ref, mine_ref, came_ref, *refs):
    token_ref, turned_ref, held_ref, qkv_sems, out_sems = refs[-5:]
    smalls = 3 if mine_ref.shape[0] > blocks else 0
    qkv_ref, out_ref = refs[-7 - smalls : -5 - smalls]
    if mine_ref.shape[0] > blocks:
        small = widen(mine_ref[blocks]) + widen(came_ref[blocks])
        attn_ref, mlp_ref, depth_ref = refs[-8:-5]
        attn_ref[...] = small[0]
        mlp_ref[...] = small[1]
        depth_ref[...] = jnp.sum(small[8 : 8 + depth_ref.shape[0]], axis=1)
    token_ref[...] = jnp.zeros_like(token_ref)
    copies = []
    for index, top, bottom in ordered_units(
        at_ref[slot], mine_ref, came_ref, blocks, 2 * PAIR // blocks
    ):
        place = pl.ds((start + index) * PAIR, PAIR)
        held_ref[index] = bottom[PAIR:].astype(jnp.float32)
        copies.append(
            pltpu.make_async_copy(held_ref.at[index], out_ref.at[place, :], out_sems.at[index])
        )
        copies[-1].start()
        for c, part in enumerate((top[:PAIR], top[PAIR:], bottom[:PAIR])):
            turned_ref[index, c] = part.T.astype(jnp.float32)
        copies.append(
            pltpu.make_async_copy(
                turned_ref.at[index], qkv_ref.at[:, :, place], qkv_sems.at[index]
            )
        )
        copies[-1].start()
    for copy in copies:
        copy.wait()


def finish(kernel, name, at, slot, start, mine, came, shapes, scratch, old=None, after=(),
           smalls=()):
    in_vmem = pl.BlockSpec(memory_space=pltpu.VMEM)
    in_hbm = pl.BlockSpec(memory_space=pltpu.HBM)
    blocks = 2 ** (SPLITS - 1)
    units = mine.shape[1] * blocks // TILE
    return pl.pallas_call(
        functools.partial(kernel, slot, start, blocks),
        in_specs=[pl.BlockSpec(memory_space=pltpu.SMEM), in_vmem, in_vmem]
        + [in_hbm] * len(old or [])
        + [pl.BlockSpec(memory_space=pl.ANY)] * len(after),
        out_specs=[in_hbm, in_hbm] + [in_vmem] * (len(smalls) + 1),
        out_shape=[
            jax.ShapeDtypeStruct(shape, jnp.float32) for shape in [*shapes, *smalls, (8, 128)]
        ],
        scratch_shapes=[pltpu.VMEM((units, *shape), jnp.float32) for shape in scratch]
        + [pltpu.SemaphoreType.DMA((units,))] * 2,
        input_output_aliases={3: 0, 4: 1} if old else {},
        compiler_params=params(12),
        cost_estimate=cost(1000, 1000),
        name=name,
    )(at, mine, came, *(old or []), *after)


def finish_mlp(at, slot, start, mine, came, width, hidden, old=None, after=()):
    shapes = [(width, hidden), (hidden, width)]
    scratch = [(width, TILE), (TILE, width)]
    return finish(
        finish_mlp_kernel, "finish_mlp", at, slot, start, mine, came, shapes, scratch, old, after
    )


def finish_attend(at, slot, start, mine, came, width, local, layers, old=None, after=()):
    shapes = [(3, width, local), (local, width)]
    scratch = [(3, width, PAIR), (PAIR, width)]
    smalls = [(width,), (width,), (layers,)] if mine.shape[0] > 2 ** (SPLITS - 1) else []
    return finish(
        finish_attend_kernel, "finish_attend", at, slot, start, mine, came, shapes, scratch, old,
        after, smalls,
    )


def mp_swap(rows):
    return lax.ppermute(rows, "mp", [(0, 1), (1, 0)])


def dp_bits():
    return lax.axis_size("dp").bit_length() - 1


def bit_swap(rows, bits):
    size, cores = lax.axis_size("dp"), lax.axis_size("mp")
    pairs = [
        (i * cores + core, (i ^ (1 << bits[core])) * cores + core)
        for i in range(size)
        for core in range(cores)
    ]
    return lax.ppermute(rows, ("dp", "mp"), pairs)


def step_bits(kind, step):
    return [order[step] for order in KINDS[kind]]


def slot_of(kind, step):
    return 1 + kind * SPLITS + step


def where_am_i():
    core, index = lax.axis_index("mp"), lax.axis_index("dp")
    values = [core]
    for kind in range(len(KINDS)):
        for step in range(SPLITS):
            bits = step_bits(kind, step)
            values.append((index >> jnp.where(core == 0, bits[0], bits[1])) & 1)
    return jnp.stack(values).astype(jnp.int32)


class Stream:
    def __init__(self, at, kind, kept, sent, small=None):
        self.at, self.kind, self.kept, self.step, self.small = at, kind, kept, 0, small
        self.extra = dp_bits() - SPLITS
        self.came = bit_swap(sent, step_bits(kind, 0))

    def advance(self, after=()):
        step, kind, at = self.step, self.kind, self.at
        self.step += 1
        joined = step - SPLITS - self.extra
        if step < SPLITS - 1:
            self.kept, sent = fold(at, slot_of(kind, step + 1), self.kept, self.came, after)
            self.came = bit_swap(sent, step_bits(kind, step + 1))
            return self.kept
        if step == SPLITS - 1:
            small = self.small() if self.small else ()
            self.kept = last_fold(at, self.kept, self.came, small, after)
        elif joined < 0:
            self.kept = again(at, self.kept, self.came, after)
        else:
            slot = slot_of(kind, SPLITS - 1 - joined)
            self.kept = join(at, slot, self.kept, self.came, 2**joined, after)
        if joined < -1:
            bit = SPLITS + joined + 1 + self.extra
            self.came = bit_swap(self.kept, [bit, bit])
        else:
            self.came = bit_swap(self.kept, step_bits(kind, SPLITS - 2 - joined))
        return self.kept


def shards(
    history,
    depth_weights,
    gain_attn,
    gain_mlp,
    qkv_weight,
    out_weight,
    up_weight,
    down_weight,
    cotangent,
):
    width = cotangent.shape[1]
    local = out_weight.shape[0]
    hidden = down_weight.shape[0]
    pairs = local // PAIR
    at = where_am_i()

    cot_other = mp_swap(cotangent)
    mixed, first = mix(depth_weights, history, gain_attn)
    first_other = mp_swap(first)
    half = cotangent.shape[0] // 2
    back_up = hidden_back(at, cotangent, down_weight, 0, half)
    qkv, att, lse, out_own, out_other = attend(
        at, first, first_other, qkv_weight, out_weight, [back_up]
    )
    back_low = hidden_back(at, cotangent, down_weight, half, half, [out_own])
    middle, second = renorm(at, mixed, out_own, mp_swap(out_other), gain_mlp, [back_low])
    back_other = hidden_back(at, cot_other, down_weight, 0, 2 * half, [second])
    second_other = mp_swap(second)
    mlp_names = [name for name in KIND if name[0] == "M"]
    *stacks, hidden_rows, grad_own, grad_upper, grad_lower = mlp(
        at, tuple(slot_of(KIND[name], 0) for name in mlp_names), second, second_other, cotangent,
        cot_other, (back_up, back_low), back_other, up_weight,
    )
    streams = {
        name: Stream(at, KIND[name], *stacks[2 * i : 2 * i + 2])
        for i, name in enumerate(mlp_names)
    }
    grad_came = [mp_swap(part) for part in (grad_upper, grad_lower)]
    made = {}

    def back_norm(after):
        made["middle"], *made["narrow"], made["gain"] = norm_back_rows(
            at, grad_own, grad_came, middle, cotangent, gain_mlp, after
        )
        made["narrow_came"] = [mp_swap(part) for part in made["narrow"]]
        return made["gain"]

    def back_pair(pair, after):
        late = pair == pairs - 1
        name, place = ("Ab", 0) if late else ("Aa", pair)
        old = () if late or pair == 0 else made["stack"]
        kept, sent, made[pair] = attend_back(
            at, slot_of(KIND[name], 0), pair, place, 1 if late else pairs - 1, qkv, att, lse,
            made["narrow"], made["narrow_came"], out_weight, first, first_other, old, after,
        )
        made["stack"] = (kept, sent)
        if pair >= pairs - 2:
            small = (lambda: (made["small"], made["small_came"])) if late else None
            streams[name] = Stream(at, KIND[name], kept, sent, small)
        return made[pair]

    def back_first(after):
        groups = [made[pair] for pair in range(pairs)]
        made["own"], *other = first_back(at, qkv_weight, groups, after)
        made["came"] = [mp_swap(part) for part in other]
        return made["own"]

    def back_start(after):
        made["mixed"], made["small"] = unmix(
            depth_weights, history, gain_attn, mixed, made["middle"], made["own"], made["came"],
            made["gain"], after,
        )
        made["small_came"] = mp_swap(made["small"])
        return made["small"]

    def give_outputs(after):
        made["history"], made["out"], token = outputs(
            depth_weights, made["mixed"], middle, made["block"], made["block_came"], after
        )
        return token

    def block_rows(after):
        made["block"], *other = rows_times(at, hidden_rows, down_weight, after)
        made["block_came"] = [mp_swap(part) for part in other]
        return made["block"]

    def end_mlp(name, start, after):
        stream = streams[name]
        *made["mlp"], token = finish_mlp(
            at, slot_of(KIND[name], 0), start, stream.kept, stream.came, width, hidden,
            made.get("mlp"), after,
        )
        return token

    def end_attend(name, start, after):
        stream = streams[name]
        grad_qkv, grad_out, *made[name], token = finish_attend(
            at, slot_of(KIND[name], 0), start, stream.kept, stream.came, width, local,
            history.shape[0], made.get("attend"), after,
        )
        made["attend"] = grad_qkv, grad_out
        return token

    units = {
        "nb": back_norm,
        "fb": back_first,
        "um": back_start,
        "um2": give_outputs,
        "blk": block_rows,
        "fAa": functools.partial(end_attend, "Aa", 0),
        "fAb": functools.partial(end_attend, "Ab", pairs - 1),
    }
    start = 0
    for name, count in zip(mlp_names, MLP_UNITS):
        units["f" + name] = functools.partial(end_mlp, name, start)
        start += count
    for pair in range(pairs):
        units["ab" + str(pair)] = functools.partial(back_pair, pair)
    last = hidden_rows
    for name in ORDER:
        if name in streams:
            if streams[name].step == SPLITS:
                for _ in range(streams[name].extra - 1):
                    last = streams[name].advance([last])
            last = streams[name].advance([last])
        else:
            last = units[name]([last])
    gain_grad_attn, gain_grad_mlp, grad_depth = made["Ab"]
    block_out, grad_history = made["out"], made["history"]
    (grad_up, grad_down), (grad_qkv, grad_out) = made["mlp"], made["attend"]
    return (
        block_out,
        grad_history,
        grad_depth,
        gain_grad_attn,
        gain_grad_mlp,
        grad_qkv,
        grad_out,
        grad_up,
        grad_down,
    )


def solution(mesh):
    in_specs = (
        P(None, ("dp", "mp"), None),
        P(),
        P(),
        P(),
        P(None, None, "mp"),
        P("mp", None),
        P(None, "mp"),
        P("mp", None),
        P(("dp", "mp"), None),
    )
    out_specs = (
        P(("dp", "mp"), None),
        P(None, ("dp", "mp"), None),
        P(),
        P(),
        P(),
        P(None, None, "mp"),
        P("mp", None),
        P(None, "mp"),
        P("mp", None),
    )
    return jax.shard_map(shards, mesh=mesh, in_specs=in_specs, out_specs=out_specs, check_vma=False)
```
